32 devices in a mesh: mem: 16 (over z, x, core), grp: 2 (over y).
Axes of the slice: x: 2, y: 2, z: 4, core: 2. Of those that a mesh axis runs over, the one named last changes fastest.
Arguments:
- queries: bfloat16 [2, 2048, 2048], P('grp', 'mem'), may hold values from -96 to 96
- d_out: bfloat16 [2, 2048, 2048], P('grp', 'mem'), may hold values from -16 to 16
- o_mem: bfloat16 [2, 2048, 2048], P('grp', 'mem'), may hold values from -3 to 3
- local_out: bfloat16 [2, 2048, 2048], P('grp', 'mem'), may hold values from -3 to 3
- mem_keys: bfloat16 [4096, 2048], P('mem'), may hold values from -4 to 4
- mem_values: bfloat16 [4096, 2048], P('mem'), may hold values from -5 to 5
- gate_logit: float32 [16], replicated, may hold values from -2 to 2
- block_ids: int32 [2, 128, 32], P('grp', 'mem'), may hold values from 0 to 255, as said below
Outputs:
- d_query: bfloat16 [2, 2048, 2048], P('grp', 'mem')
- d_gate: float32 [16], replicated
The draws below stay inside these ranges and needn't reach their ends.
Inputs may be any that keep to these rules, and one draw needn't show every extreme that they name: `block_ids`: each row lists 8 distinct shards in turn, 4 distinct blocks of each in increasing order. The query blocks of one device name each shard at most 4 times, and in every group some shard is named 4 times by the blocks of every device.
All inputs are finite; a program needn't handle non-finite values.
Results may differ from the reference program's by a relative error of at most 0.008.
Values may be sent and summed in bfloat16 or wider, within the bound.
No kernel may reach another device: no remote copies, remote signals or barrier semaphores. Data moves between devices by JAX's collectives and lax.ppermute only.
A program may use at most 64 MiB of HBM per device.

```python
import jax
import jax.numpy as jnp
from jax import lax

HEADS = 16
HD = 128
HH = 2048
BLK = 16
NSH = 8
PICK = 4
MB_DEV = 16
QB_DEV = 8
MSHARDS = 16
GROUPS = 2
TOK_GRP = 2048
NQB = 128
MEMROWS = 4096


def named_blocks(key):
    key = jax.random.fold_in(key, 101)
    key_hot, key_rank, key_rows, key_local = jax.random.split(key, 4)
    hot_order = jax.vmap(lambda sub_key: jax.random.permutation(sub_key, MSHARDS))(jax.random.split(key_hot, GROUPS))
    hot_flag = (hot_order < 4).astype(jnp.int32)
    rank_score = jax.random.randint(key_rank, (GROUPS, MSHARDS, MSHARDS), 0, MSHARDS) + MSHARDS * hot_flag[:, None, :]
    shard_order = jnp.argsort(-rank_score, axis=2, stable=True)
    positions = (jnp.arange(QB_DEV)[:, None] * NSH + jnp.arange(NSH)[None, :]) % MSHARDS
    row_score = jax.random.randint(key_rows, (GROUPS, MSHARDS, QB_DEV), 0, 1 << 20)
    row_perm = jnp.argsort(row_score, axis=2, stable=True)
    placed = positions[row_perm].reshape(GROUPS, MSHARDS, QB_DEV * NSH)
    chosen = jnp.take_along_axis(shard_order, placed, axis=2).reshape(GROUPS, MSHARDS, QB_DEV, NSH)
    local_score = jax.random.randint(key_local, (GROUPS, MSHARDS, QB_DEV, NSH, MB_DEV), 0, 1 << 20)
    local_pick = jnp.sort(jnp.argsort(local_score, axis=-1, stable=True)[..., :PICK], axis=-1)
    blocks = chosen[..., None] * MB_DEV + local_pick
    return blocks.reshape(GROUPS, NQB, NSH * PICK).astype(jnp.int32)


def base_keys(key):
    key = jax.random.fold_in(key, 202)
    return jnp.clip(jax.random.normal(key, (MEMROWS, HH), jnp.float32), -4.0, 4.0)


def draw_block_ids(key, part):
    return named_blocks(key)


def draw_mem_keys(key, part):
    keys_all = base_keys(key)
    return keys_all.astype(jnp.bfloat16)


def draw_queries(key, part):
    key = jax.random.fold_in(key, 303)
    noise_key = jax.random.fold_in(key, 0)
    values = jnp.clip(jax.random.normal(noise_key, (GROUPS, TOK_GRP, HH), jnp.float32), -4.0, 4.0)
    return values.astype(jnp.bfloat16)


def draw_d_out(key, part):
    key = jax.random.fold_in(key, 404)
    order = (jnp.arange(GROUPS)[:, None] * TOK_GRP + jnp.arange(TOK_GRP)[None, :]).astype(jnp.float32) / (GROUPS * TOK_GRP)
    values = jnp.clip(jax.random.normal(key, (GROUPS, TOK_GRP, HH), jnp.float32), -4.0, 4.0)
    ramp = 1.0 + 2.0 * order
    return jnp.clip(values * ramp[..., None], -16.0, 16.0).astype(jnp.bfloat16)


def shard_levels(stream_key, dims, cuts, least, high):
    def one(axis_at, shards_of):
        draws = jax.random.uniform(jax.random.fold_in(jax.random.fold_in(stream_key, 6), axis_at), (shards_of,), jnp.float32, least / len(cuts), high / len(cuts))
        return jnp.repeat(jnp.exp(draws), dims[axis_at] // shards_of).reshape((-1,) + (1,) * (len(dims) - axis_at - 1))

    factor_of = one(*cuts[0])
    for cut in cuts[1:]:
        factor_of = factor_of * one(*cut)
    return factor_of


def bell_draw(rng, shape, deviation, most, cuts=(), kind=jnp.bfloat16):
    array = deviation * jax.random.normal(rng, shape, jnp.float32)
    if cuts:
        array = array * shard_levels(rng, shape, cuts, -0.22, 0.18)
    return jnp.clip(array, -most, most).astype(kind)


def setup_inputs(seed: int = 0) -> dict:
    splits = jax.random.split(jax.random.key(seed), 9)
    queries = draw_queries(jax.random.fold_in(splits[8], 71), 0)
    d_out = draw_d_out(jax.random.fold_in(splits[8], 71), 0)
    o_mem = bell_draw(splits[2], (GROUPS, TOK_GRP, HH), 0.5, 3.0, ((0, 2), (1, 16)))
    local_out = bell_draw(splits[3], (GROUPS, TOK_GRP, HH), 0.5, 3.0, ((0, 2), (1, 16)))
    mem_keys = draw_mem_keys(jax.random.fold_in(splits[8], 71), 0)
    mem_values = bell_draw(splits[5], (MEMROWS, HH), 1.0, 5.0, ((0, 16),))
    gate_logit = jnp.clip(jax.random.uniform(splits[6], (HEADS,), jnp.float32, -2.0, 2.0), -2.0, 2.0)
    block_ids = draw_block_ids(jax.random.fold_in(splits[8], 71), 0)
    return dict(queries=queries, d_out=d_out, o_mem=o_mem, local_out=local_out, mem_keys=mem_keys, mem_values=mem_values, gate_logit=gate_logit, block_ids=block_ids)


def reference(queries, d_out, o_mem, local_out, mem_keys, mem_values, gate_logit, block_ids):
    scale = 1.0 / (HD ** 0.5)
    sig = jax.nn.sigmoid(gate_logit.astype(jnp.float32))
    dout_four = d_out.reshape(GROUPS, TOK_GRP, HEADS, HD)
    omem_four = o_mem.reshape(GROUPS, TOK_GRP, HEADS, HD)
    local_four = local_out.reshape(GROUPS, TOK_GRP, HEADS, HD)
    d_mem = (dout_four.astype(jnp.float32) * sig[:, None]).astype(jnp.bfloat16)
    d_mem = lax.optimization_barrier(d_mem)
    delta = jnp.sum(d_mem.astype(jnp.float32) * omem_four.astype(jnp.float32), -1).astype(jnp.bfloat16)
    keys_blocked = mem_keys.reshape(-1, BLK, HEADS, HD)
    values_blocked = mem_values.reshape(-1, BLK, HEADS, HD)
    query_blocks = queries.reshape(GROUPS * NQB, BLK, HEADS, HD)
    dmem_blocks = d_mem.reshape(GROUPS * NQB, BLK, HEADS, HD)
    delta_blocks = delta.reshape(GROUPS * NQB, BLK, HEADS)
    named = block_ids.reshape(GROUPS * NQB, NSH, PICK)

    def one_block(pieces):
        query_here, dmem_here, delta_here, named_here = pieces
        keys_here = keys_blocked[named_here].reshape(NSH, PICK * BLK, HEADS, HD).astype(jnp.float32)
        values_here = values_blocked[named_here].reshape(NSH, PICK * BLK, HEADS, HD).astype(jnp.float32)
        scores = jnp.einsum("rhd,nkhd->nrhk", query_here.astype(jnp.float32), keys_here) * scale
        high = jnp.max(scores, -1)
        expo = jnp.exp(scores - high[..., None])
        total = jnp.sum(expo, -1)
        dprod = jnp.einsum("rhd,nkhd->nrhk", dmem_here.astype(jnp.float32), values_here)
        dscore = (expo * (dprod - delta_here.astype(jnp.float32)[None, :, :, None])).astype(jnp.bfloat16)
        dscore = lax.optimization_barrier(dscore)
        part = (jnp.einsum("nrhk,nkhd->nrhd", dscore.astype(jnp.float32), keys_here) * scale).astype(jnp.bfloat16)
        part = lax.optimization_barrier(part)
        top = jnp.max(high, 0)
        lifted = jnp.exp(high - top[None])
        weight = lifted / jnp.sum(total * lifted, 0)[None]
        grad = jnp.sum(weight[..., None] * part.astype(jnp.float32), 0)
        return grad.astype(jnp.bfloat16)

    d_query = lax.map(one_block, (query_blocks, dmem_blocks, delta_blocks, named))
    d_query = d_query.reshape(GROUPS, TOK_GRP, HH)
    differ = omem_four.astype(jnp.float32) - local_four.astype(jnp.float32)
    gate_total = jnp.sum(dout_four.astype(jnp.float32) * differ, axis=(0, 1, 3))
    d_gate = sig * (1.0 - sig) * gate_total / ((GROUPS * TOK_GRP * HD) ** 0.5)
    return d_query, d_gate
```

```python
import functools
import math

import jax
import jax.numpy as jnp
from jax import lax
from jax.experimental import pallas as pl
from jax.experimental.pallas import tpu as pltpu
from jax.sharding import PartitionSpec as P

BLK = 16
LANES = 128
AXES = ("mem", "grp")
FAR = -1e30


def place(position):
    mem_index, parity = divmod(position, 2)
    return (mem_index >> 1) * 2 + parity, mem_index & 1


def pack_rows(quarter, heads, k_ref, v_ref, out_ref):
    parity = lax.axis_index("grp") % 2
    for position in range(2 * heads):
        head, half = place(position)
        rows = pl.ds(pl.multiple_of(parity * (2 * quarter) + half * quarter, quarter), quarter)
        cols = slice(head * LANES, (head + 1) * LANES)
        out_ref[position, :quarter, :] = k_ref[rows, cols]
        out_ref[position, quarter:, :] = v_ref[rows, cols]


def pack_tokens(
    heads, chunks, q_ref, dout_ref, omem_ref, local_ref, gate_ref, ids_ref, out_ref, ext_ref, delta_ref, gate_rows
):
    tokens = q_ref.shape[0]
    half_rows = tokens // 2
    qblocks, names = ids_ref.shape
    high = lax.Precision.HIGHEST
    parity = lax.axis_index("grp") % 2
    ones = jnp.ones((8, LANES), jnp.float32)
    gate_rows[...] = jnp.zeros_like(gate_rows)
    for head in range(heads):
        cols = slice(head * LANES, (head + 1) * LANES)
        sig = jax.nn.sigmoid(jnp.full((8, LANES), gate_ref[head], jnp.float32))[:1]
        d_out = dout_ref[:, cols].astype(jnp.float32)
        o_mem = omem_ref[:, cols].astype(jnp.float32)
        d_mem = (d_out * sig).astype(jnp.bfloat16)
        differ = o_mem - local_ref[:, cols].astype(jnp.float32)
        gate_rows[head : head + 1, :] = jnp.sum(d_out * differ, 0, keepdims=True)
        product = d_mem.astype(jnp.float32) * o_mem
        row = lax.dot_general(
            ones, product, (((1,), (1,)), ((), ())), precision=high, preferred_element_type=jnp.float32
        )
        delta_ref[head : head + 1, :] = row[:1]
        q = q_ref[:, cols]
        for half in range(2):
            position = ((head // 2) * 2 + half) * 2 + head % 2
            rows = slice(half * half_rows, (half + 1) * half_rows)
            out_ref[position, :half_rows, :] = q[rows]
            out_ref[position, half_rows : 2 * half_rows, :] = d_mem[rows]
    total = lax.dot_general(
        ones, gate_rows[...], (((1,), (1,)), ((), ())), precision=high, preferred_element_type=jnp.float32
    )[:1]
    first = total.astype(jnp.bfloat16).astype(jnp.float32)
    second = (total - first).astype(jnp.bfloat16).astype(jnp.float32)
    third = total - first - second
    lane = lax.broadcasted_iota(jnp.int32, (1, LANES), 1)
    shards_each = heads
    ids = ids_ref[...]
    tables = []
    for chunk in range(chunks):
        block = 16 * (chunk * shards_each + lane // 8) + 8 * ((lane // 4) % 2) + lane % 4
        pair = []
        for half in range(2):
            wanted = jnp.broadcast_to(block + 4 * half, (qblocks, LANES))
            hit = jnp.zeros((qblocks, LANES), jnp.float32)
            for name in range(names):
                hit = jnp.where(ids[:, name : name + 1] == wanted, 1.0, hit)
            pair.append(jnp.where(hit > 0.5, 0.0, FAR))
        tables.append(pair)
    bias_rows = 2 * chunks * (qblocks // 2)
    per = qblocks // 2
    for half in range(2):
        ext_ref[...] = jnp.zeros_like(ext_ref)
        for relative in range(2):
            for chunk in range(chunks):
                at = (relative * chunks + chunk) * per
                ext_ref[at : at + per, :] = tables[chunk][half ^ relative][half * per : (half + 1) * per]
        ext_ref[bias_rows + 1 : bias_rows + 2, :] = first
        ext_ref[bias_rows + 2 : bias_rows + 3, :] = second
        ext_ref[bias_rows + 3 : bias_rows + 4, :] = third
        in_half = (lane // half_rows) == parity
        for head in range(heads):
            row = delta_ref[head : head + 1, :]
            rolled = jnp.concatenate([row[:, half_rows:], row[:, :half_rows]], axis=1)
            row = jnp.where(parity == half, row, rolled)
            ext_ref[bias_rows : bias_rows + 1, :] = jnp.where(in_half, row, 0.0)
            position = ((head // 2) * 2 + half) * 2 + head % 2
            out_ref[position, 2 * half_rows :, :] = ext_ref[...].astype(jnp.bfloat16)


def attend(
    halves, per, width, own_ref, mate_ref, qd_ref, out_ref, gate_ref, kx, vx, qx, delta, scores, high, total, acc
):
    step = pl.program_id(0)
    sources, packet, _ = qd_ref.shape
    quarter = own_ref.shape[1] // 2
    tile = qx.shape[0]
    units = qx.shape[1] // LANES - 1
    rows_unit = kx.shape[0] // units
    steps_unit = rows_unit // width
    scale = 1.0 / math.sqrt(LANES)
    exponent = scale * math.log2(math.e)
    bias_rows = units * per

    @pl.when(step == 0)
    def _():
        for index, ref in enumerate((own_ref, mate_ref)):

            def fill(source, carry, index=index, ref=ref):
                at = pl.ds(pl.multiple_of((index * ref.shape[0] + source) * quarter, quarter), quarter)
                kx[at, :LANES] = ref[source, :quarter, :]
                vx[at, :] = ref[source, quarter:, :]
                return carry

            lax.fori_loop(0, ref.shape[0], fill, 0)

        lane = lax.broadcasted_iota(jnp.int32, (BLK, LANES), 1)

        def mark(block, carry):
            at = pl.ds(pl.multiple_of(block * BLK, BLK), BLK)
            kx[at, LANES:] = (lane == block % LANES).astype(jnp.float32).astype(jnp.bfloat16)
            return carry

        lax.fori_loop(0, kx.shape[0] // BLK, mark, 0)
        gate_ref[...] = jnp.zeros_like(gate_ref)

    rows_source = 2 * halves
    delta_rows = []
    gate_sum = jnp.zeros((1, LANES), jnp.float32)
    for source in range(sources):
        base = source * halves
        qx[base : base + halves, :LANES] = qd_ref[source, :halves, :]
        extra = qd_ref[source, rows_source:, :].astype(jnp.float32)
        for unit in range(units):
            for block in range(per):
                at = unit * per + block
                row = jnp.broadcast_to(extra[at : at + 1], (BLK, LANES)).astype(jnp.bfloat16)
                qx[base + block * BLK : base + (block + 1) * BLK, (1 + unit) * LANES : (2 + unit) * LANES] = row
        delta_rows.append(extra[bias_rows : bias_rows + 1])
        for part in range(1, 4):
            gate_sum = gate_sum + extra[bias_rows + part : bias_rows + part + 1]
    gate_ref[...] += jnp.broadcast_to(gate_sum, gate_ref.shape)
    for pair in range(sources // 2):
        row = delta_rows[2 * pair] + delta_rows[2 * pair + 1]
        delta[pair * LANES : (pair + 1) * LANES, :] = jnp.broadcast_to(row, (LANES, LANES)).T

    high[...] = jnp.full_like(high, -3e38)
    for unit in range(units):

        def score(index, carry, unit=unit):
            at = unit * steps_unit + index
            rows = pl.ds(pl.multiple_of(at * width, width), width)
            left = jnp.concatenate([qx[:, :LANES], qx[:, (1 + unit) * LANES : (2 + unit) * LANES]], axis=1)
            got = lax.dot_general(
                left, kx[rows, :], (((1,), (1,)), ((), ())), preferred_element_type=jnp.float32
            )
            scores[at] = got
            best = high[...]
            for column in range(width // LANES):
                best = jnp.maximum(best, got[:, column * LANES : (column + 1) * LANES])
            high[...] = best
            return carry

        lax.fori_loop(0, steps_unit, score, 0)
    high[...] = jnp.broadcast_to(jnp.max(high[...], 1, keepdims=True) * exponent, high.shape)
    total[...] = jnp.zeros_like(total)
    acc[...] = jnp.zeros_like(acc)

    def back(at, carry):
        rows = pl.ds(pl.multiple_of(at * width, width), width)
        d_mem = jnp.concatenate(
            [qd_ref[source, halves : 2 * halves, :] for source in range(sources)], axis=0
        )
        prod = lax.dot_general(
            d_mem, vx[rows, :], (((1,), (1,)), ((), ())), preferred_element_type=jnp.float32
        )
        got = scores[at]
        level = high[...]
        less = delta[...]
        added = total[...]
        pieces = []
        for column in range(width // LANES):
            cols = slice(column * LANES, (column + 1) * LANES)
            expo = jnp.exp2(got[:, cols] * exponent - level)
            added = added + expo
            pieces.append((expo * (prod[:, cols] - less)).astype(jnp.bfloat16))
        total[...] = added
        acc[...] += jnp.dot(
            jnp.concatenate(pieces, axis=1), kx[rows, :LANES], preferred_element_type=jnp.float32
        )
        return carry

    lax.fori_loop(0, units * steps_unit, back, 0)
    weight = scale / jnp.sum(total[...], 1, keepdims=True)
    result = (acc[...] * weight).astype(jnp.bfloat16)
    for source in range(sources):
        out_ref[source] = result[source * halves : (source + 1) * halves]


def unpack(heads, in_ref, out_ref):
    half_rows = in_ref.shape[1]
    for position in range(2 * heads):
        head, half = place(position)
        out_ref[half * half_rows : (half + 1) * half_rows, head * LANES : (head + 1) * LANES] = in_ref[position]


def local(queries, d_out, o_mem, local_out, mem_keys, mem_values, gate_logit, block_ids):
    shards = lax.axis_size("mem")
    groups = lax.axis_size("grp")
    tokens = queries.shape[1]
    width = queries.shape[2]
    heads = gate_logit.shape[0]
    rows_dev = mem_keys.shape[0]
    qblocks = tokens // BLK
    members = 2 * heads
    chunks = shards // heads
    assert width == heads * LANES and shards % heads == 0 and groups % 2 == 0
    assert rows_dev == 16 * BLK and heads * 8 == LANES and tokens == LANES
    quarter = rows_dev // 4
    halves = tokens // 2
    per = qblocks // 2
    bias_rows = 2 * chunks * per
    extra = -(-(bias_rows + 4) // 16) * 16
    packet = 2 * halves + extra
    vmem = pl.BlockSpec(memory_space=pltpu.VMEM)
    smem = pl.BlockSpec(memory_space=pltpu.SMEM)
    params = pltpu.CompilerParams(vmem_limit_bytes=56 << 20)

    if shards * groups == members:
        head_groups = None
    else:
        head_groups = [
            [(mo * heads + mi) * groups + 2 * go + gp for mi in range(heads) for gp in range(2)]
            for mo in range(chunks)
            for go in range(groups // 2)
        ]
    exchange = functools.partial(
        lax.all_to_all, axis_name=AXES, split_axis=0, concat_axis=0, tiled=True, axis_index_groups=head_groups
    )

    rows_out = pl.pallas_call(
        functools.partial(pack_rows, quarter, heads),
        out_shape=jax.ShapeDtypeStruct((members, 2 * quarter, LANES), jnp.bfloat16),
        in_specs=[vmem, vmem],
        out_specs=vmem,
        compiler_params=params,
        name="pack_rows",
    )(mem_keys, mem_values)
    own = exchange(rows_out)
    tokens_out = pl.pallas_call(
        functools.partial(pack_tokens, heads, chunks),
        out_shape=jax.ShapeDtypeStruct((members, packet, LANES), jnp.bfloat16),
        in_specs=[vmem, vmem, vmem, vmem, smem, vmem],
        out_specs=vmem,
        scratch_shapes=[
            pltpu.VMEM((extra, LANES), jnp.float32),
            pltpu.VMEM((max(heads, 8), LANES), jnp.float32),
            pltpu.VMEM((LANES, LANES), jnp.float32),
        ],
        compiler_params=params,
        name="pack_tokens",
    )(queries[0], d_out[0], o_mem[0], local_out[0], gate_logit, block_ids[0])
    qd = exchange(tokens_out)
    if chunks > 1:
        same = [[mo * heads + mi for mo in range(chunks)] for mi in range(heads)]
        own = lax.all_gather(own, "mem", axis_index_groups=same, axis=0, tiled=True)
    mate = lax.ppermute(own, "mem", [(i, i ^ 1) for i in range(shards)])

    units = 2 * chunks
    rows_all = 4 * quarter * shards
    tile = 512 if chunks == 1 else 256
    sources = tile // halves
    step_width = 512
    grad, gate_sum = pl.pallas_call(
        functools.partial(attend, halves, per, step_width),
        out_shape=(
            jax.ShapeDtypeStruct((members, halves, LANES), jnp.bfloat16),
            jax.ShapeDtypeStruct((8, LANES), jnp.float32),
        ),
        grid=(members // sources,),
        in_specs=[vmem, vmem, pl.BlockSpec((sources, packet, LANES), lambda i: (i, 0, 0))],
        out_specs=(
            pl.BlockSpec((sources, halves, LANES), lambda i: (i, 0, 0)),
            pl.BlockSpec((8, LANES), lambda i: (0, 0)),
        ),
        scratch_shapes=[
            pltpu.VMEM((rows_all, 2 * LANES), jnp.bfloat16),
            pltpu.VMEM((rows_all, LANES), jnp.bfloat16),
            pltpu.VMEM((tile, (1 + units) * LANES), jnp.bfloat16),
            pltpu.VMEM((tile, LANES), jnp.float32),
            pltpu.VMEM((rows_all // step_width, tile, step_width), jnp.float32),
            pltpu.VMEM((tile, LANES), jnp.float32),
            pltpu.VMEM((tile, LANES), jnp.float32),
            pltpu.VMEM((tile, LANES), jnp.float32),
        ],
        compiler_params=params,
        name="attend",
    )(own, mate, qd)
    home = exchange(grad)
    d_query = pl.pallas_call(
        functools.partial(unpack, heads),
        out_shape=jax.ShapeDtypeStruct((tokens, width), jnp.bfloat16),
        in_specs=[vmem],
        out_specs=vmem,
        compiler_params=params,
        name="unpack",
    )(home)
    gate_total = gate_sum[0, :heads]
    if head_groups is not None:
        gate_total = lax.psum(gate_total, AXES) / members
    sig = jax.nn.sigmoid(gate_logit)
    d_gate = sig * (1.0 - sig) * gate_total / (shards * groups * tokens * LANES) ** 0.5
    return (d_query[None], d_gate)


def solution(mesh):
    placed = (
        P("grp", "mem", None),
        P("grp", "mem", None),
        P("grp", "mem", None),
        P("grp", "mem", None),
        P("mem", None),
        P("mem", None),
        P(),
        P("grp", "mem", None),
    )
    return jax.shard_map(
        local, mesh=mesh, in_specs=placed, out_specs=(P("grp", "mem", None), P()), check_vma=False
    )
```

```python
import functools
import math

import jax
import jax.numpy as jnp
from jax import lax
from jax.experimental import pallas as pl
from jax.experimental.pallas import tpu as pltpu
from jax.sharding import PartitionSpec as P

BLK = 16
LANES = 128
AXES = ("mem", "grp")
FAR = -1e30


def position_here(heads):
    return (lax.axis_index("mem") % heads) * 2 + lax.axis_index("grp") % 2


def head_and_half(position):
    return (position >> 2) * 2 + (position & 1), (position >> 1) & 1


def pack_rows(quarter, heads, k_ref, v_ref, *outs):
    here = position_here(heads)
    parity = here & 1
    for step, out in enumerate(outs):
        head, half = head_and_half(here ^ step)
        rows = pl.ds(pl.multiple_of((parity * 2 + half) * quarter, quarter), quarter)
        cols = pl.ds(pl.multiple_of(head * LANES, LANES), LANES)
        out[:quarter, :] = k_ref[rows, cols]
        out[quarter:, :] = v_ref[rows, cols]


def pack_tokens(heads, chunks, q_ref, dout_ref, omem_ref, local_ref, gate_ref, ids_ref, *rest):
    members = 2 * heads
    outs = rest[:members]
    dmem_ref, halves_ref, ext_ref, delta_ref, gate_rows = rest[members:]
    tokens = q_ref.shape[0]
    half_rows = tokens // 2
    qblocks, names = ids_ref.shape
    high = lax.Precision.HIGHEST
    here = position_here(heads)
    parity = here & 1
    ones = jnp.ones((8, LANES), jnp.float32)
    gate_rows[...] = jnp.zeros_like(gate_rows)
    for head in range(heads):
        cols = slice(head * LANES, (head + 1) * LANES)
        sig = jax.nn.sigmoid(jnp.full((8, LANES), gate_ref[head], jnp.float32))[:1]
        d_out = dout_ref[:, cols].astype(jnp.float32)
        o_mem = omem_ref[:, cols].astype(jnp.float32)
        d_mem = (d_out * sig).astype(jnp.bfloat16)
        dmem_ref[:, cols] = d_mem
        differ = o_mem - local_ref[:, cols].astype(jnp.float32)
        gate_rows[head : head + 1, :] = jnp.sum(d_out * differ, 0, keepdims=True)
        product = d_mem.astype(jnp.float32) * o_mem
        row = lax.dot_general(
            ones, product, (((1,), (1,)), ((), ())), precision=high, preferred_element_type=jnp.float32
        )
        delta_ref[head : head + 1, :] = row[:1]
    total = lax.dot_general(
        ones, gate_rows[...], (((1,), (1,)), ((), ())), precision=high, preferred_element_type=jnp.float32
    )[:1]
    first = total.astype(jnp.bfloat16).astype(jnp.float32)
    second = (total - first).astype(jnp.bfloat16).astype(jnp.float32)
    third = total - first - second
    lane = lax.broadcasted_iota(jnp.int32, (1, LANES), 1)
    ids = ids_ref[...]
    per = qblocks // 2
    bias_rows = 2 * chunks * per
    halves_ref[...] = jnp.zeros_like(halves_ref)
    for chunk in range(chunks):
        block = 16 * (chunk * heads + lane // 8) + 8 * ((lane // 4) % 2) + lane % 4
        for side in range(2):
            wanted = jnp.broadcast_to(block + 4 * side, (qblocks, LANES))
            hit = jnp.zeros((qblocks, LANES), jnp.float32)
            for name in range(names):
                hit = jnp.where(ids[:, name : name + 1] == wanted, 1.0, hit)
            table = jnp.where(hit > 0.5, 0.0, FAR)
            for half in range(2):
                at = ((half ^ side) * chunks + chunk) * per
                halves_ref[half, at : at + per, :] = table[half * per : (half + 1) * per]
    for half in range(2):
        halves_ref[half, bias_rows + 1 : bias_rows + 2, :] = first
        halves_ref[half, bias_rows + 2 : bias_rows + 3, :] = second
        halves_ref[half, bias_rows + 3 : bias_rows + 4, :] = third
    in_half = (lane // half_rows) == parity
    for step, out in enumerate(outs):
        head, half = head_and_half(here ^ step)
        rows = pl.ds(pl.multiple_of(half * half_rows, half_rows), half_rows)
        cols = pl.ds(pl.multiple_of(head * LANES, LANES), LANES)
        out[:half_rows, :] = q_ref[rows, cols]
        out[half_rows : 2 * half_rows, :] = dmem_ref[rows, cols]
        row = delta_ref[pl.ds(head, 1), :]
        rolled = jnp.concatenate([row[:, half_rows:], row[:, :half_rows]], axis=1)
        ext_ref[...] = halves_ref[half]
        ext_ref[bias_rows : bias_rows + 1, :] = jnp.where(in_half, jnp.where(parity == half, row, rolled), 0.0)
        out[2 * half_rows :, :] = ext_ref[...].astype(jnp.bfloat16)


def assemble(heads, quarter, *refs):
    out = refs[-1]
    here = position_here(heads)
    for step, ref in enumerate(refs[:-1]):
        at = pl.ds(pl.multiple_of((here ^ step) * quarter, quarter), quarter)
        out[0, at, :] = ref[:quarter, :]
        out[1, at, :] = ref[quarter:, :]


def attend(count, halves, per, width, tile, own_ref, mate_ref, *refs):
    packets = refs[:count]
    outs = refs[count : 2 * count]
    gate_ref, mark, qx, dm, delta, scores, high, total, acc = refs[2 * count :]
    units = qx.shape[1] // LANES - 1
    sides = (own_ref, mate_ref)
    steps_side = own_ref.shape[1] // width
    rows_unit = mark.shape[0]
    scale = 1.0 / math.sqrt(LANES)
    exponent = scale * math.log2(math.e)
    bias_rows = units * per

    lane = lax.broadcasted_iota(jnp.int32, (BLK, LANES), 1)
    for block in range(LANES):
        mark[block * BLK : (block + 1) * BLK, :] = jnp.where(lane == block, 1.0, 0.0).astype(jnp.bfloat16)

    delta_rows = []
    gate_sum = jnp.zeros((1, LANES), jnp.float32)
    for source, packet in enumerate(packets):
        base = source * halves
        qx[base : base + halves, :LANES] = packet[:halves, :]
        dm[base : base + halves, :] = packet[halves : 2 * halves, :]
        extra = packet[2 * halves :, :].astype(jnp.float32)
        for unit in range(units):
            for block in range(per):
                at = unit * per + block
                row = jnp.broadcast_to(extra[at : at + 1], (BLK, LANES)).astype(jnp.bfloat16)
                qx[base + block * BLK : base + (block + 1) * BLK, (1 + unit) * LANES : (2 + unit) * LANES] = row
        delta_rows.append(extra[bias_rows : bias_rows + 1])
        for part in range(1, 4):
            gate_sum = gate_sum + extra[bias_rows + part : bias_rows + part + 1]
    gate_ref[...] = jnp.broadcast_to(gate_sum, gate_ref.shape)
    parity = lax.axis_index("grp") % 2
    for pair in range(count // 2):
        row = delta_rows[2 * pair] + delta_rows[2 * pair + 1]
        wide = jnp.broadcast_to(row, (LANES, LANES)).T
        lower, upper = wide[:halves], wide[halves:]
        delta[pair * LANES : pair * LANES + halves, :] = jnp.where(parity == 0, lower, upper)
        delta[pair * LANES + halves : (pair + 1) * LANES, :] = jnp.where(parity == 0, upper, lower)

    def one_tile(index, carry):
        here = pl.ds(pl.multiple_of(index * tile, tile), tile)
        high[...] = jnp.full_like(high, -3e38)
        for side, ref in enumerate(sides):
            for unit in range(units // 2):

                def score(at, carry, side=side, ref=ref, unit=unit):
                    rows = pl.ds(pl.multiple_of(unit * rows_unit + at * width, width), width)
                    marks = pl.ds(pl.multiple_of(at * width, width), width)
                    lanes = (1 + side * (units // 2) + unit) * LANES
                    left = jnp.concatenate([qx[here, :LANES], qx[here, lanes : lanes + LANES]], axis=1)
                    right = jnp.concatenate([ref[0, rows, :], mark[marks, :]], axis=1)
                    got = lax.dot_general(
                        left, right, (((1,), (1,)), ((), ())), preferred_element_type=jnp.float32
                    )
                    scores[side * steps_side + unit * (rows_unit // width) + at] = got
                    best = high[...]
                    for column in range(width // LANES):
                        best = jnp.maximum(best, got[:, column * LANES : (column + 1) * LANES])
                    high[...] = best
                    return carry

                lax.fori_loop(0, rows_unit // width, score, 0, unroll=2)
        high[...] = jnp.broadcast_to(jnp.max(high[...], 1, keepdims=True) * exponent, high.shape)
        total[...] = jnp.zeros_like(total)
        acc[...] = jnp.zeros_like(acc)
        for side, ref in enumerate(sides):

            def back(at, carry, side=side, ref=ref):
                rows = pl.ds(pl.multiple_of(at * width, width), width)
                prod = lax.dot_general(
                    dm[here, :], ref[1, rows, :], (((1,), (1,)), ((), ())), preferred_element_type=jnp.float32
                )
                got = scores[side * steps_side + at]
                level = high[...]
                less = delta[here, :]
                added = total[...]
                pieces = []
                for column in range(width // LANES):
                    cols = slice(column * LANES, (column + 1) * LANES)
                    expo = jnp.exp2(got[:, cols] * exponent - level)
                    added = added + expo
                    pieces.append((expo * (prod[:, cols] - less)).astype(jnp.bfloat16))
                total[...] = added
                acc[...] += jnp.dot(
                    jnp.concatenate(pieces, axis=1), ref[0, rows, :], preferred_element_type=jnp.float32
                )
                return carry

            lax.fori_loop(0, steps_side, back, 0, unroll=2)
        weight = scale / jnp.sum(total[...], 1, keepdims=True)
        dm[here, :] = (acc[...] * weight).astype(jnp.bfloat16)
        return carry

    lax.fori_loop(0, dm.shape[0] // tile, one_tile, 0)
    for source, out in enumerate(outs):
        out[...] = dm[source * halves : (source + 1) * halves, :]


def unpack(heads, *refs):
    out_ref = refs[-1]
    here = position_here(heads)
    for step, ref in enumerate(refs[:-1]):
        head, half = head_and_half(here ^ step)
        half_rows = ref.shape[0]
        rows = pl.ds(pl.multiple_of(half * half_rows, half_rows), half_rows)
        cols = pl.ds(pl.multiple_of(head * LANES, LANES), LANES)
        out_ref[rows, cols] = ref[...]


def local(queries, d_out, o_mem, local_out, mem_keys, mem_values, gate_logit, block_ids):
    shards = lax.axis_size("mem")
    groups = lax.axis_size("grp")
    tokens = queries.shape[1]
    width = queries.shape[2]
    heads = gate_logit.shape[0]
    rows_dev = mem_keys.shape[0]
    qblocks = tokens // BLK
    members = 2 * heads
    chunks = shards // heads
    assert width == heads * LANES and shards % heads == 0 and groups % 2 == 0
    assert rows_dev == 16 * BLK and heads * 8 == LANES and tokens == LANES
    quarter = rows_dev // 4
    halves = tokens // 2
    per = qblocks // 2
    units = 2 * chunks
    bias_rows = units * per
    extra = -(-(bias_rows + 4) // 16) * 16
    packet = 2 * halves + extra
    vmem = pl.BlockSpec(memory_space=pltpu.VMEM)
    smem = pl.BlockSpec(memory_space=pltpu.SMEM)
    bf16 = jnp.bfloat16

    def swap(pieces, only=None):
        got = list(pieces)
        for step in range(members) if only is None else only:
            if step == 0:
                continue
            pairs = []
            for mem in range(shards):
                for grp in range(groups):
                    other = ((mem % heads) * 2 + grp % 2) ^ step
                    to_mem = mem - mem % heads + (other >> 1)
                    to_grp = grp - grp % 2 + (other & 1)
                    pairs.append((mem * groups + grp, to_mem * groups + to_grp))
            got[step] = lax.ppermute(pieces[step], AXES, pairs)
        return got

    small = pltpu.CompilerParams(vmem_limit_bytes=24 << 20)
    rows_out = pl.pallas_call(
        functools.partial(pack_rows, quarter, heads),
        out_shape=[jax.ShapeDtypeStruct((2 * quarter, LANES), bf16)] * members,
        in_specs=[vmem, vmem],
        out_specs=[vmem] * members,
        compiler_params=small,
        name="pack_rows",
    )(mem_keys, mem_values)
    rows_in = swap(rows_out)
    tokens_out = pl.pallas_call(
        functools.partial(pack_tokens, heads, chunks),
        out_shape=[jax.ShapeDtypeStruct((packet, LANES), bf16)] * members,
        in_specs=[vmem, vmem, vmem, vmem, smem, vmem],
        out_specs=[vmem] * members,
        scratch_shapes=[
            pltpu.VMEM((tokens, width), bf16),
            pltpu.VMEM((2, extra, LANES), jnp.float32),
            pltpu.VMEM((extra, LANES), jnp.float32),
            pltpu.VMEM((heads, LANES), jnp.float32),
            pltpu.VMEM((LANES, LANES), jnp.float32),
        ],
        compiler_params=small,
        name="pack_tokens",
    )(queries[0], d_out[0], o_mem[0], local_out[0], gate_logit, block_ids[0])
    tokens_in = swap(tokens_out)
    own = pl.pallas_call(
        functools.partial(assemble, heads, quarter),
        out_shape=jax.ShapeDtypeStruct((2, members * quarter, LANES), bf16),
        in_specs=[vmem] * members,
        out_specs=vmem,
        compiler_params=small,
        name="assemble",
    )(*rows_in)
    if chunks > 1:
        same = [[mo * heads + mi for mo in range(chunks)] for mi in range(heads)]
        own = lax.all_gather(own, "mem", axis_index_groups=same, axis=1, tiled=True)
    mate = lax.ppermute(own, "mem", [(i, i ^ 1) for i in range(shards)])

    rows_all = 2 * own.shape[1]
    step_width = 512
    tile = 512 if chunks == 1 else 256
    calls = 2
    count = members // calls
    flops = 2 * count * halves * rows_all * LANES * 4

    def attend_some(packets):
        return pl.pallas_call(
            functools.partial(attend, count, halves, per, step_width, tile),
            out_shape=[jax.ShapeDtypeStruct((halves, LANES), bf16)] * count
            + [jax.ShapeDtypeStruct((8, LANES), jnp.float32)],
            in_specs=[vmem] * (2 + count),
            out_specs=[vmem] * (count + 1),
            scratch_shapes=[
                pltpu.VMEM((LANES * BLK, LANES), bf16),
                pltpu.VMEM((count * halves, (1 + units) * LANES), bf16),
                pltpu.VMEM((count * halves, LANES), bf16),
                pltpu.VMEM((count * halves, LANES), jnp.float32),
                pltpu.VMEM((rows_all // step_width, tile, step_width), jnp.float32),
                pltpu.VMEM((tile, LANES), jnp.float32),
                pltpu.VMEM((tile, LANES), jnp.float32),
                pltpu.VMEM((tile, LANES), jnp.float32),
            ],
            compiler_params=pltpu.CompilerParams(vmem_limit_bytes=(24 if chunks == 1 else 48) << 20),
            cost_estimate=pl.CostEstimate(
                flops=flops, bytes_accessed=4 * rows_all * LANES, transcendentals=count * halves * rows_all
            ),
            name="attend",
        )(own, mate, *packets)

    home = [None] * members
    gate_total = jnp.zeros((heads,), jnp.float32)
    for call in range(calls):
        steps = [s for s in range(members) if (s >> 1) % calls == call]
        *grads, gate_sum = attend_some([tokens_in[s] for s in steps])
        gate_total = gate_total + gate_sum[0, :heads]
        sparse = [None] * members
        for s, grad in zip(steps, grads):
            sparse[s] = grad
        back = swap(sparse, only=steps)
        for s in steps:
            home[s] = back[s]
    d_query = pl.pallas_call(
        functools.partial(unpack, heads),
        out_shape=jax.ShapeDtypeStruct((tokens, width), bf16),
        in_specs=[vmem] * members,
        out_specs=vmem,
        compiler_params=small,
        name="unpack",
    )(*home)
    if shards * groups != members:
        gate_total = lax.psum(gate_total, AXES) / members
    sig = jax.nn.sigmoid(gate_logit)
    d_gate = sig * (1.0 - sig) * gate_total / (shards * groups * tokens * LANES) ** 0.5
    return (d_query[None], d_gate)


def solution(mesh):
    placed = (
        P("grp", "mem", None),
        P("grp", "mem", None),
        P("grp", "mem", None),
        P("grp", "mem", None),
        P("mem", None),
        P("mem", None),
        P(),
        P("grp", "mem", None),
    )
    return jax.shard_map(
        local, mesh=mesh, in_specs=placed, out_specs=(P("grp", "mem", None), P()), check_vma=False
    )
```

```python
import functools
import math

import jax
import jax.numpy as jnp
from jax import lax
from jax.experimental import pallas as pl
from jax.experimental.pallas import tpu as pltpu
from jax.sharding import PartitionSpec as P

BLK = 16
LANES = 128
AXES = ("mem", "grp")
FAR = -1e30


def head_and_half(position):
    return (position >> 2) * 2 + (position & 1), (position >> 1) & 1


def pack(
    heads,
    chunks,
    early,
    k_hbm,
    v_hbm,
    q_hbm,
    dout_hbm,
    omem_hbm,
    local_hbm,
    gate_ref,
    ids_ref,
    first_out,
    second_out,
    k_ref,
    v_ref,
    q_ref,
    dout_ref,
    omem_ref,
    local_ref,
    dmem_ref,
    halves_ref,
    delta_ref,
    gate_rows,
    sems,
):
    tokens = q_ref.shape[0]
    half_rows = tokens // 2
    half_shard = k_ref.shape[0]
    quarter = half_shard // 2
    qblocks, names = ids_ref.shape
    high = lax.Precision.HIGHEST
    parity = lax.axis_index("grp") % 2
    mine = pl.ds(pl.multiple_of(parity * half_shard, half_shard), half_shard)
    copies = []
    for at, (source, target) in enumerate(
        (
            (dout_hbm, dout_ref),
            (omem_hbm, omem_ref),
            (local_hbm, local_ref),
            (q_hbm, q_ref),
            (k_hbm.at[mine, :], k_ref),
            (v_hbm.at[mine, :], v_ref),
        )
    ):
        copy = pltpu.make_async_copy(source, target, sems.at[at])
        copy.start()
        copies.append(copy)

    lane = lax.broadcasted_iota(jnp.int32, (1, LANES), 1)
    ids = ids_ref[...]
    per = qblocks // 2
    bias_rows = 2 * chunks * per
    halves_ref[...] = jnp.zeros_like(halves_ref)
    for chunk in range(chunks):
        block = 16 * (chunk * heads + lane // 8) + 8 * ((lane // 4) % 2) + lane % 4
        for side in range(2):
            wanted = jnp.broadcast_to(block + 4 * side, (qblocks, LANES))
            hit = jnp.zeros((qblocks, LANES), jnp.float32)
            for name in range(names):
                hit = jnp.where(ids[:, name : name + 1] == wanted, 1.0, hit)
            table = jnp.where(hit > 0.5, 0.0, FAR)
            for half in range(2):
                at = ((half ^ side) * chunks + chunk) * per
                halves_ref[half, at : at + per, :] = table[half * per : (half + 1) * per]

    ones = jnp.ones((8, LANES), jnp.float32)
    gate_rows[...] = jnp.zeros_like(gate_rows)
    for copy in copies[:3]:
        copy.wait()
    for head in range(heads):
        cols = slice(head * LANES, (head + 1) * LANES)
        sig = jax.nn.sigmoid(jnp.full((8, LANES), gate_ref[head], jnp.float32))[:1]
        d_out = dout_ref[:, cols].astype(jnp.float32)
        o_mem = omem_ref[:, cols].astype(jnp.float32)
        d_mem = (d_out * sig).astype(jnp.bfloat16)
        dmem_ref[:, cols] = d_mem
        differ = o_mem - local_ref[:, cols].astype(jnp.float32)
        gate_rows[head : head + 1, :] = jnp.sum(d_out * differ, 0, keepdims=True)
        product = d_mem.astype(jnp.float32) * o_mem
        row = lax.dot_general(
            ones, product, (((1,), (1,)), ((), ())), precision=high, preferred_element_type=jnp.float32
        )
        delta_ref[head : head + 1, :] = row[:1]
    total = lax.dot_general(
        ones, gate_rows[...], (((1,), (1,)), ((), ())), precision=high, preferred_element_type=jnp.float32
    )[:1]
    first = total.astype(jnp.bfloat16).astype(jnp.float32)
    second = (total - first).astype(jnp.bfloat16).astype(jnp.float32)
    third = total - first - second
    for half in range(2):
        halves_ref[half, bias_rows + 1 : bias_rows + 2, :] = first
        halves_ref[half, bias_rows + 2 : bias_rows + 3, :] = second
        halves_ref[half, bias_rows + 3 : bias_rows + 4, :] = third
    in_half = (lane // half_rows) == parity
    for copy in copies[3:]:
        copy.wait()
    for position in range(2 * heads):
        head, half = head_and_half(position)
        cols = slice(head * LANES, (head + 1) * LANES)
        base = half * half_rows
        at = 2 * quarter
        first_out[position, :quarter, :] = k_ref[half * quarter : (half + 1) * quarter, cols]
        first_out[position, quarter:at, :] = v_ref[half * quarter : (half + 1) * quarter, cols]
        first_out[position, at : at + early, :] = q_ref[base : base + early, cols]
        first_out[position, at + early : at + 2 * early, :] = dmem_ref[base : base + early, cols]
        late = half_rows - early
        second_out[position, :late, :] = q_ref[base + early : base + half_rows, cols]
        second_out[position, late:, :] = dmem_ref[base + early : base + half_rows, cols]
        row = delta_ref[head : head + 1, :]
        rolled = jnp.concatenate([row[:, half_rows:], row[:, :half_rows]], axis=1)
        halves_ref[half, bias_rows : bias_rows + 1, :] = jnp.where(
            in_half, jnp.where(parity == half, row, rolled), 0.0
        )
        first_out[position, at + 2 * early :, :] = halves_ref[half].astype(jnp.bfloat16)


def assemble(in_ref, out_ref):
    quarter = out_ref.shape[1] // in_ref.shape[0]
    for source in range(in_ref.shape[0]):
        rows = slice(source * quarter, (source + 1) * quarter)
        out_ref[0, rows, :] = in_ref[source, :quarter, :]
        out_ref[1, rows, :] = in_ref[source, quarter : 2 * quarter, :]


def attend(
    begin, count, q_at, ext_at, per, width, tile, final, own_ref, mate_ref, q_ref, ext_ref, *refs
):
    if final:
        before_ref, out_ref, mark, minus, qx, dx, scores, high, total, acc = refs
    else:
        out_ref, gate_ref, mark, minus, qx, dx, scores, high, total, acc = refs
    sources = q_ref.shape[0]
    units = qx.shape[1] // LANES - 1
    sides = (own_ref, mate_ref)
    steps_side = own_ref.shape[1] // width
    rows_unit = mark.shape[0]
    scale = 1.0 / math.sqrt(LANES)
    exponent = scale * math.log2(math.e)
    bias_rows = units * per

    lane = lax.broadcasted_iota(jnp.int32, (BLK, LANES), 1)
    for block in range(LANES):
        mark[block * BLK : (block + 1) * BLK, :] = jnp.where(lane == block, 1.0, 0.0).astype(jnp.bfloat16)
    wide_lane = lax.broadcasted_iota(jnp.int32, (LANES, LANES), 1)
    for block in range(width // LANES):
        minus[block * LANES : (block + 1) * LANES, :] = jnp.where(wide_lane == 0, -1.0, 0.0).astype(jnp.bfloat16)

    gate_sum = jnp.zeros((1, LANES), jnp.float32)
    delta_row = None
    for source in range(sources):
        base = source * count
        qx[base : base + count, :LANES] = q_ref[source, q_at : q_at + count, :]
        dx[base : base + count, :LANES] = q_ref[source, q_at + count : q_at + 2 * count, :]
        extra = ext_ref[source, ext_at:, :].astype(jnp.float32)
        for unit in range(units):
            for block in range(count // BLK):
                at = unit * per + begin // BLK + block
                row = jnp.broadcast_to(extra[at : at + 1], (BLK, LANES)).astype(jnp.bfloat16)
                qx[base + block * BLK : base + (block + 1) * BLK, (1 + unit) * LANES : (2 + unit) * LANES] = row
        if not final:
            for part in range(1, 4):
                gate_sum = gate_sum + extra[bias_rows + part : bias_rows + part + 1]
        row = extra[bias_rows : bias_rows + 1]
        if source % 2 == 0:
            delta_row = row
            continue
        wide = jnp.broadcast_to(delta_row + row, (LANES, LANES)).T
        wide = jnp.where(wide_lane == 0, wide, 0.0).astype(jnp.bfloat16)
        dx[base - count : base, LANES:] = wide[begin : begin + count]
        dx[base : base + count, LANES:] = wide[LANES // 2 + begin : LANES // 2 + begin + count]
    if not final:
        gate_ref[...] = jnp.broadcast_to(gate_sum, gate_ref.shape)

    def one_tile(index, carry):
        here = pl.ds(pl.multiple_of(index * tile, tile), tile)
        high[...] = jnp.full_like(high, -3e38)
        for side, ref in enumerate(sides):
            for unit in range(units // 2):

                def score(at, carry, side=side, ref=ref, unit=unit):
                    rows = pl.ds(pl.multiple_of(unit * rows_unit + at * width, width), width)
                    marks = pl.ds(pl.multiple_of(at * width, width), width)
                    lanes = (1 + side * (units // 2) + unit) * LANES
                    left = jnp.concatenate([qx[here, :LANES], qx[here, lanes : lanes + LANES]], axis=1)
                    right = jnp.concatenate([ref[0, rows, :], mark[marks, :]], axis=1)
                    got = lax.dot_general(
                        left, right, (((1,), (1,)), ((), ())), preferred_element_type=jnp.float32
                    )
                    scores[side * steps_side + unit * (rows_unit // width) + at] = got
                    best = high[...]
                    for column in range(width // LANES):
                        best = jnp.maximum(best, got[:, column * LANES : (column + 1) * LANES])
                    high[...] = best
                    return carry

                lax.fori_loop(0, rows_unit // width, score, 0, unroll=True)
        high[...] = jnp.broadcast_to(jnp.max(high[...], 1, keepdims=True) * exponent, high.shape)
        total[...] = jnp.zeros_like(total)
        acc[...] = jnp.zeros_like(acc)
        for side, ref in enumerate(sides):

            def back(at, carry, side=side, ref=ref):
                rows = pl.ds(pl.multiple_of(at * width, width), width)
                prod = lax.dot_general(
                    dx[here, :],
                    jnp.concatenate([ref[1, rows, :], minus[...]], axis=1),
                    (((1,), (1,)), ((), ())),
                    preferred_element_type=jnp.float32,
                )
                got = scores[side * steps_side + at]
                level = high[...]
                added = total[...]
                pieces = []
                for column in range(width // LANES):
                    cols = slice(column * LANES, (column + 1) * LANES)
                    expo = jnp.exp2(got[:, cols] * exponent - level)
                    added = added + expo
                    pieces.append((expo * prod[:, cols]).astype(jnp.bfloat16))
                total[...] = added
                acc[...] += jnp.dot(
                    jnp.concatenate(pieces, axis=1), ref[0, rows, :], preferred_element_type=jnp.float32
                )
                return carry

            lax.fori_loop(0, steps_side, back, 0, unroll=4)
        weight = scale / jnp.sum(total[...], 1, keepdims=True)
        qx[here, :LANES] = (acc[...] * weight).astype(jnp.bfloat16)
        return carry

    lax.fori_loop(0, qx.shape[0] // tile, one_tile, 0)
    for source in range(sources):
        got = qx[source * count : (source + 1) * count, :LANES]
        if final:
            out_ref[source, :begin, :] = before_ref[source]
            out_ref[source, begin:, :] = got
        else:
            out_ref[source] = got


def unpack(heads, in_ref, out_ref):
    half_rows = in_ref.shape[1]
    for position in range(2 * heads):
        head, half = head_and_half(position)
        out_ref[half * half_rows : (half + 1) * half_rows, head * LANES : (head + 1) * LANES] = in_ref[position]


def local(queries, d_out, o_mem, local_out, mem_keys, mem_values, gate_logit, block_ids):
    shards = lax.axis_size("mem")
    groups = lax.axis_size("grp")
    tokens = queries.shape[1]
    width = queries.shape[2]
    heads = gate_logit.shape[0]
    rows_dev = mem_keys.shape[0]
    qblocks = tokens // BLK
    members = 2 * heads
    chunks = shards // heads
    assert width == heads * LANES and shards % heads == 0 and groups % 2 == 0
    assert rows_dev == 16 * BLK and heads * 8 == LANES and tokens == LANES
    quarter = rows_dev // 4
    halves = tokens // 2
    per = qblocks // 2
    units = 2 * chunks
    early = halves // 2
    late = halves - early
    extra = -(-(units * per + 4) // 16) * 16
    ext_at = 2 * quarter + 2 * early
    packet = ext_at + extra
    vmem = pl.BlockSpec(memory_space=pltpu.VMEM)
    smem = pl.BlockSpec(memory_space=pltpu.SMEM)
    hbm = pl.BlockSpec(memory_space=pltpu.HBM)
    bf16 = jnp.bfloat16
    small = pltpu.CompilerParams(vmem_limit_bytes=24 << 20)

    if shards * groups == members:
        head_groups = None
    else:
        head_groups = [
            [(mo * heads + mi) * groups + 2 * go + gp for mi in range(heads) for gp in range(2)]
            for mo in range(chunks)
            for go in range(groups // 2)
        ]
    exchange = functools.partial(
        lax.all_to_all, axis_name=AXES, split_axis=0, concat_axis=0, tiled=True, axis_index_groups=head_groups
    )

    first_out, second_out = pl.pallas_call(
        functools.partial(pack, heads, chunks, early),
        out_shape=(
            jax.ShapeDtypeStruct((members, packet, LANES), bf16),
            jax.ShapeDtypeStruct((members, 2 * late, LANES), bf16),
        ),
        in_specs=[hbm] * 6 + [smem, vmem],
        out_specs=(vmem, vmem),
        scratch_shapes=[pltpu.VMEM((rows_dev // 2, width), bf16)] * 2
        + [pltpu.VMEM((tokens, width), bf16)] * 5
        + [
            pltpu.VMEM((2, extra, LANES), jnp.float32),
            pltpu.VMEM((heads, LANES), jnp.float32),
            pltpu.VMEM((LANES, LANES), jnp.float32),
            pltpu.SemaphoreType.DMA((6,)),
        ],
        compiler_params=pltpu.CompilerParams(vmem_limit_bytes=56 << 20),
        name="pack",
    )(mem_keys, mem_values, queries[0], d_out[0], o_mem[0], local_out[0], gate_logit, block_ids[0])
    first_in = exchange(first_out)
    second_in = exchange(second_out)
    own = pl.pallas_call(
        assemble,
        out_shape=jax.ShapeDtypeStruct((2, members * quarter, LANES), bf16),
        in_specs=[vmem],
        out_specs=vmem,
        compiler_params=small,
        name="assemble",
    )(first_in)
    if chunks > 1:
        same = [[mo * heads + mi for mo in range(chunks)] for mi in range(heads)]
        own = lax.all_gather(own, "mem", axis_index_groups=same, axis=1, tiled=True)
    mate = lax.ppermute(own, "mem", [(i, i ^ 1) for i in range(shards)])

    rows_all = 2 * own.shape[1]
    step_width = 512
    tile = 512 if chunks == 1 else 256

    def attend_some(begin, count, q_at, final, out_shape, *args):
        return pl.pallas_call(
            functools.partial(attend, begin, count, q_at, ext_at, per, step_width, tile, final),
            out_shape=out_shape,
            in_specs=[vmem] * len(args),
            out_specs=[vmem] * len(out_shape),
            scratch_shapes=[
                pltpu.VMEM((LANES * BLK, LANES), bf16),
                pltpu.VMEM((step_width, LANES), bf16),
                pltpu.VMEM((members * count, (1 + units) * LANES), bf16),
                pltpu.VMEM((members * count, 2 * LANES), bf16),
                pltpu.VMEM((rows_all // step_width, tile, step_width), jnp.float32),
                pltpu.VMEM((tile, LANES), jnp.float32),
                pltpu.VMEM((tile, LANES), jnp.float32),
                pltpu.VMEM((tile, LANES), jnp.float32),
            ],
            compiler_params=pltpu.CompilerParams(vmem_limit_bytes=(24 if chunks == 1 else 44) << 20),
            cost_estimate=pl.CostEstimate(
                flops=2 * members * count * rows_all * LANES * 5,
                bytes_accessed=4 * rows_all * LANES,
                transcendentals=members * count * rows_all,
            ),
            name="attend",
        )(*args)

    part, gate_sum = attend_some(
        0,
        early,
        2 * quarter,
        False,
        [jax.ShapeDtypeStruct((members, early, LANES), bf16), jax.ShapeDtypeStruct((8, LANES), jnp.float32)],
        own,
        mate,
        first_in,
        first_in,
    )
    (grad,) = attend_some(
        early,
        late,
        0,
        True,
        [jax.ShapeDtypeStruct((members, halves, LANES), bf16)],
        own,
        mate,
        second_in,
        first_in,
        part,
    )
    home = exchange(grad)
    d_query = pl.pallas_call(
        functools.partial(unpack, heads),
        out_shape=jax.ShapeDtypeStruct((tokens, width), bf16),
        in_specs=[vmem],
        out_specs=vmem,
        compiler_params=small,
        name="unpack",
    )(home)
    gate_total = gate_sum[0, :heads]
    if head_groups is not None:
        gate_total = lax.psum(gate_total, AXES) / members
    sig = jax.nn.sigmoid(gate_logit)
    d_gate = sig * (1.0 - sig) * gate_total / (shards * groups * tokens * LANES) ** 0.5
    return (d_query[None], d_gate)


def solution(mesh):
    placed = (
        P("grp", "mem", None),
        P("grp", "mem", None),
        P("grp", "mem", None),
        P("grp", "mem", None),
        P("mem", None),
        P("mem", None),
        P(),
        P("grp", "mem", None),
    )
    return jax.shard_map(
        local, mesh=mesh, in_specs=placed, out_specs=(P("grp", "mem", None), P()), check_vma=False
    )
```

```python
import functools
import math

import jax
import jax.numpy as jnp
from jax import lax
from jax.experimental import pallas as pl
from jax.experimental.pallas import tpu as pltpu
from jax.sharding import PartitionSpec as P

BLK = 16
LANES = 128
AXES = ("mem", "grp")
FAR = -1e30


def head_and_half(position):
    return (position >> 2) * 2 + (position & 1), (position >> 1) & 1


def pack(
    heads,
    chunks,
    early,
    k_hbm,
    v_hbm,
    q_hbm,
    dout_hbm,
    omem_hbm,
    local_hbm,
    gate_ref,
    ids_ref,
    first_out,
    second_out,
    k_ref,
    v_ref,
    q_ref,
    dout_ref,
    omem_ref,
    local_ref,
    dmem_ref,
    halves_ref,
    delta_ref,
    gate_rows,
    sems,
):
    tokens = q_ref.shape[0]
    half_rows = tokens // 2
    half_shard = k_ref.shape[0]
    quarter = half_shard // 2
    qblocks, names = ids_ref.shape
    high = lax.Precision.HIGHEST
    parity = lax.axis_index("grp") % 2
    mine = pl.ds(pl.multiple_of(parity * half_shard, half_shard), half_shard)
    copies = []
    for at, (source, target) in enumerate(
        (
            (dout_hbm, dout_ref),
            (omem_hbm, omem_ref),
            (local_hbm, local_ref),
            (q_hbm, q_ref),
            (k_hbm.at[mine, :], k_ref),
            (v_hbm.at[mine, :], v_ref),
        )
    ):
        copy = pltpu.make_async_copy(source, target, sems.at[at])
        copy.start()
        copies.append(copy)

    lane = lax.broadcasted_iota(jnp.int32, (1, LANES), 1)
    ids = ids_ref[...]
    per = qblocks // 2
    bias_rows = 2 * chunks * per
    halves_ref[...] = jnp.zeros_like(halves_ref)
    for chunk in range(chunks):
        block = 16 * (chunk * heads + lane // 8) + 8 * ((lane // 4) % 2) + lane % 4
        for side in range(2):
            wanted = jnp.broadcast_to(block + 4 * side, (qblocks, LANES))
            hit = jnp.zeros((qblocks, LANES), jnp.float32)
            for name in range(names):
                hit = jnp.where(ids[:, name : name + 1] == wanted, 1.0, hit)
            table = jnp.where(hit > 0.5, 0.0, FAR)
            for half in range(2):
                at = ((half ^ side) * chunks + chunk) * per
                halves_ref[half, at : at + per, :] = table[half * per : (half + 1) * per]

    ones = jnp.ones((8, LANES), jnp.float32)
    wide_ones = jnp.ones((16, 2 * LANES), jnp.bfloat16)
    gate_rows[...] = jnp.zeros_like(gate_rows)
    for copy in copies[:3]:
        copy.wait()
    for head in range(heads):
        cols = slice(head * LANES, (head + 1) * LANES)
        sig = jax.nn.sigmoid(jnp.full((8, LANES), gate_ref[head], jnp.float32))[:1]
        d_out = dout_ref[:, cols].astype(jnp.float32)
        o_mem = omem_ref[:, cols].astype(jnp.float32)
        d_mem = (d_out * sig).astype(jnp.bfloat16)
        dmem_ref[:, cols] = d_mem
        differ = o_mem - local_ref[:, cols].astype(jnp.float32)
        gate_rows[head : head + 1, :] = jnp.sum(d_out * differ, 0, keepdims=True)
        product = d_mem.astype(jnp.float32) * o_mem
        upper = product.astype(jnp.bfloat16)
        lower = (product - upper.astype(jnp.float32)).astype(jnp.bfloat16)
        row = lax.dot_general(
            wide_ones,
            jnp.concatenate([upper, lower], axis=1),
            (((1,), (1,)), ((), ())),
            preferred_element_type=jnp.float32,
        )
        delta_ref[head : head + 1, :] = row[:1]
    total = lax.dot_general(
        ones, gate_rows[...], (((1,), (1,)), ((), ())), precision=high, preferred_element_type=jnp.float32
    )[:1]
    first = total.astype(jnp.bfloat16).astype(jnp.float32)
    second = (total - first).astype(jnp.bfloat16).astype(jnp.float32)
    third = total - first - second
    for half in range(2):
        halves_ref[half, bias_rows + 1 : bias_rows + 2, :] = first
        halves_ref[half, bias_rows + 2 : bias_rows + 3, :] = second
        halves_ref[half, bias_rows + 3 : bias_rows + 4, :] = third
    in_half = (lane // half_rows) == parity
    for copy in copies[3:]:
        copy.wait()
    for position in range(2 * heads):
        head, half = head_and_half(position)
        cols = slice(head * LANES, (head + 1) * LANES)
        base = half * half_rows
        at = 2 * quarter
        first_out[position, :quarter, :] = k_ref[half * quarter : (half + 1) * quarter, cols]
        first_out[position, quarter:at, :] = v_ref[half * quarter : (half + 1) * quarter, cols]
        first_out[position, at : at + early, :] = q_ref[base : base + early, cols]
        first_out[position, at + early : at + 2 * early, :] = dmem_ref[base : base + early, cols]
        late = half_rows - early
        second_out[position, :late, :] = q_ref[base + early : base + half_rows, cols]
        second_out[position, late:, :] = dmem_ref[base + early : base + half_rows, cols]
        row = delta_ref[head : head + 1, :]
        rolled = jnp.concatenate([row[:, half_rows:], row[:, :half_rows]], axis=1)
        halves_ref[half, bias_rows : bias_rows + 1, :] = jnp.where(
            in_half, jnp.where(parity == half, row, rolled), 0.0
        )
        first_out[position, at + 2 * early :, :] = halves_ref[half].astype(jnp.bfloat16)


def assemble(in_ref, out_ref):
    quarter = out_ref.shape[1] // in_ref.shape[0]
    for source in range(in_ref.shape[0]):
        rows = slice(source * quarter, (source + 1) * quarter)
        out_ref[0, rows, :] = in_ref[source, :quarter, :]
        out_ref[1, rows, :] = in_ref[source, quarter : 2 * quarter, :]


def attend(
    begin, count, q_at, ext_at, per, width, tile, final, own_ref, mate_ref, q_ref, ext_ref, *refs
):
    if final:
        before_ref, out_ref, mark, minus, qx, dx, scores, high, total, acc, kept = refs
    else:
        out_ref, gate_ref, mark, minus, qx, dx, scores, high, total, acc = refs
    sources = q_ref.shape[0]
    units = qx.shape[1] // LANES - 1
    sides = (own_ref, mate_ref)
    steps_side = own_ref.shape[1] // width
    rows_unit = mark.shape[0]
    scale = 1.0 / math.sqrt(LANES)
    exponent = scale * math.log2(math.e)
    bias_rows = units * per

    lane = lax.broadcasted_iota(jnp.int32, (BLK, LANES), 1)
    for block in range(LANES):
        mark[block * BLK : (block + 1) * BLK, :] = jnp.where(lane == block, 1.0, 0.0).astype(jnp.bfloat16)
    wide_lane = lax.broadcasted_iota(jnp.int32, (LANES, LANES), 1)
    for block in range(width // LANES):
        minus[block * LANES : (block + 1) * LANES, :] = jnp.where(wide_lane == 0, -1.0, 0.0).astype(jnp.bfloat16)

    gate_sum = jnp.zeros((1, LANES), jnp.float32)
    delta_row = None
    for source in range(sources):
        base = source * count
        qx[base : base + count, :LANES] = q_ref[source, q_at : q_at + count, :]
        dx[base : base + count, :LANES] = q_ref[source, q_at + count : q_at + 2 * count, :]
        extra = ext_ref[source, ext_at:, :].astype(jnp.float32)
        for unit in range(units):
            for block in range(count // BLK):
                at = unit * per + begin // BLK + block
                row = jnp.broadcast_to(extra[at : at + 1], (BLK, LANES)).astype(jnp.bfloat16)
                qx[base + block * BLK : base + (block + 1) * BLK, (1 + unit) * LANES : (2 + unit) * LANES] = row
        if not final:
            for part in range(1, 4):
                gate_sum = gate_sum + extra[bias_rows + part : bias_rows + part + 1]
        row = extra[bias_rows : bias_rows + 1]
        if source % 2 == 0:
            delta_row = row
            continue
        wide = jnp.broadcast_to(delta_row + row, (LANES, LANES)).T
        wide = jnp.where(wide_lane == 0, wide, 0.0).astype(jnp.bfloat16)
        dx[base - count : base, LANES:] = wide[begin : begin + count]
        dx[base : base + count, LANES:] = wide[LANES // 2 + begin : LANES // 2 + begin + count]
    if not final:
        gate_ref[...] = jnp.broadcast_to(gate_sum, gate_ref.shape)

    def one_tile(index, carry):
        here = pl.ds(pl.multiple_of(index * tile, tile), tile)
        groups = [slice(at, at + 64) for at in range(0, tile, 64)]
        high[...] = jnp.full_like(high, -3e38)
        for side, ref in enumerate(sides):
            for unit in range(units // 2):

                def score(at, carry, side=side, ref=ref, unit=unit):
                    rows = pl.ds(pl.multiple_of(unit * rows_unit + at * width, width), width)
                    marks = pl.ds(pl.multiple_of(at * width, width), width)
                    lanes = (1 + side * (units // 2) + unit) * LANES
                    left = jnp.concatenate([qx[here, :LANES], qx[here, lanes : lanes + LANES]], axis=1)
                    right = jnp.concatenate([ref[0, rows, :], mark[marks, :]], axis=1)
                    got = lax.dot_general(
                        left, right, (((1,), (1,)), ((), ())), preferred_element_type=jnp.float32
                    )
                    index = side * steps_side + unit * (rows_unit // width) + at
                    for group in groups:
                        piece = got[group]
                        scores[index, group, :] = piece
                        high[group] = jnp.maximum(high[group], jnp.maximum(piece[:, :LANES], piece[:, LANES:]))
                    return carry

                lax.fori_loop(0, rows_unit // width, score, 0, unroll=4)
        high[...] = jnp.broadcast_to(jnp.max(high[...], 1, keepdims=True) * exponent, high.shape)
        total[...] = jnp.zeros_like(total)
        acc[...] = jnp.zeros_like(acc)
        for side, ref in enumerate(sides):

            def back(at, carry, side=side, ref=ref):
                rows = pl.ds(pl.multiple_of(at * width, width), width)
                prod = lax.dot_general(
                    dx[here, :],
                    jnp.concatenate([ref[1, rows, :], minus[...]], axis=1),
                    (((1,), (1,)), ((), ())),
                    preferred_element_type=jnp.float32,
                )
                pieces = []
                for group in groups:
                    got = scores[side * steps_side + at, group, :]
                    level = high[group]
                    expo = [jnp.exp2(got[:, c : c + LANES] * exponent - level) for c in (0, LANES)]
                    total[group] += expo[0] + expo[1]
                    piece = jnp.concatenate(
                        [e * prod[group, c : c + LANES] for e, c in zip(expo, (0, LANES))], axis=1
                    ).astype(jnp.bfloat16)
                    if final:
                        kept[group, pl.ds(pl.multiple_of(side * steps_side * width + at * width, width), width)] = piece
                    else:
                        pieces.append(piece)
                if not final:
                    acc[...] += jnp.dot(
                        jnp.concatenate(pieces, axis=0), ref[0, rows, :], preferred_element_type=jnp.float32
                    )
                return carry

            lax.fori_loop(0, steps_side, back, 0, unroll=4)
        if final:
            for side, ref in enumerate(sides):
                cols = slice(side * steps_side * width, (side + 1) * steps_side * width)
                acc[...] += jnp.dot(kept[:, cols], ref[0], preferred_element_type=jnp.float32)
        weight = scale / jnp.sum(total[...], 1, keepdims=True)
        qx[here, :LANES] = (acc[...] * weight).astype(jnp.bfloat16)
        return carry

    lax.fori_loop(0, qx.shape[0] // tile, one_tile, 0)
    for source in range(sources):
        got = qx[source * count : (source + 1) * count, :LANES]
        if final:
            out_ref[source, :begin, :] = before_ref[source]
            out_ref[source, begin:, :] = got
        else:
            out_ref[source] = got


def unpack(heads, in_ref, out_ref):
    half_rows = in_ref.shape[1]
    for position in range(2 * heads):
        head, half = head_and_half(position)
        out_ref[half * half_rows : (half + 1) * half_rows, head * LANES : (head + 1) * LANES] = in_ref[position]


def local(queries, d_out, o_mem, local_out, mem_keys, mem_values, gate_logit, block_ids):
    shards = lax.axis_size("mem")
    groups = lax.axis_size("grp")
    tokens = queries.shape[1]
    width = queries.shape[2]
    heads = gate_logit.shape[0]
    rows_dev = mem_keys.shape[0]
    qblocks = tokens // BLK
    members = 2 * heads
    chunks = shards // heads
    assert width == heads * LANES and shards % heads == 0 and groups % 2 == 0
    assert rows_dev == 16 * BLK and heads * 8 == LANES and tokens == LANES
    quarter = rows_dev // 4
    halves = tokens // 2
    per = qblocks // 2
    units = 2 * chunks
    early = halves // 2
    late = halves - early
    extra = -(-(units * per + 4) // 16) * 16
    ext_at = 2 * quarter + 2 * early
    packet = ext_at + extra
    vmem = pl.BlockSpec(memory_space=pltpu.VMEM)
    smem = pl.BlockSpec(memory_space=pltpu.SMEM)
    hbm = pl.BlockSpec(memory_space=pltpu.HBM)
    bf16 = jnp.bfloat16
    small = pltpu.CompilerParams(vmem_limit_bytes=24 << 20)

    if shards * groups == members:
        head_groups = None
    else:
        head_groups = [
            [(mo * heads + mi) * groups + 2 * go + gp for mi in range(heads) for gp in range(2)]
            for mo in range(chunks)
            for go in range(groups // 2)
        ]
    exchange = functools.partial(
        lax.all_to_all, axis_name=AXES, split_axis=0, concat_axis=0, tiled=True, axis_index_groups=head_groups
    )

    first_out, second_out = pl.pallas_call(
        functools.partial(pack, heads, chunks, early),
        out_shape=(
            jax.ShapeDtypeStruct((members, packet, LANES), bf16),
            jax.ShapeDtypeStruct((members, 2 * late, LANES), bf16),
        ),
        in_specs=[hbm] * 6 + [smem, vmem],
        out_specs=(vmem, vmem),
        scratch_shapes=[pltpu.VMEM((rows_dev // 2, width), bf16)] * 2
        + [pltpu.VMEM((tokens, width), bf16)] * 5
        + [
            pltpu.VMEM((2, extra, LANES), jnp.float32),
            pltpu.VMEM((heads, LANES), jnp.float32),
            pltpu.VMEM((LANES, LANES), jnp.float32),
            pltpu.SemaphoreType.DMA((6,)),
        ],
        compiler_params=pltpu.CompilerParams(vmem_limit_bytes=56 << 20),
        name="pack",
    )(mem_keys, mem_values, queries[0], d_out[0], o_mem[0], local_out[0], gate_logit, block_ids[0])
    first_in = exchange(first_out)
    second_in = exchange(second_out)
    own = pl.pallas_call(
        assemble,
        out_shape=jax.ShapeDtypeStruct((2, members * quarter, LANES), bf16),
        in_specs=[vmem],
        out_specs=vmem,
        compiler_params=small,
        name="assemble",
    )(first_in)
    if chunks > 1:
        same = [[mo * heads + mi for mo in range(chunks)] for mi in range(heads)]
        own = lax.all_gather(own, "mem", axis_index_groups=same, axis=1, tiled=True)
    mate = lax.ppermute(own, "mem", [(i, i ^ 1) for i in range(shards)])

    rows_all = 2 * own.shape[1]
    step_width = 2 * LANES
    tile = 512 if chunks == 1 else 256

    def attend_some(begin, count, q_at, final, out_shape, *args):
        return pl.pallas_call(
            functools.partial(attend, begin, count, q_at, ext_at, per, step_width, tile, final),
            out_shape=out_shape,
            in_specs=[vmem] * len(args),
            out_specs=[vmem] * len(out_shape),
            scratch_shapes=[
                pltpu.VMEM((LANES * BLK, LANES), bf16),
                pltpu.VMEM((step_width, LANES), bf16),
                pltpu.VMEM((members * count, (1 + units) * LANES), bf16),
                pltpu.VMEM((members * count, 2 * LANES), bf16),
                pltpu.VMEM((rows_all // step_width, tile, step_width), jnp.float32),
                pltpu.VMEM((tile, LANES), jnp.float32),
                pltpu.VMEM((tile, LANES), jnp.float32),
                pltpu.VMEM((tile, LANES), jnp.float32),
            ]
            + [pltpu.VMEM((tile, rows_all), bf16)] * final,
            compiler_params=pltpu.CompilerParams(vmem_limit_bytes=(24 if chunks == 1 else 44) << 20),
            cost_estimate=pl.CostEstimate(
                flops=2 * members * count * rows_all * LANES * 5,
                bytes_accessed=4 * rows_all * LANES,
                transcendentals=members * count * rows_all,
            ),
            name="attend",
        )(*args)

    part, gate_sum = attend_some(
        0,
        early,
        2 * quarter,
        False,
        [jax.ShapeDtypeStruct((members, early, LANES), bf16), jax.ShapeDtypeStruct((8, LANES), jnp.float32)],
        own,
        mate,
        first_in,
        first_in,
    )
    (grad,) = attend_some(
        early,
        late,
        0,
        True,
        [jax.ShapeDtypeStruct((members, halves, LANES), bf16)],
        own,
        mate,
        second_in,
        first_in,
        part,
    )
    home = exchange(grad)
    d_query = pl.pallas_call(
        functools.partial(unpack, heads),
        out_shape=jax.ShapeDtypeStruct((tokens, width), bf16),
        in_specs=[vmem],
        out_specs=vmem,
        compiler_params=small,
        name="unpack",
    )(home)
    gate_total = gate_sum[0, :heads]
    if head_groups is not None:
        gate_total = lax.psum(gate_total, AXES) / members
    sig = jax.nn.sigmoid(gate_logit)
    d_gate = sig * (1.0 - sig) * gate_total / (shards * groups * tokens * LANES) ** 0.5
    return (d_query[None], d_gate)


def solution(mesh):
    placed = (
        P("grp", "mem", None),
        P("grp", "mem", None),
        P("grp", "mem", None),
        P("grp", "mem", None),
        P("mem", None),
        P("mem", None),
        P(),
        P("grp", "mem", None),
    )
    return jax.shard_map(
        local, mesh=mesh, in_specs=placed, out_specs=(P("grp", "mem", None), P()), check_vma=False
    )
```

```python
import functools
import math

import jax
import jax.numpy as jnp
from jax import lax
from jax.experimental import pallas as pl
from jax.experimental.pallas import tpu as pltpu
from jax.sharding import PartitionSpec as P

BLK = 16
LANES = 128
AXES = ("mem", "grp")
FAR = -1e30


def head_and_half(position):
    return (position >> 2) * 2 + (position & 1), (position >> 1) & 1


def pack(
    heads,
    chunks,
    early,
    k_hbm,
    v_hbm,
    q_hbm,
    dout_hbm,
    omem_hbm,
    local_hbm,
    gate_ref,
    ids_ref,
    first_out,
    second_out,
    k_ref,
    v_ref,
    q_ref,
    dout_ref,
    omem_ref,
    local_ref,
    dmem_ref,
    halves_ref,
    delta_ref,
    gate_rows,
    sems,
):
    tokens = q_ref.shape[0]
    half_rows = tokens // 2
    half_shard = k_ref.shape[0]
    quarter = half_shard // 2
    qblocks, names = ids_ref.shape
    high = lax.Precision.HIGHEST
    parity = lax.axis_index("grp") % 2
    mine = pl.ds(pl.multiple_of(parity * half_shard, half_shard), half_shard)
    copies = []
    for at, (source, target) in enumerate(
        (
            (dout_hbm, dout_ref),
            (omem_hbm, omem_ref),
            (local_hbm, local_ref),
            (q_hbm, q_ref),
            (k_hbm.at[mine, :], k_ref),
            (v_hbm.at[mine, :], v_ref),
        )
    ):
        copy = pltpu.make_async_copy(source, target, sems.at[at])
        copy.start()
        copies.append(copy)

    lane = lax.broadcasted_iota(jnp.int32, (1, LANES), 1)
    ids = ids_ref[...]
    per = qblocks // 2
    bias_rows = 2 * chunks * per
    halves_ref[...] = jnp.zeros_like(halves_ref)
    for chunk in range(chunks):
        block = 16 * (chunk * heads + lane // 8) + 8 * ((lane // 4) % 2) + lane % 4
        for side in range(2):
            wanted = jnp.broadcast_to(block + 4 * side, (qblocks, LANES))
            hit = jnp.zeros((qblocks, LANES), jnp.float32)
            for name in range(names):
                hit = jnp.where(ids[:, name : name + 1] == wanted, 1.0, hit)
            table = jnp.where(hit > 0.5, 0.0, FAR)
            for half in range(2):
                at = ((half ^ side) * chunks + chunk) * per
                halves_ref[half, at : at + per, :] = table[half * per : (half + 1) * per]

    ones = jnp.ones((8, LANES), jnp.float32)
    wide_ones = jnp.ones((16, 2 * LANES), jnp.bfloat16)
    gate_rows[...] = jnp.zeros_like(gate_rows)
    for copy in copies[:3]:
        copy.wait()
    for head in range(heads):
        cols = slice(head * LANES, (head + 1) * LANES)
        sig = jax.nn.sigmoid(jnp.full((8, LANES), gate_ref[head], jnp.float32))[:1]
        d_out = dout_ref[:, cols].astype(jnp.float32)
        o_mem = omem_ref[:, cols].astype(jnp.float32)
        d_mem = (d_out * sig).astype(jnp.bfloat16)
        dmem_ref[:, cols] = d_mem
        differ = o_mem - local_ref[:, cols].astype(jnp.float32)
        gate_rows[head : head + 1, :] = jnp.sum(d_out * differ, 0, keepdims=True)
        product = d_mem.astype(jnp.float32) * o_mem
        upper = product.astype(jnp.bfloat16)
        lower = (product - upper.astype(jnp.float32)).astype(jnp.bfloat16)
        row = lax.dot_general(
            wide_ones,
            jnp.concatenate([upper, lower], axis=1),
            (((1,), (1,)), ((), ())),
            preferred_element_type=jnp.float32,
        )
        delta_ref[head : head + 1, :] = row[:1]
    total = lax.dot_general(
        ones, gate_rows[...], (((1,), (1,)), ((), ())), precision=high, preferred_element_type=jnp.float32
    )[:1]
    first = total.astype(jnp.bfloat16).astype(jnp.float32)
    second = (total - first).astype(jnp.bfloat16).astype(jnp.float32)
    third = total - first - second
    for half in range(2):
        halves_ref[half, bias_rows + 1 : bias_rows + 2, :] = first
        halves_ref[half, bias_rows + 2 : bias_rows + 3, :] = second
        halves_ref[half, bias_rows + 3 : bias_rows + 4, :] = third
    in_half = (lane // half_rows) == parity
    for copy in copies[3:]:
        copy.wait()
    for position in range(2 * heads):
        head, half = head_and_half(position)
        cols = slice(head * LANES, (head + 1) * LANES)
        base = half * half_rows
        at = 2 * quarter
        first_out[position, :quarter, :] = k_ref[half * quarter : (half + 1) * quarter, cols]
        first_out[position, quarter:at, :] = v_ref[half * quarter : (half + 1) * quarter, cols]
        first_out[position, at : at + early, :] = q_ref[base : base + early, cols]
        first_out[position, at + early : at + 2 * early, :] = dmem_ref[base : base + early, cols]
        late = half_rows - early
        second_out[position, :late, :] = q_ref[base + early : base + half_rows, cols]
        second_out[position, late:, :] = dmem_ref[base + early : base + half_rows, cols]
        row = delta_ref[head : head + 1, :]
        rolled = jnp.concatenate([row[:, half_rows:], row[:, :half_rows]], axis=1)
        halves_ref[half, bias_rows : bias_rows + 1, :] = jnp.where(
            in_half, jnp.where(parity == half, row, rolled), 0.0
        )
        first_out[position, at + 2 * early :, :] = halves_ref[half].astype(jnp.bfloat16)


def assemble(in_ref, out_ref):
    quarter = out_ref.shape[1] // in_ref.shape[0]
    for source in range(in_ref.shape[0]):
        rows = slice(source * quarter, (source + 1) * quarter)
        out_ref[0, rows, :] = in_ref[source, :quarter, :]
        out_ref[1, rows, :] = in_ref[source, quarter : 2 * quarter, :]


def attend(
    begin, count, q_at, ext_at, per, width, tile, final, own_ref, mate_ref, q_ref, ext_ref, *refs
):
    if final:
        out_ref, mark, minus, qx, dx, scores, high, total, acc = refs
    else:
        out_ref, gate_ref, mark, minus, qx, dx, scores, high, total, acc = refs
    sources = q_ref.shape[0]
    units = qx.shape[1] // LANES - 1
    sides = (own_ref, mate_ref)
    steps_side = own_ref.shape[1] // width
    rows_unit = mark.shape[0]
    scale = 1.0 / math.sqrt(LANES)
    exponent = scale * math.log2(math.e)
    bias_rows = units * per

    lane = lax.broadcasted_iota(jnp.int32, (BLK, LANES), 1)
    for block in range(LANES):
        mark[block * BLK : (block + 1) * BLK, :] = jnp.where(lane == block, 1.0, 0.0).astype(jnp.bfloat16)
    wide_lane = lax.broadcasted_iota(jnp.int32, (LANES, LANES), 1)
    for block in range(width // LANES):
        minus[block * LANES : (block + 1) * LANES, :] = jnp.where(wide_lane == 0, -1.0, 0.0).astype(jnp.bfloat16)

    gate_sum = jnp.zeros((1, LANES), jnp.float32)
    delta_row = None
    for source in range(sources):
        base = source * count
        qx[base : base + count, :LANES] = q_ref[source, q_at : q_at + count, :]
        dx[base : base + count, :LANES] = q_ref[source, q_at + count : q_at + 2 * count, :]
        extra = ext_ref[source, ext_at:, :].astype(jnp.float32)
        for unit in range(units):
            for block in range(count // BLK):
                at = unit * per + begin // BLK + block
                row = jnp.broadcast_to(extra[at : at + 1], (BLK, LANES)).astype(jnp.bfloat16)
                qx[base + block * BLK : base + (block + 1) * BLK, (1 + unit) * LANES : (2 + unit) * LANES] = row
        if not final:
            for part in range(1, 4):
                gate_sum = gate_sum + extra[bias_rows + part : bias_rows + part + 1]
        row = extra[bias_rows : bias_rows + 1]
        if source % 2 == 0:
            delta_row = row
            continue
        wide = jnp.broadcast_to(delta_row + row, (LANES, LANES)).T
        wide = jnp.where(wide_lane == 0, wide, 0.0).astype(jnp.bfloat16)
        dx[base - count : base, LANES:] = wide[begin : begin + count]
        dx[base : base + count, LANES:] = wide[LANES // 2 + begin : LANES // 2 + begin + count]
    if not final:
        gate_ref[...] = jnp.broadcast_to(gate_sum, gate_ref.shape)

    def one_tile(index, carry):
        here = pl.ds(pl.multiple_of(index * tile, tile), tile)
        high[...] = jnp.full_like(high, -3e38)
        for side, ref in enumerate(sides):
            for unit in range(units // 2):

                def score(at, carry, side=side, ref=ref, unit=unit):
                    rows = pl.ds(pl.multiple_of(unit * rows_unit + at * width, width), width)
                    marks = pl.ds(pl.multiple_of(at * width, width), width)
                    lanes = (1 + side * (units // 2) + unit) * LANES
                    left = jnp.concatenate([qx[here, :LANES], qx[here, lanes : lanes + LANES]], axis=1)
                    right = jnp.concatenate([ref[0, rows, :], mark[marks, :]], axis=1)
                    got = lax.dot_general(
                        left, right, (((1,), (1,)), ((), ())), preferred_element_type=jnp.float32
                    )
                    scores[side * steps_side + unit * (rows_unit // width) + at] = got
                    best = high[...]
                    for column in range(width // LANES):
                        best = jnp.maximum(best, got[:, column * LANES : (column + 1) * LANES])
                    high[...] = best
                    return carry

                lax.fori_loop(0, rows_unit // width, score, 0, unroll=True)
        high[...] = jnp.broadcast_to(jnp.max(high[...], 1, keepdims=True) * exponent, high.shape)
        total[...] = jnp.zeros_like(total)
        acc[...] = jnp.zeros_like(acc)
        for side, ref in enumerate(sides):

            def back(at, carry, side=side, ref=ref):
                rows = pl.ds(pl.multiple_of(at * width, width), width)
                prod = lax.dot_general(
                    dx[here, :],
                    jnp.concatenate([ref[1, rows, :], minus[...]], axis=1),
                    (((1,), (1,)), ((), ())),
                    preferred_element_type=jnp.float32,
                )
                got = scores[side * steps_side + at]
                level = high[...]
                added = total[...]
                pieces = []
                for column in range(width // LANES):
                    cols = slice(column * LANES, (column + 1) * LANES)
                    expo = jnp.exp2(got[:, cols] * exponent - level)
                    added = added + expo
                    pieces.append((expo * prod[:, cols]).astype(jnp.bfloat16))
                total[...] = added
                acc[...] += jnp.dot(
                    jnp.concatenate(pieces, axis=1), ref[0, rows, :], preferred_element_type=jnp.float32
                )
                return carry

            lax.fori_loop(0, steps_side, back, 0, unroll=4)
        weight = scale / jnp.sum(total[...], 1, keepdims=True)
        qx[here, :LANES] = (acc[...] * weight).astype(jnp.bfloat16)
        return carry

    lax.fori_loop(0, qx.shape[0] // tile, one_tile, 0)
    for source in range(sources):
        out_ref[source] = qx[source * count : (source + 1) * count, :LANES]


def unpack(heads, early_ref, late_ref, out_ref):
    early, late = early_ref.shape[1], late_ref.shape[1]
    for position in range(2 * heads):
        head, half = head_and_half(position)
        cols = slice(head * LANES, (head + 1) * LANES)
        middle = half * (early + late) + early
        out_ref[middle - early : middle, cols] = early_ref[position]
        out_ref[middle : middle + late, cols] = late_ref[position]


def local(queries, d_out, o_mem, local_out, mem_keys, mem_values, gate_logit, block_ids):
    shards = lax.axis_size("mem")
    groups = lax.axis_size("grp")
    tokens = queries.shape[1]
    width = queries.shape[2]
    heads = gate_logit.shape[0]
    rows_dev = mem_keys.shape[0]
    qblocks = tokens // BLK
    members = 2 * heads
    chunks = shards // heads
    assert width == heads * LANES and shards % heads == 0 and groups % 2 == 0
    assert rows_dev == 16 * BLK and heads * 8 == LANES and tokens == LANES
    quarter = rows_dev // 4
    halves = tokens // 2
    per = qblocks // 2
    units = 2 * chunks
    early = halves // 2
    late = halves - early
    extra = -(-(units * per + 4) // 16) * 16
    ext_at = 2 * quarter + 2 * early
    packet = ext_at + extra
    vmem = pl.BlockSpec(memory_space=pltpu.VMEM)
    smem = pl.BlockSpec(memory_space=pltpu.SMEM)
    hbm = pl.BlockSpec(memory_space=pltpu.HBM)
    bf16 = jnp.bfloat16
    small = pltpu.CompilerParams(vmem_limit_bytes=24 << 20)

    if shards * groups == members:
        head_groups = None
    else:
        head_groups = [
            [(mo * heads + mi) * groups + 2 * go + gp for mi in range(heads) for gp in range(2)]
            for mo in range(chunks)
            for go in range(groups // 2)
        ]
    exchange = functools.partial(
        lax.all_to_all, axis_name=AXES, split_axis=0, concat_axis=0, tiled=True, axis_index_groups=head_groups
    )

    first_out, second_out = pl.pallas_call(
        functools.partial(pack, heads, chunks, early),
        out_shape=(
            jax.ShapeDtypeStruct((members, packet, LANES), bf16),
            jax.ShapeDtypeStruct((members, 2 * late, LANES), bf16),
        ),
        in_specs=[hbm] * 6 + [smem, vmem],
        out_specs=(vmem, vmem),
        scratch_shapes=[pltpu.VMEM((rows_dev // 2, width), bf16)] * 2
        + [pltpu.VMEM((tokens, width), bf16)] * 5
        + [
            pltpu.VMEM((2, extra, LANES), jnp.float32),
            pltpu.VMEM((heads, LANES), jnp.float32),
            pltpu.VMEM((LANES, LANES), jnp.float32),
            pltpu.SemaphoreType.DMA((6,)),
        ],
        compiler_params=pltpu.CompilerParams(vmem_limit_bytes=56 << 20),
        name="pack",
    )(mem_keys, mem_values, queries[0], d_out[0], o_mem[0], local_out[0], gate_logit, block_ids[0])
    first_in = exchange(first_out)
    second_in = exchange(second_out)
    own = pl.pallas_call(
        assemble,
        out_shape=jax.ShapeDtypeStruct((2, members * quarter, LANES), bf16),
        in_specs=[vmem],
        out_specs=vmem,
        compiler_params=small,
        name="assemble",
    )(first_in)
    if chunks > 1:
        same = [[mo * heads + mi for mo in range(chunks)] for mi in range(heads)]
        own = lax.all_gather(own, "mem", axis_index_groups=same, axis=1, tiled=True)
    mate = lax.ppermute(own, "mem", [(i, i ^ 1) for i in range(shards)])

    rows_all = 2 * own.shape[1]

    def attend_some(begin, count, q_at, final, tile, step_width, out_shape, *args):
        if chunks > 1:
            tile, step_width = 256, 512
        return pl.pallas_call(
            functools.partial(attend, begin, count, q_at, ext_at, per, step_width, tile, final),
            out_shape=out_shape,
            in_specs=[vmem] * len(args),
            out_specs=[vmem] * len(out_shape),
            scratch_shapes=[
                pltpu.VMEM((LANES * BLK, LANES), bf16),
                pltpu.VMEM((step_width, LANES), bf16),
                pltpu.VMEM((members * count, (1 + units) * LANES), bf16),
                pltpu.VMEM((members * count, 2 * LANES), bf16),
                pltpu.VMEM((rows_all // step_width, tile, step_width), jnp.float32),
                pltpu.VMEM((tile, LANES), jnp.float32),
                pltpu.VMEM((tile, LANES), jnp.float32),
                pltpu.VMEM((tile, LANES), jnp.float32),
            ],
            compiler_params=pltpu.CompilerParams(vmem_limit_bytes=(34 if chunks == 1 else 44) << 20),
            cost_estimate=pl.CostEstimate(
                flops=2 * members * count * rows_all * LANES * 5,
                bytes_accessed=4 * rows_all * LANES,
                transcendentals=members * count * rows_all,
            ),
            name="attend",
        )(*args)

    part, gate_sum = attend_some(
        0,
        early,
        2 * quarter,
        False,
        1024,
        512,
        [jax.ShapeDtypeStruct((members, early, LANES), bf16), jax.ShapeDtypeStruct((8, LANES), jnp.float32)],
        own,
        mate,
        first_in,
        first_in,
    )
    (grad,) = attend_some(
        early,
        late,
        0,
        True,
        512,
        2048,
        [jax.ShapeDtypeStruct((members, late, LANES), bf16)],
        own,
        mate,
        second_in,
        first_in,
    )
    home = (exchange(part), exchange(grad))
    d_query = pl.pallas_call(
        functools.partial(unpack, heads),
        out_shape=jax.ShapeDtypeStruct((tokens, width), bf16),
        in_specs=[vmem, vmem],
        out_specs=vmem,
        compiler_params=small,
        name="unpack",
    )(*home)
    gate_total = gate_sum[0, :heads]
    if head_groups is not None:
        gate_total = lax.psum(gate_total, AXES) / members
    sig = jax.nn.sigmoid(gate_logit)
    d_gate = sig * (1.0 - sig) * gate_total / (shards * groups * tokens * LANES) ** 0.5
    return (d_query[None], d_gate)


def solution(mesh):
    placed = (
        P("grp", "mem", None),
        P("grp", "mem", None),
        P("grp", "mem", None),
        P("grp", "mem", None),
        P("mem", None),
        P("mem", None),
        P(),
        P("grp", "mem", None),
    )
    return jax.shard_map(
        local, mesh=mesh, in_specs=placed, out_specs=(P("grp", "mem", None), P()), check_vma=False
    )
```

```python
import functools
import math

import jax
import jax.numpy as jnp
from jax import lax
from jax.experimental import pallas as pl
from jax.experimental.pallas import tpu as pltpu
from jax.sharding import PartitionSpec as P

BLK = 16
LANES = 128
AXES = ("mem", "grp")
FAR = -1e30


def head_and_half(position):
    return (position >> 2) * 2 + (position & 1), (position >> 1) & 1


def pack(
    heads,
    chunks,
    early,
    k_hbm,
    v_hbm,
    q_hbm,
    dout_hbm,
    omem_hbm,
    local_hbm,
    gate_ref,
    ids_ref,
    first_out,
    second_out,
    k_ref,
    v_ref,
    q_ref,
    dout_ref,
    omem_ref,
    local_ref,
    dmem_ref,
    halves_ref,
    delta_ref,
    gate_rows,
    sems,
):
    tokens = q_ref.shape[0]
    half_rows = tokens // 2
    half_shard = k_ref.shape[0]
    quarter = half_shard // 2
    qblocks, names = ids_ref.shape
    high = lax.Precision.HIGHEST
    parity = lax.axis_index("grp") % 2
    mine = pl.ds(pl.multiple_of(parity * half_shard, half_shard), half_shard)
    copies = []
    for at, (source, target) in enumerate(
        (
            (dout_hbm, dout_ref),
            (omem_hbm, omem_ref),
            (local_hbm, local_ref),
            (q_hbm, q_ref),
            (k_hbm.at[mine, :], k_ref),
            (v_hbm.at[mine, :], v_ref),
        )
    ):
        copy = pltpu.make_async_copy(source, target, sems.at[at])
        copy.start()
        copies.append(copy)

    lane = lax.broadcasted_iota(jnp.int32, (1, LANES), 1)
    ids = ids_ref[...]
    per = qblocks // 2
    bias_rows = 2 * chunks * per
    halves_ref[...] = jnp.zeros_like(halves_ref)
    for chunk in range(chunks):
        block = 16 * (chunk * heads + lane // 8) + 8 * ((lane // 4) % 2) + lane % 4
        for side in range(2):
            wanted = jnp.broadcast_to(block + 4 * side, (qblocks, LANES))
            hit = jnp.zeros((qblocks, LANES), jnp.float32)
            for name in range(names):
                hit = jnp.where(ids[:, name : name + 1] == wanted, 1.0, hit)
            table = jnp.where(hit > 0.5, 0.0, FAR)
            for half in range(2):
                at = ((half ^ side) * chunks + chunk) * per
                halves_ref[half, at : at + per, :] = table[half * per : (half + 1) * per]

    ones = jnp.ones((8, LANES), jnp.float32)
    wide_ones = jnp.ones((16, 2 * LANES), jnp.bfloat16)
    gate_rows[...] = jnp.zeros_like(gate_rows)
    for copy in copies[:3]:
        copy.wait()
    for head in range(heads):
        cols = slice(head * LANES, (head + 1) * LANES)
        sig = jax.nn.sigmoid(jnp.full((8, LANES), gate_ref[head], jnp.float32))[:1]
        d_out = dout_ref[:, cols].astype(jnp.float32)
        o_mem = omem_ref[:, cols].astype(jnp.float32)
        d_mem = (d_out * sig).astype(jnp.bfloat16)
        dmem_ref[:, cols] = d_mem
        differ = o_mem - local_ref[:, cols].astype(jnp.float32)
        gate_rows[head : head + 1, :] = jnp.sum(d_out * differ, 0, keepdims=True)
        product = d_mem.astype(jnp.float32) * o_mem
        upper = product.astype(jnp.bfloat16)
        lower = (product - upper.astype(jnp.float32)).astype(jnp.bfloat16)
        row = lax.dot_general(
            wide_ones,
            jnp.concatenate([upper, lower], axis=1),
            (((1,), (1,)), ((), ())),
            preferred_element_type=jnp.float32,
        )
        delta_ref[head : head + 1, :] = row[:1]
    total = lax.dot_general(
        ones, gate_rows[...], (((1,), (1,)), ((), ())), precision=high, preferred_element_type=jnp.float32
    )[:1]
    first = total.astype(jnp.bfloat16).astype(jnp.float32)
    second = (total - first).astype(jnp.bfloat16).astype(jnp.float32)
    third = total - first - second
    for half in range(2):
        halves_ref[half, bias_rows + 1 : bias_rows + 2, :] = first
        halves_ref[half, bias_rows + 2 : bias_rows + 3, :] = second
        halves_ref[half, bias_rows + 3 : bias_rows + 4, :] = third
    turn = (lax.axis_index("mem") % 2) * 2 + parity
    quarter_lanes = LANES // 4
    in_turn = lax.broadcasted_iota(jnp.int32, (heads, LANES), 1) // quarter_lanes == turn
    deltas = {}
    for half in range(2):
        for part in range(2):
            shift = lax.rem(quarter_lanes * (turn + 8 - 2 * half - part), LANES)
            deltas[half, part] = jnp.where(in_turn, pltpu.roll(delta_ref[...], shift, 1), 0.0)
    for copy in copies[3:]:
        copy.wait()
    for position in range(2 * heads):
        head, half = head_and_half(position)
        cols = slice(head * LANES, (head + 1) * LANES)
        base = half * half_rows
        at = 2 * quarter
        first_out[position, :quarter, :] = k_ref[half * quarter : (half + 1) * quarter, cols]
        first_out[position, quarter:at, :] = v_ref[half * quarter : (half + 1) * quarter, cols]
        first_out[position, at : at + early, :] = q_ref[base : base + early, cols]
        first_out[position, at + early : at + 2 * early, :] = dmem_ref[base : base + early, cols]
        late = half_rows - early
        second_out[position, :late, :] = q_ref[base + early : base + half_rows, cols]
        second_out[position, late:, :] = dmem_ref[base + early : base + half_rows, cols]
        halves_ref[half, bias_rows : bias_rows + 1, :] = deltas[half, 0][head : head + 1]
        halves_ref[half, bias_rows + 4 : bias_rows + 5, :] = deltas[half, 1][head : head + 1]
        first_out[position, at + 2 * early :, :] = halves_ref[half].astype(jnp.bfloat16)


def assemble(in_ref, out_ref):
    quarter = out_ref.shape[1] // in_ref.shape[0]
    for source in range(in_ref.shape[0]):
        rows = slice(source * quarter, (source + 1) * quarter)
        out_ref[0, rows, :] = in_ref[source, :quarter, :]
        out_ref[1, rows, :] = in_ref[source, quarter : 2 * quarter, :]


def attend(
    begin, count, q_at, ext_at, per, tile, width, final, own_ref, mate_ref, q_ref, ext_ref, *refs
):
    if final:
        kt, before_ref, out_ref, mark, qx, dm, delta, scores, acc = refs
    else:
        out_ref, gate_ref, kt, mark, qx, dm, delta, scores, acc = refs
    sources = q_ref.shape[0]
    units = qx.shape[1] // LANES - 1
    sides = (own_ref, mate_ref)
    rows_side = own_ref.shape[1]
    rows_unit = mark.shape[0]
    scale = 1.0 / math.sqrt(LANES)
    exponent = scale * math.log2(math.e)
    bias_rows = units * per
    together = LANES // count

    lane = lax.broadcasted_iota(jnp.int32, (BLK, LANES), 1)
    for block in range(LANES):
        mark[block * BLK : (block + 1) * BLK, :] = jnp.where(lane == block, 1.0, 0.0).astype(jnp.bfloat16)
    if not final:
        for side, ref in enumerate(sides):
            for at in range(0, rows_side, LANES):
                turned = ref[0, at : at + LANES, :].astype(jnp.float32).T
                kt[side, :, at : at + LANES] = turned.astype(jnp.bfloat16)

    gate_sum = jnp.zeros((1, LANES), jnp.float32)
    for source in range(sources):
        base = source * count
        qx[base : base + count, :LANES] = q_ref[source, q_at : q_at + count, :]
        dm[base : base + count, :] = q_ref[source, q_at + count : q_at + 2 * count, :]
        extra = ext_ref[source, ext_at:, :].astype(jnp.float32)
        for unit in range(units):
            for block in range(count // BLK):
                at = unit * per + begin // BLK + block
                row = jnp.broadcast_to(extra[at : at + 1], (BLK, LANES)).astype(jnp.bfloat16)
                qx[base + block * BLK : base + (block + 1) * BLK, (1 + unit) * LANES : (2 + unit) * LANES] = row
        if not final:
            for part in range(1, 4):
                gate_sum = gate_sum + extra[bias_rows + part : bias_rows + part + 1]
        at = bias_rows + (4 if final else 0)
        row = extra[at : at + 1]
        delta_row = row if source % together == 0 else delta_row + row
        if source % together == together - 1:
            end = base + count
            delta[:, end - LANES : end] = jnp.broadcast_to(delta_row, (8, LANES))
    if not final:
        gate_ref[...] = jnp.broadcast_to(gate_sum, gate_ref.shape)

    for start in range(0, sources * count, tile):
        here = slice(start, start + tile)
        best = jnp.full((8, tile), -3e38, jnp.float32)
        for side, ref in enumerate(sides):
            for unit in range(units // 2):
                lanes = (1 + side * (units // 2) + unit) * LANES

                def score(at, best, side=side, ref=ref, unit=unit, lanes=lanes):
                    at = pl.multiple_of(at * width, width)
                    rows = pl.ds(unit * rows_unit + at, width)
                    left = jnp.concatenate([ref[0, rows, :], mark[pl.ds(at, width), :]], axis=1)
                    right = jnp.concatenate([qx[here, :LANES], qx[here, lanes : lanes + LANES]], axis=1)
                    got = lax.dot_general(
                        left, right, (((1,), (1,)), ((), ())), preferred_element_type=jnp.float32
                    )
                    scores[pl.ds(side * rows_side + unit * rows_unit + at, width), :] = got
                    return jnp.maximum(best, jnp.max(got.reshape(width // 8, 8, tile), axis=0))

                best = lax.fori_loop(0, rows_unit // width, score, best, unroll=2)
        level = jnp.max(best, 0, keepdims=True) * exponent
        less = delta[:1, here]
        total = jnp.zeros((8, tile), jnp.float32)
        acc[...] = jnp.zeros_like(acc)
        for side, ref in enumerate(sides):

            def back(at, total, side=side, ref=ref):
                at = pl.multiple_of(at * width, width)
                rows = pl.ds(at, width)
                prod = lax.dot_general(
                    ref[1, rows, :], dm[here, :], (((1,), (1,)), ((), ())), preferred_element_type=jnp.float32
                )
                expo = jnp.exp2(scores[pl.ds(side * rows_side + at, width), :] * exponent - level)
                ds = (expo * (prod - less)).astype(jnp.bfloat16)
                acc[...] += jnp.dot(kt[side, :, rows], ds, preferred_element_type=jnp.float32)
                return total + jnp.sum(expo.reshape(width // 8, 8, tile), axis=0)

            total = lax.fori_loop(0, rows_side // width, back, total, unroll=2)
        weight = scale / jnp.sum(total, 0, keepdims=True)
        for at in range(0, tile, LANES):
            turned = (acc[:, at : at + LANES] * weight[:, at : at + LANES]).T.astype(jnp.bfloat16)
            for inner in range(together):
                source = (start + at) // count + inner
                got = turned[inner * count : (inner + 1) * count]
                if final:
                    out_ref[source, :begin, :] = before_ref[source]
                    out_ref[source, begin:, :] = got
                else:
                    out_ref[source] = got


def unpack(heads, in_ref, out_ref):
    half_rows = in_ref.shape[1]
    for position in range(2 * heads):
        head, half = head_and_half(position)
        out_ref[half * half_rows : (half + 1) * half_rows, head * LANES : (head + 1) * LANES] = in_ref[position]


def local(queries, d_out, o_mem, local_out, mem_keys, mem_values, gate_logit, block_ids):
    shards = lax.axis_size("mem")
    groups = lax.axis_size("grp")
    tokens = queries.shape[1]
    width = queries.shape[2]
    heads = gate_logit.shape[0]
    rows_dev = mem_keys.shape[0]
    qblocks = tokens // BLK
    members = 2 * heads
    chunks = shards // heads
    assert width == heads * LANES and shards % heads == 0 and groups % 2 == 0
    assert rows_dev == 16 * BLK and heads * 8 == LANES and tokens == LANES
    quarter = rows_dev // 4
    halves = tokens // 2
    per = qblocks // 2
    units = 2 * chunks
    early = halves // 2
    late = halves - early
    extra = -(-(units * per + 5) // 16) * 16
    ext_at = 2 * quarter + 2 * early
    packet = ext_at + extra
    vmem = pl.BlockSpec(memory_space=pltpu.VMEM)
    smem = pl.BlockSpec(memory_space=pltpu.SMEM)
    hbm = pl.BlockSpec(memory_space=pltpu.HBM)
    bf16 = jnp.bfloat16
    small = pltpu.CompilerParams(vmem_limit_bytes=24 << 20)

    if shards * groups == members:
        head_groups = None
    else:
        head_groups = [
            [(mo * heads + mi) * groups + 2 * go + gp for mi in range(heads) for gp in range(2)]
            for mo in range(chunks)
            for go in range(groups // 2)
        ]
    exchange = functools.partial(
        lax.all_to_all, axis_name=AXES, split_axis=0, concat_axis=0, tiled=True, axis_index_groups=head_groups
    )

    first_out, second_out = pl.pallas_call(
        functools.partial(pack, heads, chunks, early),
        out_shape=(
            jax.ShapeDtypeStruct((members, packet, LANES), bf16),
            jax.ShapeDtypeStruct((members, 2 * late, LANES), bf16),
        ),
        in_specs=[hbm] * 6 + [smem, vmem],
        out_specs=(vmem, vmem),
        scratch_shapes=[pltpu.VMEM((rows_dev // 2, width), bf16)] * 2
        + [pltpu.VMEM((tokens, width), bf16)] * 5
        + [
            pltpu.VMEM((2, extra, LANES), jnp.float32),
            pltpu.VMEM((heads, LANES), jnp.float32),
            pltpu.VMEM((LANES, LANES), jnp.float32),
            pltpu.SemaphoreType.DMA((6,)),
        ],
        compiler_params=pltpu.CompilerParams(vmem_limit_bytes=56 << 20),
        name="pack",
    )(mem_keys, mem_values, queries[0], d_out[0], o_mem[0], local_out[0], gate_logit, block_ids[0])
    first_in = exchange(first_out)
    second_in = exchange(second_out)
    own = pl.pallas_call(
        assemble,
        out_shape=jax.ShapeDtypeStruct((2, members * quarter, LANES), bf16),
        in_specs=[vmem],
        out_specs=vmem,
        compiler_params=small,
        name="assemble",
    )(first_in)
    if chunks > 1:
        same = [[mo * heads + mi for mo in range(chunks)] for mi in range(heads)]
        own = lax.all_gather(own, "mem", axis_index_groups=same, axis=1, tiled=True)
    mate = lax.ppermute(own, "mem", [(i, i ^ 1) for i in range(shards)])

    rows_all = 2 * own.shape[1]
    step_width = 512
    tile = 512 if chunks == 1 else 256

    def attend_some(begin, count, q_at, final, out_shape, *args):
        return pl.pallas_call(
            functools.partial(attend, begin, count, q_at, ext_at, per, tile, step_width, final),
            out_shape=out_shape,
            in_specs=[vmem] * len(args),
            out_specs=[vmem] * len(out_shape),
            scratch_shapes=[
                pltpu.VMEM((LANES * BLK, LANES), bf16),
                pltpu.VMEM((members * count, (1 + units) * LANES), bf16),
                pltpu.VMEM((members * count, LANES), bf16),
                pltpu.VMEM((8, members * count), jnp.float32),
                pltpu.VMEM((rows_all, tile), jnp.float32),
                pltpu.VMEM((LANES, tile), jnp.float32),
            ],
            compiler_params=pltpu.CompilerParams(vmem_limit_bytes=(24 if chunks == 1 else 44) << 20),
            cost_estimate=pl.CostEstimate(
                flops=2 * members * count * rows_all * LANES * 4,
                bytes_accessed=4 * rows_all * LANES,
                transcendentals=members * count * rows_all,
            ),
            name="attend",
        )(*args)

    assert early == late and 4 * early == 2 * halves == LANES
    part, gate_sum, keys_turned = attend_some(
        0,
        early,
        2 * quarter,
        False,
        [
            jax.ShapeDtypeStruct((members, early, LANES), bf16),
            jax.ShapeDtypeStruct((8, LANES), jnp.float32),
            jax.ShapeDtypeStruct((2, LANES, rows_all // 2), bf16),
        ],
        own,
        mate,
        first_in,
        first_in,
    )
    (grad,) = attend_some(
        early,
        late,
        0,
        True,
        [jax.ShapeDtypeStruct((members, halves, LANES), bf16)],
        own,
        mate,
        second_in,
        first_in,
        keys_turned,
        part,
    )
    home = exchange(grad)
    d_query = pl.pallas_call(
        functools.partial(unpack, heads),
        out_shape=jax.ShapeDtypeStruct((tokens, width), bf16),
        in_specs=[vmem],
        out_specs=vmem,
        compiler_params=small,
        name="unpack",
    )(home)
    gate_total = gate_sum[0, :heads]
    if head_groups is not None:
        gate_total = lax.psum(gate_total, AXES) / members
    sig = jax.nn.sigmoid(gate_logit)
    d_gate = sig * (1.0 - sig) * gate_total / (shards * groups * tokens * LANES) ** 0.5
    return (d_query[None], d_gate)


def solution(mesh):
    placed = (
        P("grp", "mem", None),
        P("grp", "mem", None),
        P("grp", "mem", None),
        P("grp", "mem", None),
        P("mem", None),
        P("mem", None),
        P(),
        P("grp", "mem", None),
    )
    return jax.shard_map(
        local, mesh=mesh, in_specs=placed, out_specs=(P("grp", "mem", None), P()), check_vma=False
    )
```

```python
import functools
import math

import jax
import jax.numpy as jnp
from jax import lax
from jax.experimental import pallas as pl
from jax.experimental.pallas import tpu as pltpu
from jax.sharding import PartitionSpec as P

BLK = 16
LANES = 128
AXES = ("mem", "grp")
FAR = -1e30


def pack(
    heads,
    chunks,
    early,
    k_hbm,
    v_hbm,
    q_hbm,
    dout_hbm,
    omem_hbm,
    local_hbm,
    gate_ref,
    ids_ref,
    first_hbm,
    second_hbm,
    k_ref,
    v_ref,
    q_ref,
    dout_ref,
    omem_ref,
    local_ref,
    dmem_ref,
    ext_ref,
    late_ref,
    delta_ref,
    gate_rows,
    first_out,
    second_out,
    sems,
    out_sems,
):
    tokens = q_ref.shape[0]
    half_shard = k_ref.shape[0]
    qblocks, names = ids_ref.shape
    high = lax.Precision.HIGHEST
    core = lax.axis_index("mem") % 2
    parity = lax.axis_index("grp") % 2
    mine = pl.ds(pl.multiple_of(parity * half_shard, half_shard), half_shard)
    copies = []
    for at, (source, target) in enumerate(
        (
            (dout_hbm, dout_ref),
            (omem_hbm, omem_ref),
            (local_hbm, local_ref),
            (q_hbm, q_ref),
            (k_hbm.at[mine, :], k_ref),
            (v_hbm.at[mine, :], v_ref),
        )
    ):
        copy = pltpu.make_async_copy(source, target, sems.at[at])
        copy.start()
        copies.append(copy)

    lane = lax.broadcasted_iota(jnp.int32, (1, LANES), 1)
    ids = ids_ref[...]
    per = qblocks // 2
    bias_rows = 2 * chunks * per
    ext_ref[...] = jnp.zeros_like(ext_ref)
    late_ref[...] = jnp.zeros_like(late_ref)
    for side in range(2):
        for chunk in range(chunks):
            shard = chunk * heads + 2 * (lane // 16) + (core + side) % 2
            wanted = jnp.broadcast_to(16 * shard + lane % 16, (qblocks, LANES))
            hit = jnp.zeros((qblocks, LANES), jnp.float32)
            for name in range(names):
                hit = jnp.where(ids[:, name : name + 1] == wanted, 1.0, hit)
            table = jnp.where(hit > 0.5, 0.0, FAR)
            at = (side * chunks + chunk) * per
            ext_ref[at : at + per, :] = table[:per]
            late_ref[at : at + per, :] = table[per:]

    ones = jnp.ones((8, LANES), jnp.float32)
    wide_ones = jnp.ones((16, 2 * LANES), jnp.bfloat16)
    gate_rows[...] = jnp.zeros_like(gate_rows)
    for copy in copies[:3]:
        copy.wait()
    for head in range(heads):
        cols = slice(head * LANES, (head + 1) * LANES)
        sig = jax.nn.sigmoid(jnp.full((8, LANES), gate_ref[head], jnp.float32))[:1]
        d_out = dout_ref[:, cols].astype(jnp.float32)
        o_mem = omem_ref[:, cols].astype(jnp.float32)
        d_mem = (d_out * sig).astype(jnp.bfloat16)
        dmem_ref[:, cols] = d_mem
        differ = o_mem - local_ref[:, cols].astype(jnp.float32)
        gate_rows[head : head + 1, :] = jnp.sum(d_out * differ, 0, keepdims=True)
        product = d_mem.astype(jnp.float32) * o_mem
        upper = product.astype(jnp.bfloat16)
        lower = (product - upper.astype(jnp.float32)).astype(jnp.bfloat16)
        row = lax.dot_general(
            wide_ones,
            jnp.concatenate([upper, lower], axis=1),
            (((1,), (1,)), ((), ())),
            preferred_element_type=jnp.float32,
        )
        delta_ref[head : head + 1, :] = row[:1]
    total = lax.dot_general(
        ones, gate_rows[...], (((1,), (1,)), ((), ())), precision=high, preferred_element_type=jnp.float32
    )
    first = total.astype(jnp.bfloat16).astype(jnp.float32)
    second = (total - first).astype(jnp.bfloat16).astype(jnp.float32)
    third = total - first - second
    addends = first + pltpu.roll(second, heads, 1) + pltpu.roll(third, 2 * heads, 1)
    ext_ref[bias_rows + 1 : bias_rows + 2, :] = addends[:1]
    late_extra = late_ref[...].astype(jnp.bfloat16)
    for copy in copies[3:]:
        copy.wait()
    at = 2 * half_shard
    late = tokens - early
    sent = []
    bunch = heads // 4
    for head in range(heads):
        cols = slice(head * LANES, (head + 1) * LANES)
        first_out[head, :half_shard, :] = k_ref[:, cols]
        first_out[head, half_shard:at, :] = v_ref[:, cols]
        first_out[head, at : at + early, :] = q_ref[:early, cols]
        first_out[head, at + early : at + 2 * early, :] = dmem_ref[:early, cols]
        ext_ref[bias_rows : bias_rows + 1, :] = delta_ref[head : head + 1, :]
        first_out[head, at + 2 * early :, :] = ext_ref[...].astype(jnp.bfloat16)
        second_out[head, :late, :] = q_ref[early:, cols]
        second_out[head, late : 2 * late, :] = dmem_ref[early:, cols]
        second_out[head, 2 * late :, :] = late_extra
        if head % bunch == bunch - 1:
            some = slice(head + 1 - bunch, head + 1)
            for index, (source, target) in enumerate(((first_out, first_hbm), (second_out, second_hbm))):
                copy = pltpu.make_async_copy(
                    source.at[some], target.at[some], out_sems.at[index, head // bunch]
                )
                copy.start()
                sent.append(copy)
    for copy in sent:
        copy.wait()


def assemble(in_ref, out_ref):
    part = out_ref.shape[1] // in_ref.shape[0]
    for source in range(in_ref.shape[0]):
        rows = slice(source * part, (source + 1) * part)
        out_ref[0, rows, :] = in_ref[source, :part, :]
        out_ref[1, rows, :] = in_ref[source, part : 2 * part, :]


def attend(begin, count, q_at, ext_at, per, width, tile, final, own_ref, mate_ref, q_ref, ext_ref, *refs):
    if final:
        before_ref, out_ref, mark, minus, qx, dx, scores, high, total, acc, stage, sems = refs
        early_copy = pltpu.make_async_copy(before_ref, out_ref.at[:, :begin, :], sems.at[0])
        early_copy.start()
    else:
        out_ref, gate_ref, mark, minus, qx, dx, scores, high, total, acc = refs
    sources = q_ref.shape[0]
    units = qx.shape[1] // LANES - 1
    sides = (own_ref, mate_ref)
    steps_side = own_ref.shape[1] // width
    rows_unit = mark.shape[0]
    scale = 1.0 / math.sqrt(LANES)
    exponent = scale * math.log2(math.e)
    bias_rows = units * per

    lane = lax.broadcasted_iota(jnp.int32, (BLK, LANES), 1)
    for block in range(LANES):
        mark[block * BLK : (block + 1) * BLK, :] = jnp.where(lane == block, 1.0, 0.0).astype(jnp.bfloat16)
    wide_lane = lax.broadcasted_iota(jnp.int32, (LANES, LANES), 1)
    for block in range(width // LANES):
        minus[block * LANES : (block + 1) * LANES, :] = jnp.where(wide_lane == 0, -1.0, 0.0).astype(jnp.bfloat16)

    gate_sum = jnp.zeros((1, LANES), jnp.float32)
    for source in range(sources):
        base = source * count
        qx[base : base + count, :LANES] = q_ref[source, q_at : q_at + count, :]
        dx[base : base + count, :LANES] = q_ref[source, q_at + count : q_at + 2 * count, :]
        bias = q_ref[source, q_at + 2 * count :, :].astype(jnp.float32)
        for unit in range(units):
            for block in range(count // BLK):
                at = unit * per + block
                row = jnp.broadcast_to(bias[at : at + 1], (BLK, LANES)).astype(jnp.bfloat16)
                qx[base + block * BLK : base + (block + 1) * BLK, (1 + unit) * LANES : (2 + unit) * LANES] = row
        extra = ext_ref[source, ext_at:, :].astype(jnp.float32)
        if not final:
            gate_sum = gate_sum + extra[bias_rows + 1 : bias_rows + 2]
        wide = jnp.broadcast_to(extra[bias_rows : bias_rows + 1], (LANES, LANES)).T
        wide = jnp.where(wide_lane == 0, wide, 0.0).astype(jnp.bfloat16)
        dx[base : base + count, LANES:] = wide[begin : begin + count]
    if not final:
        gate_ref[...] = jnp.broadcast_to(gate_sum, gate_ref.shape)

    def one_tile(index, carry):
        here = pl.ds(pl.multiple_of(index * tile, tile), tile)
        high[...] = jnp.full_like(high, -3e38)
        for side, ref in enumerate(sides):
            for unit in range(units // 2):

                def score(at, carry, side=side, ref=ref, unit=unit):
                    rows = pl.ds(pl.multiple_of(unit * rows_unit + at * width, width), width)
                    marks = pl.ds(pl.multiple_of(at * width, width), width)
                    lanes = (1 + side * (units // 2) + unit) * LANES
                    left = jnp.concatenate([qx[here, :LANES], qx[here, lanes : lanes + LANES]], axis=1)
                    right = jnp.concatenate([ref[0, rows, :], mark[marks, :]], axis=1)
                    got = lax.dot_general(
                        left, right, (((1,), (1,)), ((), ())), preferred_element_type=jnp.float32
                    )
                    scores[side * steps_side + unit * (rows_unit // width) + at] = got
                    best = high[...]
                    for column in range(width // LANES):
                        best = jnp.maximum(best, got[:, column * LANES : (column + 1) * LANES])
                    high[...] = best
                    return carry

                lax.fori_loop(0, rows_unit // width, score, 0, unroll=True)
        high[...] = jnp.broadcast_to(jnp.max(high[...], 1, keepdims=True) * exponent, high.shape)
        total[...] = jnp.zeros_like(total)
        acc[...] = jnp.zeros_like(acc)
        for side, ref in enumerate(sides):

            def back(at, carry, side=side, ref=ref):
                rows = pl.ds(pl.multiple_of(at * width, width), width)
                prod = lax.dot_general(
                    dx[here, :],
                    jnp.concatenate([ref[1, rows, :], minus[...]], axis=1),
                    (((1,), (1,)), ((), ())),
                    preferred_element_type=jnp.float32,
                )
                got = scores[side * steps_side + at]
                level = high[...]
                added = total[...]
                pieces = []
                for column in range(width // LANES):
                    cols = slice(column * LANES, (column + 1) * LANES)
                    expo = jnp.exp2(got[:, cols] * exponent - level)
                    added = added + expo
                    pieces.append((expo * prod[:, cols]).astype(jnp.bfloat16))
                total[...] = added
                acc[...] += jnp.dot(
                    jnp.concatenate(pieces, axis=1), ref[0, rows, :], preferred_element_type=jnp.float32
                )
                return carry

            lax.fori_loop(0, steps_side, back, 0, unroll=4)
        weight = scale / jnp.sum(total[...], 1, keepdims=True)
        qx[here, :LANES] = (acc[...] * weight).astype(jnp.bfloat16)
        return carry

    lax.fori_loop(0, qx.shape[0] // tile, one_tile, 0)
    for source in range(sources):
        (stage if final else out_ref)[source] = qx[source * count : (source + 1) * count, :LANES]
    if final:
        late_copy = pltpu.make_async_copy(stage, out_ref.at[:, begin:, :], sems.at[1])
        late_copy.start()
        early_copy.wait()
        late_copy.wait()


def unpack(in_ref, out_ref):
    for head in range(in_ref.shape[0]):
        out_ref[:, head * LANES : (head + 1) * LANES] = in_ref[head]


def local(queries, d_out, o_mem, local_out, mem_keys, mem_values, gate_logit, block_ids):
    shards = lax.axis_size("mem")
    groups = lax.axis_size("grp")
    tokens = queries.shape[1]
    width = queries.shape[2]
    heads = gate_logit.shape[0]
    rows_dev = mem_keys.shape[0]
    qblocks = tokens // BLK
    members = heads
    chunks = shards // heads
    assert width == heads * LANES and shards % heads == 0 and groups % 2 == 0
    assert rows_dev == 16 * BLK and heads * 8 == LANES and tokens == LANES
    half_shard = rows_dev // 2
    per = qblocks // 2
    units = 2 * chunks
    early = tokens // 2
    late = tokens - early
    extra = -(-(units * per + 2) // 16) * 16
    late_extra = -(-units * per // 16) * 16
    ext_at = 2 * half_shard + 2 * early
    vmem = pl.BlockSpec(memory_space=pltpu.VMEM)
    smem = pl.BlockSpec(memory_space=pltpu.SMEM)
    hbm = pl.BlockSpec(memory_space=pltpu.HBM)
    bf16 = jnp.bfloat16
    small = pltpu.CompilerParams(vmem_limit_bytes=24 << 20)

    core_groups = [
        [(mo * heads + 2 * chip + core) * groups + 2 * go + gp for chip in range(heads // 2) for gp in range(2)]
        for mo in range(chunks)
        for go in range(groups // 2)
        for core in range(2)
    ]
    exchange = functools.partial(
        lax.all_to_all, axis_name=AXES, split_axis=0, concat_axis=0, tiled=True, axis_index_groups=core_groups
    )

    first_shape = (members, ext_at + extra, LANES)
    second_shape = (members, 2 * late + late_extra, LANES)
    first_out, second_out = pl.pallas_call(
        functools.partial(pack, heads, chunks, early),
        out_shape=(pltpu.HBM(first_shape, bf16), pltpu.HBM(second_shape, bf16)),
        in_specs=[hbm] * 6 + [smem, vmem],
        out_specs=(hbm, hbm),
        scratch_shapes=[pltpu.VMEM((half_shard, width), bf16)] * 2
        + [pltpu.VMEM((tokens, width), bf16)] * 5
        + [
            pltpu.VMEM((extra, LANES), jnp.float32),
            pltpu.VMEM((late_extra, LANES), jnp.float32),
            pltpu.VMEM((heads, LANES), jnp.float32),
            pltpu.VMEM((LANES, LANES), jnp.float32),
            pltpu.VMEM(first_shape, bf16),
            pltpu.VMEM(second_shape, bf16),
            pltpu.SemaphoreType.DMA((6,)),
            pltpu.SemaphoreType.DMA((2, 4)),
        ],
        compiler_params=pltpu.CompilerParams(vmem_limit_bytes=56 << 20),
        name="pack",
    )(mem_keys, mem_values, queries[0], d_out[0], o_mem[0], local_out[0], gate_logit, block_ids[0])
    first_in = exchange(first_out)
    second_in = exchange(second_out)
    own = pl.pallas_call(
        assemble,
        out_shape=jax.ShapeDtypeStruct((2, members * half_shard, LANES), bf16),
        in_specs=[vmem],
        out_specs=vmem,
        compiler_params=small,
        name="assemble",
    )(first_in)
    if chunks > 1:
        same = [[mo * heads + mi for mo in range(chunks)] for mi in range(heads)]
        own = lax.all_gather(own, "mem", axis_index_groups=same, axis=1, tiled=True)
    mate = lax.ppermute(own, "mem", [(i, i ^ 1) for i in range(shards)])

    rows_all = 2 * own.shape[1]
    step_width = 512
    tile = 1024 if chunks == 1 else 256

    def attend_some(begin, count, q_at, final, out_shape, out_specs, *args):
        return pl.pallas_call(
            functools.partial(attend, begin, count, q_at, ext_at, per, step_width, tile, final),
            out_shape=out_shape,
            in_specs=[vmem] * len(args),
            out_specs=out_specs,
            scratch_shapes=[
                pltpu.VMEM((LANES * BLK, LANES), bf16),
                pltpu.VMEM((step_width, LANES), bf16),
                pltpu.VMEM((members * count, (1 + units) * LANES), bf16),
                pltpu.VMEM((members * count, 2 * LANES), bf16),
                pltpu.VMEM((rows_all // step_width, tile, step_width), jnp.float32),
                pltpu.VMEM((tile, LANES), jnp.float32),
                pltpu.VMEM((tile, LANES), jnp.float32),
                pltpu.VMEM((tile, LANES), jnp.float32),
            ]
            + [pltpu.VMEM((members, count, LANES), bf16), pltpu.SemaphoreType.DMA((2,))] * final,
            compiler_params=pltpu.CompilerParams(vmem_limit_bytes=(34 if chunks == 1 else 44) << 20),
            cost_estimate=pl.CostEstimate(
                flops=2 * members * count * rows_all * LANES * 5,
                bytes_accessed=4 * rows_all * LANES,
                transcendentals=members * count * rows_all,
            ),
            name="attend",
        )(*args)

    part, gate_sum = attend_some(
        0,
        early,
        2 * half_shard,
        False,
        [jax.ShapeDtypeStruct((members, early, LANES), bf16), jax.ShapeDtypeStruct((8, LANES), jnp.float32)],
        [vmem, vmem],
        own,
        mate,
        first_in,
        first_in,
    )
    gate_mate = lax.ppermute(gate_sum, "mem", [(i, i ^ 1) for i in range(shards)])
    grad = attend_some(
        early,
        late,
        0,
        True,
        pltpu.HBM((members, tokens, LANES), bf16),
        hbm,
        own,
        mate,
        second_in,
        first_in,
        part,
    )
    home = exchange(grad)
    d_query = pl.pallas_call(
        unpack,
        out_shape=jax.ShapeDtypeStruct((tokens, width), bf16),
        in_specs=[vmem],
        out_specs=vmem,
        compiler_params=small,
        name="unpack",
    )(home)
    addends = (gate_sum + gate_mate)[0, : 3 * heads]
    gate_total = addends[:heads] + addends[heads : 2 * heads] + addends[2 * heads :]
    if chunks > 1 or groups > 2:
        gate_total = lax.psum(gate_total, AXES) / (2 * members)
    sig = jax.nn.sigmoid(gate_logit)
    d_gate = sig * (1.0 - sig) * gate_total / (shards * groups * tokens * LANES) ** 0.5
    return (d_query[None], d_gate)


def solution(mesh):
    placed = (
        P("grp", "mem", None),
        P("grp", "mem", None),
        P("grp", "mem", None),
        P("grp", "mem", None),
        P("mem", None),
        P("mem", None),
        P(),
        P("grp", "mem", None),
    )
    return jax.shard_map(
        local, mesh=mesh, in_specs=placed, out_specs=(P("grp", "mem", None), P()), check_vma=False
    )
```

```python
import functools
import math

import jax
import jax.numpy as jnp
from jax import lax
from jax.experimental import pallas as pl
from jax.experimental.pallas import tpu as pltpu
from jax.sharding import PartitionSpec as P

BLK = 16
LANES = 128
AXES = ("mem", "grp")
FAR = -1e30


def pack(
    heads,
    chunks,
    early,
    k_hbm,
    v_hbm,
    q_hbm,
    dout_hbm,
    omem_hbm,
    local_hbm,
    gate_ref,
    ids_ref,
    first_hbm,
    second_hbm,
    k_ref,
    v_ref,
    q_ref,
    dout_ref,
    omem_ref,
    local_ref,
    ext_ref,
    delta_ref,
    gate_rows,
    first_out,
    second_out,
    sems,
    out_sems,
):
    tokens = q_ref.shape[0]
    half_shard = k_ref.shape[0]
    qblocks, names = ids_ref.shape
    core = lax.axis_index("mem") % 2
    parity = lax.axis_index("grp") % 2
    mine = pl.ds(pl.multiple_of(parity * half_shard, half_shard), half_shard)
    bunches = sems.shape[0]
    bunch = heads // bunches
    copies = []
    for index in range(bunches):
        cols = slice(index * bunch * LANES, (index + 1) * bunch * LANES)
        copies.append([])
        for at, (source, target) in enumerate(
            (
                (dout_hbm.at[:, cols], dout_ref),
                (omem_hbm.at[:, cols], omem_ref),
                (local_hbm.at[:, cols], local_ref),
                (q_hbm.at[:, cols], q_ref),
                (k_hbm.at[mine, cols], k_ref),
                (v_hbm.at[mine, cols], v_ref),
            )
        ):
            copy = pltpu.make_async_copy(source, target.at[:, cols], sems.at[index, at])
            copy.start()
            copies[index].append(copy)

    lane = lax.broadcasted_iota(jnp.int32, (1, LANES), 1)
    ids = ids_ref[...]
    bias_rows = chunks * qblocks
    ext_ref[...] = jnp.zeros_like(ext_ref)
    for chunk in range(chunks):
        hits = []
        for side in range(2):
            shard = chunk * heads + 2 * (lane // 16) + (core + side) % 2
            wanted = jnp.broadcast_to(16 * shard + lane % 16, (qblocks, LANES))
            hit = jnp.zeros((qblocks, LANES), jnp.float32)
            for name in range(names):
                hit = jnp.where(ids[:, name : name + 1] == wanted, 1.0, hit)
            hits.append(hit)
        ext_ref[chunk * qblocks : (chunk + 1) * qblocks, :] = hits[0] + 2.0 * hits[1]

    ones = jnp.ones((8, LANES), jnp.float32)
    wide_ones = jnp.ones((16, 2 * LANES), jnp.bfloat16)
    gate_rows[...] = jnp.zeros_like(gate_rows)
    at = 2 * half_shard
    late = tokens - early
    sent = []
    for head in range(heads):
        if head % bunch == 0:
            for copy in copies[head // bunch]:
                copy.wait()
        cols = slice(head * LANES, (head + 1) * LANES)
        sig = jax.nn.sigmoid(jnp.full((8, LANES), gate_ref[head], jnp.float32))[:1]
        d_out = dout_ref[:, cols].astype(jnp.float32)
        o_mem = omem_ref[:, cols].astype(jnp.float32)
        d_mem = (d_out * sig).astype(jnp.bfloat16)
        differ = o_mem - local_ref[:, cols].astype(jnp.float32)
        gate_rows[head : head + 1, :] = jnp.sum(d_out * differ, 0, keepdims=True)
        product = d_mem.astype(jnp.float32) * o_mem
        upper = product.astype(jnp.bfloat16)
        lower = (product - upper.astype(jnp.float32)).astype(jnp.bfloat16)
        row = lax.dot_general(
            wide_ones,
            jnp.concatenate([upper, lower], axis=1),
            (((1,), (1,)), ((), ())),
            preferred_element_type=jnp.float32,
        )
        delta_ref[head : head + 1, :] = row[:1]
        first_out[head, :half_shard, :] = k_ref[:, cols]
        first_out[head, half_shard:at, :] = v_ref[:, cols]
        first_out[head, at : at + early, :] = q_ref[:early, cols]
        first_out[head, at + early : at + 2 * early, :] = d_mem[:early]
        second_out[head, :late, :] = q_ref[early:, cols]
        second_out[head, late:, :] = d_mem[early:]
        if head % bunch == bunch - 1:
            some = slice(head + 1 - bunch, head + 1)
            body = slice(0, at + 2 * early)
            for index, (source, target) in enumerate(
                ((first_out.at[some, body], first_hbm.at[some, body]), (second_out.at[some], second_hbm.at[some]))
            ):
                copy = pltpu.make_async_copy(source, target, out_sems.at[index, head // bunch])
                copy.start()
                sent.append(copy)
    total = lax.dot_general(
        ones,
        gate_rows[...],
        (((1,), (1,)), ((), ())),
        precision=lax.Precision.HIGHEST,
        preferred_element_type=jnp.float32,
    )
    first = total.astype(jnp.bfloat16).astype(jnp.float32)
    second = (total - first).astype(jnp.bfloat16).astype(jnp.float32)
    third = total - first - second
    addends = first + pltpu.roll(second, heads, 1) + pltpu.roll(third, 2 * heads, 1)
    ext_ref[bias_rows + 1 : bias_rows + 2, :] = addends[:1]
    for head in range(heads):
        ext_ref[bias_rows : bias_rows + 1, :] = delta_ref[head : head + 1, :]
        first_out[head, at + 2 * early :, :] = ext_ref[...].astype(jnp.bfloat16)
    body = slice(at + 2 * early, first_out.shape[1])
    copy = pltpu.make_async_copy(first_out.at[:, body], first_hbm.at[:, body], out_sems.at[0, bunches])
    copy.start()
    sent.append(copy)
    for copy in sent:
        copy.wait()


def assemble(in_ref, out_ref):
    part = out_ref.shape[1] // in_ref.shape[0]
    for source in range(in_ref.shape[0]):
        rows = slice(source * part, (source + 1) * part)
        out_ref[0, rows, :] = in_ref[source, :part, :]
        out_ref[1, rows, :] = in_ref[source, part : 2 * part, :]


def attend(begin, count, q_at, ext_at, qblocks, width, tile, final, own_ref, mate_ref, q_ref, ext_ref, *refs):
    if final:
        before_ref, out_ref, mark, minus, qx, dx, scores, high, total, acc, stage, sems = refs
        early_copy = pltpu.make_async_copy(before_ref, out_ref.at[:, :begin, :], sems.at[0])
        early_copy.start()
    else:
        out_ref, gate_ref, mark, minus, qx, dx, scores, high, total, acc = refs
    sources = q_ref.shape[0]
    units = qx.shape[1] // LANES - 1
    sides = (own_ref, mate_ref)
    steps_side = own_ref.shape[1] // width
    rows_unit = mark.shape[0]
    scale = 1.0 / math.sqrt(LANES)
    exponent = scale * math.log2(math.e)
    chunks = units // 2
    bias_rows = chunks * qblocks

    lane = lax.broadcasted_iota(jnp.int32, (BLK, LANES), 1)
    for block in range(LANES):
        mark[block * BLK : (block + 1) * BLK, :] = jnp.where(lane == block, 1.0, 0.0).astype(jnp.bfloat16)
    wide_lane = lax.broadcasted_iota(jnp.int32, (LANES, LANES), 1)
    for block in range(width // LANES):
        minus[block * LANES : (block + 1) * LANES, :] = jnp.where(wide_lane == 0, -1.0, 0.0).astype(jnp.bfloat16)

    gate_sum = jnp.zeros((1, LANES), jnp.float32)
    for source in range(sources):
        base = source * count
        qx[base : base + count, :LANES] = q_ref[source, q_at : q_at + count, :]
        dx[base : base + count, :LANES] = q_ref[source, q_at + count : q_at + 2 * count, :]
        extra = ext_ref[source, ext_at:, :].astype(jnp.float32)
        code = extra[:bias_rows]
        second = jnp.where(code > 1.5, 1.0, 0.0)
        first = code - 2.0 * second
        for side, hit in enumerate((first, second)):
            bias = jnp.where(hit > 0.5, 0.0, FAR)
            for chunk in range(chunks):
                lanes = (1 + side * chunks + chunk) * LANES
                for block in range(count // BLK):
                    at = chunk * qblocks + begin // BLK + block
                    row = jnp.broadcast_to(bias[at : at + 1], (BLK, LANES)).astype(jnp.bfloat16)
                    qx[base + block * BLK : base + (block + 1) * BLK, lanes : lanes + LANES] = row
        if not final:
            gate_sum = gate_sum + extra[bias_rows + 1 : bias_rows + 2]
        wide = jnp.broadcast_to(extra[bias_rows : bias_rows + 1], (LANES, LANES)).T
        wide = jnp.where(wide_lane == 0, wide, 0.0).astype(jnp.bfloat16)
        dx[base : base + count, LANES:] = wide[begin : begin + count]
    if not final:
        gate_ref[...] = jnp.broadcast_to(gate_sum, gate_ref.shape)

    def one_tile(index, carry):
        here = pl.ds(pl.multiple_of(index * tile, tile), tile)
        high[...] = jnp.full_like(high, -3e38)
        for side, ref in enumerate(sides):
            for unit in range(units // 2):

                def score(at, carry, side=side, ref=ref, unit=unit):
                    rows = pl.ds(pl.multiple_of(unit * rows_unit + at * width, width), width)
                    marks = pl.ds(pl.multiple_of(at * width, width), width)
                    lanes = (1 + side * (units // 2) + unit) * LANES
                    left = jnp.concatenate([qx[here, :LANES], qx[here, lanes : lanes + LANES]], axis=1)
                    right = jnp.concatenate([ref[0, rows, :], mark[marks, :]], axis=1)
                    got = lax.dot_general(
                        left, right, (((1,), (1,)), ((), ())), preferred_element_type=jnp.float32
                    )
                    scores[side * steps_side + unit * (rows_unit // width) + at] = got
                    best = high[...]
                    for column in range(width // LANES):
                        best = jnp.maximum(best, got[:, column * LANES : (column + 1) * LANES])
                    high[...] = best
                    return carry

                lax.fori_loop(0, rows_unit // width, score, 0, unroll=2)
        high[...] = jnp.broadcast_to(jnp.max(high[...], 1, keepdims=True) * exponent, high.shape)
        total[...] = jnp.zeros_like(total)
        acc[...] = jnp.zeros_like(acc)
        for side, ref in enumerate(sides):

            def back(at, carry, side=side, ref=ref):
                rows = pl.ds(pl.multiple_of(at * width, width), width)
                prod = lax.dot_general(
                    dx[here, :],
                    jnp.concatenate([ref[1, rows, :], minus[...]], axis=1),
                    (((1,), (1,)), ((), ())),
                    preferred_element_type=jnp.float32,
                )
                got = scores[side * steps_side + at]
                level = high[...]
                added = total[...]
                pieces = []
                for column in range(width // LANES):
                    cols = slice(column * LANES, (column + 1) * LANES)
                    expo = jnp.exp2(got[:, cols] * exponent - level)
                    added = added + expo
                    pieces.append((expo * prod[:, cols]).astype(jnp.bfloat16))
                total[...] = added
                acc[...] += jnp.dot(
                    jnp.concatenate(pieces, axis=1), ref[0, rows, :], preferred_element_type=jnp.float32
                )
                return carry

            lax.fori_loop(0, steps_side, back, 0, unroll=2)
        weight = scale / jnp.sum(total[...], 1, keepdims=True)
        qx[here, :LANES] = (acc[...] * weight).astype(jnp.bfloat16)
        return carry

    lax.fori_loop(0, qx.shape[0] // tile, one_tile, 0)
    for source in range(sources):
        (stage if final else out_ref)[source] = qx[source * count : (source + 1) * count, :LANES]
    if final:
        late_copy = pltpu.make_async_copy(stage, out_ref.at[:, begin:, :], sems.at[1])
        late_copy.start()
        early_copy.wait()
        late_copy.wait()


def unpack(in_ref, out_ref):
    for head in range(in_ref.shape[0]):
        out_ref[:, head * LANES : (head + 1) * LANES] = in_ref[head]


def local(queries, d_out, o_mem, local_out, mem_keys, mem_values, gate_logit, block_ids):
    shards = lax.axis_size("mem")
    groups = lax.axis_size("grp")
    tokens = queries.shape[1]
    width = queries.shape[2]
    heads = gate_logit.shape[0]
    rows_dev = mem_keys.shape[0]
    qblocks = tokens // BLK
    members = heads
    chunks = shards // heads
    assert width == heads * LANES and shards % heads == 0 and groups % 2 == 0
    assert rows_dev == 16 * BLK and heads * 8 == LANES and tokens == LANES
    half_shard = rows_dev // 2
    units = 2 * chunks
    early = 5 * tokens // 8
    late = tokens - early
    extra = -(-(chunks * qblocks + 2) // 16) * 16
    ext_at = 2 * half_shard + 2 * early
    vmem = pl.BlockSpec(memory_space=pltpu.VMEM)
    smem = pl.BlockSpec(memory_space=pltpu.SMEM)
    hbm = pl.BlockSpec(memory_space=pltpu.HBM)
    bf16 = jnp.bfloat16
    small = pltpu.CompilerParams(vmem_limit_bytes=24 << 20)

    core_groups = [
        [(mo * heads + 2 * chip + core) * groups + 2 * go + gp for chip in range(heads // 2) for gp in range(2)]
        for mo in range(chunks)
        for go in range(groups // 2)
        for core in range(2)
    ]
    exchange = functools.partial(
        lax.all_to_all, axis_name=AXES, split_axis=0, concat_axis=0, tiled=True, axis_index_groups=core_groups
    )

    first_shape = (members, ext_at + extra, LANES)
    second_shape = (members, 2 * late, LANES)
    first_out, second_out = pl.pallas_call(
        functools.partial(pack, heads, chunks, early),
        out_shape=(pltpu.HBM(first_shape, bf16), pltpu.HBM(second_shape, bf16)),
        in_specs=[hbm] * 6 + [smem, vmem],
        out_specs=(hbm, hbm),
        scratch_shapes=[pltpu.VMEM((half_shard, width), bf16)] * 2
        + [pltpu.VMEM((tokens, width), bf16)] * 4
        + [
            pltpu.VMEM((extra, LANES), jnp.float32),
            pltpu.VMEM((heads, LANES), jnp.float32),
            pltpu.VMEM((LANES, LANES), jnp.float32),
            pltpu.VMEM(first_shape, bf16),
            pltpu.VMEM(second_shape, bf16),
            pltpu.SemaphoreType.DMA((4, 6)),
            pltpu.SemaphoreType.DMA((2, 5)),
        ],
        compiler_params=pltpu.CompilerParams(vmem_limit_bytes=56 << 20),
        name="pack",
    )(mem_keys, mem_values, queries[0], d_out[0], o_mem[0], local_out[0], gate_logit, block_ids[0])
    first_in = exchange(first_out)
    second_in = exchange(second_out)
    own = pl.pallas_call(
        assemble,
        out_shape=jax.ShapeDtypeStruct((2, members * half_shard, LANES), bf16),
        in_specs=[vmem],
        out_specs=vmem,
        compiler_params=small,
        name="assemble",
    )(first_in)
    if chunks > 1:
        same = [[mo * heads + mi for mo in range(chunks)] for mi in range(heads)]
        own = lax.all_gather(own, "mem", axis_index_groups=same, axis=1, tiled=True)
    mate = lax.ppermute(own, "mem", [(i, i ^ 1) for i in range(shards)])

    rows_all = 2 * own.shape[1]
    step_width = 512

    def attend_some(begin, count, q_at, final, out_shape, out_specs, *args):
        tile = members * count if chunks == 1 else 256
        return pl.pallas_call(
            functools.partial(attend, begin, count, q_at, ext_at, qblocks, step_width, tile, final),
            out_shape=out_shape,
            in_specs=[vmem] * len(args),
            out_specs=out_specs,
            scratch_shapes=[
                pltpu.VMEM((LANES * BLK, LANES), bf16),
                pltpu.VMEM((step_width, LANES), bf16),
                pltpu.VMEM((members * count, (1 + units) * LANES), bf16),
                pltpu.VMEM((members * count, 2 * LANES), bf16),
                pltpu.VMEM((rows_all // step_width, tile, step_width), jnp.float32),
                pltpu.VMEM((tile, LANES), jnp.float32),
                pltpu.VMEM((tile, LANES), jnp.float32),
                pltpu.VMEM((tile, LANES), jnp.float32),
            ]
            + [pltpu.VMEM((members, count, LANES), bf16), pltpu.SemaphoreType.DMA((2,))] * final,
            compiler_params=pltpu.CompilerParams(vmem_limit_bytes=(40 if chunks == 1 else 44) << 20),
            cost_estimate=pl.CostEstimate(
                flops=2 * members * count * rows_all * LANES * 5,
                bytes_accessed=4 * rows_all * LANES,
                transcendentals=members * count * rows_all,
            ),
            name="attend",
        )(*args)

    part, gate_sum = attend_some(
        0,
        early,
        2 * half_shard,
        False,
        [jax.ShapeDtypeStruct((members, early, LANES), bf16), jax.ShapeDtypeStruct((8, LANES), jnp.float32)],
        [vmem, vmem],
        own,
        mate,
        first_in,
        first_in,
    )
    gate_mate = lax.ppermute(gate_sum, "mem", [(i, i ^ 1) for i in range(shards)])
    grad = attend_some(
        early,
        late,
        0,
        True,
        pltpu.HBM((members, tokens, LANES), bf16),
        hbm,
        own,
        mate,
        second_in,
        first_in,
        part,
    )
    home = exchange(grad)
    d_query = pl.pallas_call(
        unpack,
        out_shape=jax.ShapeDtypeStruct((tokens, width), bf16),
        in_specs=[vmem],
        out_specs=vmem,
        compiler_params=small,
        name="unpack",
    )(home)
    addends = (gate_sum + gate_mate)[0, : 3 * heads]
    gate_total = addends[:heads] + addends[heads : 2 * heads] + addends[2 * heads :]
    if chunks > 1 or groups > 2:
        gate_total = lax.psum(gate_total, AXES) / (2 * members)
    sig = jax.nn.sigmoid(gate_logit)
    d_gate = sig * (1.0 - sig) * gate_total / (shards * groups * tokens * LANES) ** 0.5
    return (d_query[None], d_gate)


def solution(mesh):
    placed = (
        P("grp", "mem", None),
        P("grp", "mem", None),
        P("grp", "mem", None),
        P("grp", "mem", None),
        P("mem", None),
        P("mem", None),
        P(),
        P("grp", "mem", None),
    )
    return jax.shard_map(
        local, mesh=mesh, in_specs=placed, out_specs=(P("grp", "mem", None), P()), check_vma=False
    )
```

```python
import functools
import math

import jax
import jax.numpy as jnp
from jax import lax
from jax.experimental import pallas as pl
from jax.experimental.pallas import tpu as pltpu
from jax.sharding import PartitionSpec as P

BLK = 16
LANES = 128
AXES = ("mem", "grp")
FAR = -1e30


def pack(
    heads,
    chunks,
    early,
    k_hbm,
    v_hbm,
    q_hbm,
    dout_hbm,
    omem_hbm,
    local_hbm,
    gate_ref,
    ids_ref,
    first_hbm,
    second_hbm,
    dout_ref,
    omem_ref,
    local_ref,
    ext_ref,
    delta_ref,
    gate_rows,
    early_ref,
    late_ref,
    extras_ref,
    sems,
    through_sems,
    out_sems,
):
    tokens = q_hbm.shape[0]
    half_shard = k_hbm.shape[0] // 2
    qblocks, names = ids_ref.shape
    late = tokens - early
    at = 2 * half_shard
    core = lax.axis_index("mem") % 2
    parity = lax.axis_index("grp") % 2
    mine = pl.ds(pl.multiple_of(parity * half_shard, half_shard), half_shard)
    bunches = sems.shape[0]
    bunch = heads // bunches
    copies = []
    for index in range(bunches):
        cols = slice(index * bunch * LANES, (index + 1) * bunch * LANES)
        copies.append([])
        for which, (source, target) in enumerate(
            ((dout_hbm, dout_ref), (omem_hbm, omem_ref), (local_hbm, local_ref))
        ):
            copy = pltpu.make_async_copy(source.at[:, cols], target.at[:, cols], sems.at[index, which])
            copy.start()
            copies[index].append(copy)
    sent = []
    for head in range(heads):
        cols = slice(head * LANES, (head + 1) * LANES)
        for which, (source, target) in enumerate(
            (
                (k_hbm.at[mine, cols], first_hbm.at[head, :half_shard]),
                (v_hbm.at[mine, cols], first_hbm.at[head, half_shard:at]),
                (q_hbm.at[:early, cols], first_hbm.at[head, at : at + early]),
                (q_hbm.at[early:, cols], second_hbm.at[head, :late]),
            )
        ):
            copy = pltpu.make_async_copy(source, target, through_sems.at[which, head])
            copy.start()
            sent.append(copy)

    lane = lax.broadcasted_iota(jnp.int32, (1, LANES), 1)
    ids = ids_ref[...]
    bias_rows = chunks * qblocks
    ext_ref[...] = jnp.zeros_like(ext_ref)
    for chunk in range(chunks):
        hits = []
        for side in range(2):
            shard = chunk * heads + 2 * (lane // 16) + (core + side) % 2
            wanted = jnp.broadcast_to(16 * shard + lane % 16, (qblocks, LANES))
            hit = jnp.zeros((qblocks, LANES), jnp.float32)
            for name in range(names):
                hit = jnp.where(ids[:, name : name + 1] == wanted, 1.0, hit)
            hits.append(hit)
        ext_ref[chunk * qblocks : (chunk + 1) * qblocks, :] = hits[0] + 2.0 * hits[1]

    ones = jnp.ones((8, LANES), jnp.float32)
    wide_ones = jnp.ones((16, 2 * LANES), jnp.bfloat16)
    gate_rows[...] = jnp.zeros_like(gate_rows)
    for head in range(heads):
        if head % bunch == 0:
            for copy in copies[head // bunch]:
                copy.wait()
        cols = slice(head * LANES, (head + 1) * LANES)
        sig = jax.nn.sigmoid(jnp.full((8, LANES), gate_ref[head], jnp.float32))[:1]
        d_out = dout_ref[:, cols].astype(jnp.float32)
        o_mem = omem_ref[:, cols].astype(jnp.float32)
        d_mem = (d_out * sig).astype(jnp.bfloat16)
        differ = o_mem - local_ref[:, cols].astype(jnp.float32)
        gate_rows[head : head + 1, :] = jnp.sum(d_out * differ, 0, keepdims=True)
        product = d_mem.astype(jnp.float32) * o_mem
        upper = product.astype(jnp.bfloat16)
        lower = (product - upper.astype(jnp.float32)).astype(jnp.bfloat16)
        row = lax.dot_general(
            wide_ones,
            jnp.concatenate([upper, lower], axis=1),
            (((1,), (1,)), ((), ())),
            preferred_element_type=jnp.float32,
        )
        delta_ref[head : head + 1, :] = row[:1]
        early_ref[head] = d_mem[:early]
        late_ref[head] = d_mem[early:]
        if head % bunch == bunch - 1:
            some = slice(head + 1 - bunch, head + 1)
            for index, (source, target) in enumerate(
                (
                    (early_ref.at[some], first_hbm.at[some, at + early : at + 2 * early]),
                    (late_ref.at[some], second_hbm.at[some, late:]),
                )
            ):
                copy = pltpu.make_async_copy(source, target, out_sems.at[index, head // bunch])
                copy.start()
                sent.append(copy)
    total = lax.dot_general(
        ones,
        gate_rows[...],
        (((1,), (1,)), ((), ())),
        precision=lax.Precision.HIGHEST,
        preferred_element_type=jnp.float32,
    )
    first = total.astype(jnp.bfloat16).astype(jnp.float32)
    second = (total - first).astype(jnp.bfloat16).astype(jnp.float32)
    third = total - first - second
    addends = first + pltpu.roll(second, heads, 1) + pltpu.roll(third, 2 * heads, 1)
    ext_ref[bias_rows + 1 : bias_rows + 2, :] = addends[:1]
    for head in range(heads):
        ext_ref[bias_rows : bias_rows + 1, :] = delta_ref[head : head + 1, :]
        extras_ref[head] = ext_ref[...].astype(jnp.bfloat16)
    copy = pltpu.make_async_copy(extras_ref, first_hbm.at[:, at + 2 * early :], out_sems.at[0, bunches])
    copy.start()
    sent.append(copy)
    for copy in sent:
        copy.wait()


def assemble(gate_at, in_ref, out_ref):
    sources = in_ref.shape[0]
    part = (out_ref.shape[1] - BLK) // sources
    gate = jnp.zeros((1, LANES), jnp.float32)
    for source in range(sources):
        rows = slice(source * part, (source + 1) * part)
        out_ref[0, rows, :] = in_ref[source, :part, :]
        out_ref[1, rows, :] = in_ref[source, part : 2 * part, :]
        block = gate_at // BLK * BLK
        extra = in_ref[source, block : block + BLK, :].astype(jnp.float32)
        gate = gate + extra[gate_at - block : gate_at - block + 1]
    first = gate.astype(jnp.bfloat16).astype(jnp.float32)
    second = (gate - first).astype(jnp.bfloat16).astype(jnp.float32)
    third = gate - first - second
    row = lax.broadcasted_iota(jnp.int32, (BLK, LANES), 0)
    split = jnp.where(row == 0, first, jnp.where(row == 1, second, jnp.where(row == 2, third, 0.0)))
    out_ref[0, sources * part :, :] = split.astype(jnp.bfloat16)
    out_ref[1, sources * part :, :] = jnp.zeros((BLK, LANES), jnp.bfloat16)


def attend(begin, count, q_at, ext_at, qblocks, width, tile, final, own_ref, mate_ref, q_ref, ext_ref, *refs):
    if final:
        before_ref, out_ref, mark, minus, qx, dx, scores, high, total, acc, stage, sems = refs
        early_copy = pltpu.make_async_copy(before_ref, out_ref.at[:, :begin, :], sems.at[0])
        early_copy.start()
    else:
        out_ref, gate_ref, mark, minus, qx, dx, scores, high, total, acc = refs
    sources = q_ref.shape[0]
    units = qx.shape[1] // LANES - 1
    sides = (own_ref, mate_ref)
    rows_unit = mark.shape[0]
    stride = rows_unit + BLK
    steps_unit = rows_unit // width
    scale = 1.0 / math.sqrt(LANES)
    exponent = scale * math.log2(math.e)
    chunks = units // 2
    bias_rows = chunks * qblocks

    lane = lax.broadcasted_iota(jnp.int32, (BLK, LANES), 1)
    for block in range(LANES):
        mark[block * BLK : (block + 1) * BLK, :] = jnp.where(lane == block, 1.0, 0.0).astype(jnp.bfloat16)
    wide_lane = lax.broadcasted_iota(jnp.int32, (LANES, LANES), 1)
    wide_row = lax.broadcasted_iota(jnp.int32, (LANES, LANES), 0)
    minus[...] = jnp.full_like(minus, -1.0)

    for source in range(sources):
        base = source * count
        qx[base : base + count, :LANES] = q_ref[source, q_at : q_at + count, :]
        dx[base : base + count, :LANES] = q_ref[source, q_at + count : q_at + 2 * count, :]
        extra = ext_ref[source, ext_at:, :].astype(jnp.float32)
        code = extra[:bias_rows]
        second = jnp.where(code > 1.5, 1.0, 0.0)
        first = code - 2.0 * second
        for side, hit in enumerate((first, second)):
            bias = jnp.where(hit > 0.5, 0.0, FAR)
            for chunk in range(chunks):
                lanes = (1 + side * chunks + chunk) * LANES
                for block in range(count // BLK):
                    at = chunk * qblocks + begin // BLK + block
                    row = jnp.broadcast_to(bias[at : at + 1], (BLK, LANES)).astype(jnp.bfloat16)
                    qx[base + block * BLK : base + (block + 1) * BLK, lanes : lanes + LANES] = row
        wide = jnp.where(wide_lane == wide_row, extra[bias_rows : bias_rows + 1], 0.0).astype(jnp.bfloat16)
        dx[base : base + count, LANES:] = wide[begin : begin + count]
    if not final:
        gate_sum = jnp.zeros((1, LANES), jnp.float32)
        for ref in sides:
            for unit in range(units // 2):
                at = unit * stride + rows_unit
                gate_sum = gate_sum + jnp.sum(ref[0, at : at + BLK, :].astype(jnp.float32), 0, keepdims=True)
        gate_ref[...] = jnp.broadcast_to(gate_sum, gate_ref.shape)

    def one_tile(index, carry):
        here = pl.ds(pl.multiple_of(index * tile, tile), tile)
        high[...] = jnp.full_like(high, -3e38)
        for side, ref in enumerate(sides):
            for unit in range(units // 2):

                def score(at, carry, side=side, ref=ref, unit=unit):
                    rows = pl.ds(pl.multiple_of(unit * stride + at * width, BLK), width)
                    marks = pl.ds(pl.multiple_of(at * width, width), width)
                    lanes = (1 + side * (units // 2) + unit) * LANES
                    left = jnp.concatenate([qx[here, :LANES], qx[here, lanes : lanes + LANES]], axis=1)
                    right = jnp.concatenate([ref[0, rows, :], mark[marks, :]], axis=1)
                    got = lax.dot_general(
                        left, right, (((1,), (1,)), ((), ())), preferred_element_type=jnp.float32
                    )
                    scores[(side * (units // 2) + unit) * steps_unit + at] = got
                    best = high[...]
                    for column in range(width // LANES):
                        best = jnp.maximum(best, got[:, column * LANES : (column + 1) * LANES])
                    high[...] = best
                    return carry

                lax.fori_loop(0, steps_unit, score, 0, unroll=2)
        high[...] = jnp.broadcast_to(jnp.max(high[...], 1, keepdims=True) * exponent, high.shape)
        total[...] = jnp.zeros_like(total)
        acc[...] = jnp.zeros_like(acc)
        for side, ref in enumerate(sides):
            for unit in range(units // 2):

                def back(at, carry, side=side, ref=ref, unit=unit):
                    rows = pl.ds(pl.multiple_of(unit * stride + at * width, BLK), width)
                    prod = lax.dot_general(
                        dx[here, :],
                        jnp.concatenate([ref[1, rows, :], minus[...]], axis=1),
                        (((1,), (1,)), ((), ())),
                        preferred_element_type=jnp.float32,
                    )
                    got = scores[(side * (units // 2) + unit) * steps_unit + at]
                    level = high[...]
                    added = total[...]
                    pieces = []
                    for column in range(width // LANES):
                        cols = slice(column * LANES, (column + 1) * LANES)
                        expo = jnp.exp2(got[:, cols] * exponent - level)
                        added = added + expo
                        pieces.append((expo * prod[:, cols]).astype(jnp.bfloat16))
                    total[...] = added
                    acc[...] += jnp.dot(
                        jnp.concatenate(pieces, axis=1), ref[0, rows, :], preferred_element_type=jnp.float32
                    )
                    return carry

                lax.fori_loop(0, steps_unit, back, 0, unroll=2)
        weight = scale / jnp.sum(total[...], 1, keepdims=True)
        qx[here, :LANES] = (acc[...] * weight).astype(jnp.bfloat16)
        return carry

    lax.fori_loop(0, qx.shape[0] // tile, one_tile, 0)
    for source in range(sources):
        (stage if final else out_ref)[source] = qx[source * count : (source + 1) * count, :LANES]
    if final:
        late_copy = pltpu.make_async_copy(stage, out_ref.at[:, begin:, :], sems.at[1])
        late_copy.start()
        early_copy.wait()
        late_copy.wait()


def unpack(in_ref, out_hbm, sems):
    copies = []
    for head in range(in_ref.shape[0]):
        cols = slice(head * LANES, (head + 1) * LANES)
        copies.append(pltpu.make_async_copy(in_ref.at[head], out_hbm.at[:, cols], sems.at[head]))
        copies[-1].start()
    for copy in copies:
        copy.wait()


def local(queries, d_out, o_mem, local_out, mem_keys, mem_values, gate_logit, block_ids):
    shards = lax.axis_size("mem")
    groups = lax.axis_size("grp")
    tokens = queries.shape[1]
    width = queries.shape[2]
    heads = gate_logit.shape[0]
    rows_dev = mem_keys.shape[0]
    qblocks = tokens // BLK
    members = heads
    chunks = shards // heads
    assert width == heads * LANES and shards % heads == 0 and groups % 2 == 0
    assert rows_dev == 16 * BLK and heads * 8 == LANES and tokens == LANES
    half_shard = rows_dev // 2
    units = 2 * chunks
    early = 5 * tokens // 8
    late = tokens - early
    extra = -(-(chunks * qblocks + 2) // 16) * 16
    ext_at = 2 * half_shard + 2 * early
    vmem = pl.BlockSpec(memory_space=pltpu.VMEM)
    smem = pl.BlockSpec(memory_space=pltpu.SMEM)
    hbm = pl.BlockSpec(memory_space=pltpu.HBM)
    bf16 = jnp.bfloat16
    small = pltpu.CompilerParams(vmem_limit_bytes=24 << 20)

    core_groups = [
        [(mo * heads + 2 * chip + core) * groups + 2 * go + gp for chip in range(heads // 2) for gp in range(2)]
        for mo in range(chunks)
        for go in range(groups // 2)
        for core in range(2)
    ]
    exchange = functools.partial(
        lax.all_to_all, axis_name=AXES, split_axis=0, concat_axis=0, tiled=True, axis_index_groups=core_groups
    )

    first_shape = (members, ext_at + extra, LANES)
    second_shape = (members, 2 * late, LANES)
    first_out, second_out = pl.pallas_call(
        functools.partial(pack, heads, chunks, early),
        out_shape=(pltpu.HBM(first_shape, bf16), pltpu.HBM(second_shape, bf16)),
        in_specs=[hbm] * 6 + [smem, vmem],
        out_specs=(hbm, hbm),
        scratch_shapes=[pltpu.VMEM((tokens, width), bf16)] * 3
        + [
            pltpu.VMEM((extra, LANES), jnp.float32),
            pltpu.VMEM((heads, LANES), jnp.float32),
            pltpu.VMEM((LANES, LANES), jnp.float32),
            pltpu.VMEM((members, early, LANES), bf16),
            pltpu.VMEM((members, late, LANES), bf16),
            pltpu.VMEM((members, extra, LANES), bf16),
            pltpu.SemaphoreType.DMA((4, 3)),
            pltpu.SemaphoreType.DMA((4, heads)),
            pltpu.SemaphoreType.DMA((2, 5)),
        ],
        compiler_params=pltpu.CompilerParams(vmem_limit_bytes=56 << 20),
        name="pack",
    )(mem_keys, mem_values, queries[0], d_out[0], o_mem[0], local_out[0], gate_logit, block_ids[0])
    first_in = exchange(first_out)
    second_in = exchange(second_out)
    own = pl.pallas_call(
        functools.partial(assemble, ext_at + chunks * qblocks + 1),
        out_shape=jax.ShapeDtypeStruct((2, members * half_shard + BLK, LANES), bf16),
        in_specs=[vmem],
        out_specs=vmem,
        compiler_params=small,
        name="assemble",
    )(first_in)
    if chunks > 1:
        same = [[mo * heads + mi for mo in range(chunks)] for mi in range(heads)]
        own = lax.all_gather(own, "mem", axis_index_groups=same, axis=1, tiled=True)
    mate = lax.ppermute(own, "mem", [(i, i ^ 1) for i in range(shards)])

    rows_all = rows_dev * shards
    step_width = 512

    def attend_some(begin, count, q_at, final, out_shape, out_specs, *args):
        tile = members * count if chunks == 1 else 256
        return pl.pallas_call(
            functools.partial(attend, begin, count, q_at, ext_at, qblocks, step_width, tile, final),
            out_shape=out_shape,
            in_specs=[vmem] * len(args),
            out_specs=out_specs,
            scratch_shapes=[
                pltpu.VMEM((LANES * BLK, LANES), bf16),
                pltpu.VMEM((step_width, LANES), bf16),
                pltpu.VMEM((members * count, (1 + units) * LANES), bf16),
                pltpu.VMEM((members * count, 2 * LANES), bf16),
                pltpu.VMEM((rows_all // step_width, tile, step_width), jnp.float32),
                pltpu.VMEM((tile, LANES), jnp.float32),
                pltpu.VMEM((tile, LANES), jnp.float32),
                pltpu.VMEM((tile, LANES), jnp.float32),
            ]
            + [pltpu.VMEM((members, count, LANES), bf16), pltpu.SemaphoreType.DMA((2,))] * final,
            compiler_params=pltpu.CompilerParams(vmem_limit_bytes=(40 if chunks == 1 else 44) << 20),
            cost_estimate=pl.CostEstimate(
                flops=2 * members * count * rows_all * LANES * 5,
                bytes_accessed=4 * rows_all * LANES,
                transcendentals=members * count * rows_all,
            ),
            name="attend",
        )(*args)

    part, gate_sum = attend_some(
        0,
        early,
        2 * half_shard,
        False,
        [jax.ShapeDtypeStruct((members, early, LANES), bf16), jax.ShapeDtypeStruct((8, LANES), jnp.float32)],
        [vmem, vmem],
        own,
        mate,
        first_in,
        first_in,
    )
    grad = attend_some(
        early,
        late,
        0,
        True,
        pltpu.HBM((members, tokens, LANES), bf16),
        hbm,
        own,
        mate,
        second_in,
        first_in,
        part,
    )
    home = exchange(grad)
    d_query = pl.pallas_call(
        unpack,
        out_shape=pltpu.HBM((tokens, width), bf16),
        in_specs=[vmem],
        out_specs=hbm,
        scratch_shapes=[pltpu.SemaphoreType.DMA((heads,))],
        compiler_params=small,
        name="unpack",
    )(home)
    addends = gate_sum[0, : 3 * heads]
    gate_total = addends[:heads] + addends[heads : 2 * heads] + addends[2 * heads :]
    if chunks > 1 or groups > 2:
        gate_total = lax.psum(gate_total, AXES) / (2 * shards)
    sig = jax.nn.sigmoid(gate_logit)
    d_gate = sig * (1.0 - sig) * gate_total / (shards * groups * tokens * LANES) ** 0.5
    return (d_query[None], d_gate)


def solution(mesh):
    placed = (
        P("grp", "mem", None),
        P("grp", "mem", None),
        P("grp", "mem", None),
        P("grp", "mem", None),
        P("mem", None),
        P("mem", None),
        P(),
        P("grp", "mem", None),
    )
    return jax.shard_map(
        local, mesh=mesh, in_specs=placed, out_specs=(P("grp", "mem", None), P()), check_vma=False
    )
```

```python
import functools
import math

import jax
import jax.numpy as jnp
from jax import lax
from jax.experimental import pallas as pl
from jax.experimental.pallas import tpu as pltpu
from jax.sharding import PartitionSpec as P

BLK = 16
LANES = 128
AXES = ("mem", "grp")
FAR = -1e30
FAN = 4


def position_here(heads):
    return (lax.axis_index("mem") % heads) // 2 * 2 + lax.axis_index("grp") % 2


def pack(
    heads,
    chunks,
    early,
    k_hbm,
    v_hbm,
    q_hbm,
    dout_hbm,
    omem_hbm,
    local_hbm,
    gate_ref,
    ids_ref,
    first_hbm,
    second_hbm,
    k_ref,
    v_ref,
    q_ref,
    dout_ref,
    omem_ref,
    local_ref,
    ext_ref,
    delta_ref,
    gate_rows,
    first_out,
    second_out,
    sems,
    out_sems,
):
    tokens = q_ref.shape[0]
    half_shard = k_ref.shape[0]
    qblocks, names = ids_ref.shape
    core = lax.axis_index("mem") % 2
    parity = lax.axis_index("grp") % 2
    mine = pl.ds(pl.multiple_of(parity * half_shard, half_shard), half_shard)
    bunches = sems.shape[0]
    bunch = heads // bunches
    copies = []
    for index in range(bunches):
        cols = slice(index * bunch * LANES, (index + 1) * bunch * LANES)
        copies.append([])
        for at, (source, target) in enumerate(
            (
                (dout_hbm.at[:, cols], dout_ref),
                (omem_hbm.at[:, cols], omem_ref),
                (local_hbm.at[:, cols], local_ref),
                (q_hbm.at[:, cols], q_ref),
                (k_hbm.at[mine, cols], k_ref),
                (v_hbm.at[mine, cols], v_ref),
            )
        ):
            copy = pltpu.make_async_copy(source, target.at[:, cols], sems.at[index, at])
            copy.start()
            copies[index].append(copy)

    lane = lax.broadcasted_iota(jnp.int32, (1, LANES), 1)
    ids = ids_ref[...]
    bias_rows = chunks * qblocks
    ext_ref[...] = jnp.zeros_like(ext_ref)
    for chunk in range(chunks):
        hits = []
        for side in range(2):
            shard = chunk * heads + 2 * (lane // 16) + (core + side) % 2
            wanted = jnp.broadcast_to(16 * shard + lane % 16, (qblocks, LANES))
            hit = jnp.zeros((qblocks, LANES), jnp.float32)
            for name in range(names):
                hit = jnp.where(ids[:, name : name + 1] == wanted, 1.0, hit)
            hits.append(hit)
        ext_ref[chunk * qblocks : (chunk + 1) * qblocks, :] = hits[0] + 2.0 * hits[1]

    ones = jnp.ones((8, LANES), jnp.float32)
    wide_ones = jnp.ones((16, 2 * LANES), jnp.bfloat16)
    gate_rows[...] = jnp.zeros_like(gate_rows)
    at = 2 * half_shard
    late = tokens - early
    sent = []
    for head in range(heads):
        if head % bunch == 0:
            for copy in copies[head // bunch]:
                copy.wait()
        cols = slice(head * LANES, (head + 1) * LANES)
        sig = jax.nn.sigmoid(jnp.full((8, LANES), gate_ref[head], jnp.float32))[:1]
        d_out = dout_ref[:, cols].astype(jnp.float32)
        o_mem = omem_ref[:, cols].astype(jnp.float32)
        d_mem = (d_out * sig).astype(jnp.bfloat16)
        differ = o_mem - local_ref[:, cols].astype(jnp.float32)
        gate_rows[head : head + 1, :] = jnp.sum(d_out * differ, 0, keepdims=True)
        product = d_mem.astype(jnp.float32) * o_mem
        upper = product.astype(jnp.bfloat16)
        lower = (product - upper.astype(jnp.float32)).astype(jnp.bfloat16)
        row = lax.dot_general(
            wide_ones,
            jnp.concatenate([upper, lower], axis=1),
            (((1,), (1,)), ((), ())),
            preferred_element_type=jnp.float32,
        )
        delta_ref[head : head + 1, :] = row[:1]
        first_out[head, :half_shard, :] = k_ref[:, cols]
        first_out[head, half_shard:at, :] = v_ref[:, cols]
        first_out[head, at : at + early, :] = q_ref[:early, cols]
        first_out[head, at + early : at + 2 * early, :] = d_mem[:early]
        second_out[head, :late, :] = q_ref[early:, cols]
        second_out[head, late:, :] = d_mem[early:]
        if head % bunch == bunch - 1:
            some = slice(head + 1 - bunch, head + 1)
            body = slice(0, at + 2 * early)
            for index, (source, target) in enumerate(
                ((first_out.at[some, body], first_hbm.at[some, body]), (second_out.at[some], second_hbm.at[some]))
            ):
                copy = pltpu.make_async_copy(source, target, out_sems.at[index, head // bunch])
                copy.start()
                sent.append(copy)
    total = lax.dot_general(
        ones,
        gate_rows[...],
        (((1,), (1,)), ((), ())),
        precision=lax.Precision.HIGHEST,
        preferred_element_type=jnp.float32,
    )
    first = total.astype(jnp.bfloat16).astype(jnp.float32)
    second = (total - first).astype(jnp.bfloat16).astype(jnp.float32)
    third = total - first - second
    addends = first + pltpu.roll(second, heads, 1) + pltpu.roll(third, 2 * heads, 1)
    ext_ref[bias_rows + 1 : bias_rows + 2, :] = addends[:1]
    for head in range(heads):
        ext_ref[bias_rows : bias_rows + 1, :] = delta_ref[head : head + 1, :]
        first_out[head, at + 2 * early :, :] = ext_ref[...].astype(jnp.bfloat16)
    body = slice(at + 2 * early, first_out.shape[1])
    copy = pltpu.make_async_copy(first_out.at[:, body], first_hbm.at[:, body], out_sems.at[0, bunches])
    copy.start()
    sent.append(copy)
    for copy in sent:
        copy.wait()


def assemble(gate_at, in_ref, out_ref):
    sources = in_ref.shape[0]
    part = (out_ref.shape[1] - BLK) // sources
    gate = jnp.zeros((1, LANES), jnp.float32)
    for source in range(sources):
        rows = slice(source * part, (source + 1) * part)
        out_ref[0, rows, :] = in_ref[source, :part, :]
        out_ref[1, rows, :] = in_ref[source, part : 2 * part, :]
        block = gate_at // BLK * BLK
        extra = in_ref[source, block : block + BLK, :].astype(jnp.float32)
        gate = gate + extra[gate_at - block : gate_at - block + 1]
    first = gate.astype(jnp.bfloat16).astype(jnp.float32)
    second = (gate - first).astype(jnp.bfloat16).astype(jnp.float32)
    third = gate - first - second
    row = lax.broadcasted_iota(jnp.int32, (BLK, LANES), 0)
    split = jnp.where(row == 0, first, jnp.where(row == 1, second, jnp.where(row == 2, third, 0.0)))
    out_ref[0, sources * part :, :] = split.astype(jnp.bfloat16)
    out_ref[1, sources * part :, :] = jnp.zeros((BLK, LANES), jnp.bfloat16)


def attend(begin, count, q_at, ext_at, qblocks, width, tile, final, own_ref, mate_ref, q_ref, ext_ref, *refs):
    if final:
        outs, (mark, minus, qx, dx, scores, high, total, acc) = refs[:FAN], refs[FAN:]
    else:
        outs, (gate_ref, mark, minus, qx, dx, scores, high, total, acc) = refs[:FAN], refs[FAN:]
    sources = q_ref.shape[0]
    units = qx.shape[1] // LANES - 1
    sides = (own_ref, mate_ref)
    rows_unit = mark.shape[0]
    stride = rows_unit + BLK
    steps_unit = rows_unit // width
    scale = 1.0 / math.sqrt(LANES)
    exponent = scale * math.log2(math.e)
    chunks = units // 2
    bias_rows = chunks * qblocks

    lane = lax.broadcasted_iota(jnp.int32, (BLK, LANES), 1)
    for block in range(LANES):
        mark[block * BLK : (block + 1) * BLK, :] = jnp.where(lane == block, 1.0, 0.0).astype(jnp.bfloat16)
    wide_lane = lax.broadcasted_iota(jnp.int32, (LANES, LANES), 1)
    for block in range(width // LANES):
        minus[block * LANES : (block + 1) * LANES, :] = jnp.where(wide_lane == 0, -1.0, 0.0).astype(jnp.bfloat16)

    for source in range(sources):
        base = source * count
        qx[base : base + count, :LANES] = q_ref[source, q_at : q_at + count, :]
        dx[base : base + count, :LANES] = q_ref[source, q_at + count : q_at + 2 * count, :]
        extra = ext_ref[source, ext_at:, :].astype(jnp.float32)
        code = extra[:bias_rows]
        second = jnp.where(code > 1.5, 1.0, 0.0)
        first = code - 2.0 * second
        for side, hit in enumerate((first, second)):
            bias = jnp.where(hit > 0.5, 0.0, FAR)
            for chunk in range(chunks):
                lanes = (1 + side * chunks + chunk) * LANES
                for block in range(count // BLK):
                    at = chunk * qblocks + begin // BLK + block
                    row = jnp.broadcast_to(bias[at : at + 1], (BLK, LANES)).astype(jnp.bfloat16)
                    qx[base + block * BLK : base + (block + 1) * BLK, lanes : lanes + LANES] = row
        wide = jnp.broadcast_to(extra[bias_rows : bias_rows + 1], (LANES, LANES)).T
        wide = jnp.where(wide_lane == 0, wide, 0.0).astype(jnp.bfloat16)
        dx[base : base + count, LANES:] = wide[begin : begin + count]
    if not final:
        gate_sum = jnp.zeros((1, LANES), jnp.float32)
        for ref in sides:
            for unit in range(units // 2):
                at = unit * stride + rows_unit
                gate_sum = gate_sum + jnp.sum(ref[0, at : at + BLK, :].astype(jnp.float32), 0, keepdims=True)
        gate_ref[...] = jnp.broadcast_to(gate_sum, gate_ref.shape)

    def one_tile(index, carry):
        here = pl.ds(pl.multiple_of(index * tile, tile), tile)
        high[...] = jnp.full_like(high, -3e38)
        for side, ref in enumerate(sides):
            for unit in range(units // 2):

                def score(at, carry, side=side, ref=ref, unit=unit):
                    rows = pl.ds(unit * stride + pl.multiple_of(at * width, width), width)
                    marks = pl.ds(pl.multiple_of(at * width, width), width)
                    lanes = (1 + side * (units // 2) + unit) * LANES
                    left = jnp.concatenate([qx[here, :LANES], qx[here, lanes : lanes + LANES]], axis=1)
                    right = jnp.concatenate([ref[0, rows, :], mark[marks, :]], axis=1)
                    got = lax.dot_general(
                        left, right, (((1,), (1,)), ((), ())), preferred_element_type=jnp.float32
                    )
                    scores[(side * (units // 2) + unit) * steps_unit + at] = got
                    best = high[...]
                    for column in range(width // LANES):
                        best = jnp.maximum(best, got[:, column * LANES : (column + 1) * LANES])
                    high[...] = best
                    return carry

                lax.fori_loop(0, steps_unit, score, 0, unroll=2)
        high[...] = jnp.broadcast_to(jnp.max(high[...], 1, keepdims=True) * exponent, high.shape)
        total[...] = jnp.zeros_like(total)
        acc[...] = jnp.zeros_like(acc)
        for side, ref in enumerate(sides):
            for unit in range(units // 2):

                def back(at, carry, side=side, ref=ref, unit=unit):
                    rows = pl.ds(unit * stride + pl.multiple_of(at * width, width), width)
                    prod = lax.dot_general(
                        dx[here, :],
                        jnp.concatenate([ref[1, rows, :], minus[...]], axis=1),
                        (((1,), (1,)), ((), ())),
                        preferred_element_type=jnp.float32,
                    )
                    got = scores[(side * (units // 2) + unit) * steps_unit + at]
                    level = high[...]
                    added = total[...]
                    pieces = []
                    for column in range(width // LANES):
                        cols = slice(column * LANES, (column + 1) * LANES)
                        expo = jnp.exp2(got[:, cols] * exponent - level)
                        added = added + expo
                        pieces.append((expo * prod[:, cols]).astype(jnp.bfloat16))
                    total[...] = added
                    acc[...] += jnp.dot(
                        jnp.concatenate(pieces, axis=1), ref[0, rows, :], preferred_element_type=jnp.float32
                    )
                    return carry

                lax.fori_loop(0, steps_unit, back, 0, unroll=2)
        weight = scale / jnp.sum(total[...], 1, keepdims=True)
        qx[here, :LANES] = (acc[...] * weight).astype(jnp.bfloat16)
        return carry

    lax.fori_loop(0, qx.shape[0] // tile, one_tile, 0)
    upper = position_here(sources) // FAN
    for step, out in enumerate(outs):
        for lower in range(FAN):
            at = ((upper ^ step) * FAN + lower) * count
            out[lower] = qx[pl.ds(pl.multiple_of(at, BLK), count), :LANES]


def turn(*refs):
    early, late, outs = refs[:FAN], refs[FAN : 2 * FAN], refs[2 * FAN :]
    begin = early[0].shape[1]
    lower = position_here(FAN * FAN) % FAN
    for step in range(FAN):
        for other in range(FAN):
            outs[other][step, :begin, :] = early[step][lower ^ other]
            outs[other][step, begin:, :] = late[step][lower ^ other]


def unpack(*refs):
    out_ref = refs[-1]
    here = position_here(FAN * FAN)
    for other, ref in enumerate(refs[:-1]):
        for step in range(FAN):
            head = here ^ (step * FAN + other)
            out_ref[:, pl.ds(pl.multiple_of(head * LANES, LANES), LANES)] = ref[step]


def local(queries, d_out, o_mem, local_out, mem_keys, mem_values, gate_logit, block_ids):
    shards = lax.axis_size("mem")
    groups = lax.axis_size("grp")
    tokens = queries.shape[1]
    width = queries.shape[2]
    heads = gate_logit.shape[0]
    rows_dev = mem_keys.shape[0]
    qblocks = tokens // BLK
    members = heads
    chunks = shards // heads
    assert width == heads * LANES and shards % heads == 0 and groups % 2 == 0
    assert heads == FAN * FAN and rows_dev == 16 * BLK and heads * 8 == LANES and tokens == LANES
    half_shard = rows_dev // 2
    units = 2 * chunks
    early = 5 * tokens // 8
    late = tokens - early
    extra = -(-(chunks * qblocks + 2) // 16) * 16
    ext_at = 2 * half_shard + 2 * early
    vmem = pl.BlockSpec(memory_space=pltpu.VMEM)
    smem = pl.BlockSpec(memory_space=pltpu.SMEM)
    hbm = pl.BlockSpec(memory_space=pltpu.HBM)
    bf16 = jnp.bfloat16
    small = pltpu.CompilerParams(vmem_limit_bytes=24 << 20)

    core_groups = [
        [(mo * heads + 2 * chip + core) * groups + 2 * go + gp for chip in range(heads // 2) for gp in range(2)]
        for mo in range(chunks)
        for go in range(groups // 2)
        for core in range(2)
    ]
    exchange = functools.partial(
        lax.all_to_all, axis_name=AXES, split_axis=0, concat_axis=0, tiled=True, axis_index_groups=core_groups
    )

    first_shape = (members, ext_at + extra, LANES)
    second_shape = (members, 2 * late, LANES)
    first_out, second_out = pl.pallas_call(
        functools.partial(pack, heads, chunks, early),
        out_shape=(pltpu.HBM(first_shape, bf16), pltpu.HBM(second_shape, bf16)),
        in_specs=[hbm] * 6 + [smem, vmem],
        out_specs=(hbm, hbm),
        scratch_shapes=[pltpu.VMEM((half_shard, width), bf16)] * 2
        + [pltpu.VMEM((tokens, width), bf16)] * 4
        + [
            pltpu.VMEM((extra, LANES), jnp.float32),
            pltpu.VMEM((heads, LANES), jnp.float32),
            pltpu.VMEM((LANES, LANES), jnp.float32),
            pltpu.VMEM(first_shape, bf16),
            pltpu.VMEM(second_shape, bf16),
            pltpu.SemaphoreType.DMA((4, 6)),
            pltpu.SemaphoreType.DMA((2, 5)),
        ],
        compiler_params=pltpu.CompilerParams(vmem_limit_bytes=56 << 20),
        name="pack",
    )(mem_keys, mem_values, queries[0], d_out[0], o_mem[0], local_out[0], gate_logit, block_ids[0])
    first_in = exchange(first_out)
    second_in = exchange(second_out)
    own = pl.pallas_call(
        functools.partial(assemble, ext_at + chunks * qblocks + 1),
        out_shape=jax.ShapeDtypeStruct((2, members * half_shard + BLK, LANES), bf16),
        in_specs=[vmem],
        out_specs=vmem,
        compiler_params=small,
        name="assemble",
    )(first_in)
    if chunks > 1:
        same = [[mo * heads + mi for mo in range(chunks)] for mi in range(heads)]
        own = lax.all_gather(own, "mem", axis_index_groups=same, axis=1, tiled=True)
    mate = lax.ppermute(own, "mem", [(i, i ^ 1) for i in range(shards)])

    rows_all = rows_dev * shards
    step_width = 512

    def attend_some(begin, count, q_at, final, out_shape, out_specs, *args):
        tile = members * count if chunks == 1 else 256
        return pl.pallas_call(
            functools.partial(attend, begin, count, q_at, ext_at, qblocks, step_width, tile, final),
            out_shape=out_shape,
            in_specs=[vmem] * len(args),
            out_specs=out_specs,
            scratch_shapes=[
                pltpu.VMEM((LANES * BLK, LANES), bf16),
                pltpu.VMEM((step_width, LANES), bf16),
                pltpu.VMEM((members * count, (1 + units) * LANES), bf16),
                pltpu.VMEM((members * count, 2 * LANES), bf16),
                pltpu.VMEM((rows_all // step_width, tile, step_width), jnp.float32),
                pltpu.VMEM((tile, LANES), jnp.float32),
                pltpu.VMEM((tile, LANES), jnp.float32),
                pltpu.VMEM((tile, LANES), jnp.float32),
            ],
            compiler_params=pltpu.CompilerParams(vmem_limit_bytes=(40 if chunks == 1 else 44) << 20),
            cost_estimate=pl.CostEstimate(
                flops=2 * members * count * rows_all * LANES * 5,
                bytes_accessed=4 * rows_all * LANES,
                transcendentals=members * count * rows_all,
            ),
            name="attend",
        )(*args)

    def swap(pieces, unit):
        got = [pieces[0]]
        for step in range(1, FAN):
            pairs = []
            for mem in range(shards):
                for grp in range(groups):
                    other = ((mem % heads) // 2 * 2 + grp % 2) ^ (step * unit)
                    to_mem = mem - mem % heads + other // 2 * 2 + mem % 2
                    pairs.append((mem * groups + grp, to_mem * groups + grp - grp % 2 + other % 2))
            got.append(lax.ppermute(pieces[step], AXES, pairs))
        return got

    *early_parts, gate_sum = attend_some(
        0,
        early,
        2 * half_shard,
        False,
        [jax.ShapeDtypeStruct((FAN, early, LANES), bf16)] * FAN + [jax.ShapeDtypeStruct((8, LANES), jnp.float32)],
        [vmem] * (FAN + 1),
        own,
        mate,
        first_in,
        first_in,
    )
    early_home = swap(early_parts, FAN)
    second_in, gate_sum = lax.optimization_barrier((second_in, gate_sum))
    late_parts = attend_some(
        early,
        late,
        0,
        True,
        [jax.ShapeDtypeStruct((FAN, late, LANES), bf16)] * FAN,
        [vmem] * FAN,
        own,
        mate,
        second_in,
        first_in,
    )
    early_home, late_parts = lax.optimization_barrier((early_home, late_parts))
    late_home = swap(late_parts, FAN)
    turned = pl.pallas_call(
        turn,
        out_shape=[jax.ShapeDtypeStruct((FAN, tokens, LANES), bf16)] * FAN,
        in_specs=[vmem] * (2 * FAN),
        out_specs=[vmem] * FAN,
        compiler_params=small,
        name="turn",
    )(*early_home, *late_home)
    d_query = pl.pallas_call(
        unpack,
        out_shape=jax.ShapeDtypeStruct((tokens, width), bf16),
        in_specs=[vmem] * FAN,
        out_specs=vmem,
        compiler_params=small,
        name="unpack",
    )(*swap(turned, 1))
    addends = gate_sum[0, : 3 * heads]
    gate_total = addends[:heads] + addends[heads : 2 * heads] + addends[2 * heads :]
    if chunks > 1 or groups > 2:
        gate_total = lax.psum(gate_total, AXES) / (2 * shards)
    sig = jax.nn.sigmoid(gate_logit)
    d_gate = sig * (1.0 - sig) * gate_total / (shards * groups * tokens * LANES) ** 0.5
    return (d_query[None], d_gate)


def solution(mesh):
    placed = (
        P("grp", "mem", None),
        P("grp", "mem", None),
        P("grp", "mem", None),
        P("grp", "mem", None),
        P("mem", None),
        P("mem", None),
        P(),
        P("grp", "mem", None),
    )
    return jax.shard_map(
        local, mesh=mesh, in_specs=placed, out_specs=(P("grp", "mem", None), P()), check_vma=False
    )
```

```python
import functools
import math

import jax
import jax.numpy as jnp
from jax import lax
from jax.experimental import pallas as pl
from jax.experimental.pallas import tpu as pltpu
from jax.sharding import PartitionSpec as P

BLK = 16
LANES = 128
AXES = ("mem", "grp")
FAR = -1e30


def pack(
    heads,
    chunks,
    early,
    k_hbm,
    v_hbm,
    q_hbm,
    dout_hbm,
    omem_hbm,
    local_hbm,
    gate_ref,
    ids_ref,
    first_hbm,
    second_hbm,
    k_ref,
    v_ref,
    q_ref,
    dout_ref,
    omem_ref,
    local_ref,
    ext_ref,
    delta_ref,
    gate_rows,
    first_out,
    second_out,
    sems,
    out_sems,
):
    tokens = q_ref.shape[0]
    half_shard = k_ref.shape[0]
    qblocks, names = ids_ref.shape
    core = lax.axis_index("mem") % 2
    parity = lax.axis_index("grp") % 2
    mine = pl.ds(pl.multiple_of(parity * half_shard, half_shard), half_shard)
    bunches = sems.shape[0]
    bunch = heads // bunches
    copies = []
    for index in range(bunches):
        cols = slice(index * bunch * LANES, (index + 1) * bunch * LANES)
        copies.append([])
        for at, (source, target) in enumerate(
            (
                (dout_hbm.at[:, cols], dout_ref),
                (omem_hbm.at[:, cols], omem_ref),
                (local_hbm.at[:, cols], local_ref),
                (q_hbm.at[:, cols], q_ref),
                (k_hbm.at[mine, cols], k_ref),
                (v_hbm.at[mine, cols], v_ref),
            )
        ):
            copy = pltpu.make_async_copy(source, target.at[:, cols], sems.at[index, at])
            copy.start()
            copies[index].append(copy)

    lane = lax.broadcasted_iota(jnp.int32, (1, LANES), 1)
    ids = ids_ref[...]
    bias_rows = chunks * qblocks
    ext_ref[...] = jnp.zeros_like(ext_ref)
    for chunk in range(chunks):
        hits = []
        for side in range(2):
            shard = chunk * heads + 2 * (lane // 16) + (core + side) % 2
            wanted = jnp.broadcast_to(16 * shard + lane % 16, (qblocks, LANES))
            hit = jnp.zeros((qblocks, LANES), jnp.float32)
            for name in range(names):
                hit = jnp.where(ids[:, name : name + 1] == wanted, 1.0, hit)
            hits.append(hit)
        ext_ref[chunk * qblocks : (chunk + 1) * qblocks, :] = hits[0] + 2.0 * hits[1]

    ones = jnp.ones((8, LANES), jnp.float32)
    wide_ones = jnp.ones((16, 2 * LANES), jnp.bfloat16)
    gate_rows[...] = jnp.zeros_like(gate_rows)
    at = 2 * half_shard
    late = tokens - early
    sent = []

    def one_head(head, carry):
        cols = pl.ds(pl.multiple_of(head * LANES, LANES), LANES)
        sig = jax.nn.sigmoid(jnp.full((8, LANES), gate_ref[head], jnp.float32))[:1]
        d_out = dout_ref[:, cols].astype(jnp.float32)
        o_mem = omem_ref[:, cols].astype(jnp.float32)
        d_mem = (d_out * sig).astype(jnp.bfloat16)
        differ = o_mem - local_ref[:, cols].astype(jnp.float32)
        gate_rows[pl.ds(head, 1), :] = jnp.sum(d_out * differ, 0, keepdims=True)
        product = d_mem.astype(jnp.float32) * o_mem
        upper = product.astype(jnp.bfloat16)
        lower = (product - upper.astype(jnp.float32)).astype(jnp.bfloat16)
        row = lax.dot_general(
            wide_ones,
            jnp.concatenate([upper, lower], axis=1),
            (((1,), (1,)), ((), ())),
            preferred_element_type=jnp.float32,
        )
        delta_ref[pl.ds(head, 1), :] = row[:1]
        first_out[head, :half_shard, :] = k_ref[:, cols]
        first_out[head, half_shard:at, :] = v_ref[:, cols]
        first_out[head, at : at + early, :] = q_ref[:early, cols]
        first_out[head, at + early : at + 2 * early, :] = d_mem[:early]
        second_out[head, :late, :] = q_ref[early:, cols]
        second_out[head, late:, :] = d_mem[early:]
        return carry

    for index in range(bunches):
        for copy in copies[index]:
            copy.wait()
        lax.fori_loop(index * bunch, (index + 1) * bunch, one_head, 0)
        some = slice(index * bunch, (index + 1) * bunch)
        body = slice(0, at + 2 * early)
        for which, (source, target) in enumerate(
            ((first_out.at[some, body], first_hbm.at[some, body]), (second_out.at[some], second_hbm.at[some]))
        ):
            copy = pltpu.make_async_copy(source, target, out_sems.at[which, index])
            copy.start()
            sent.append(copy)
    total = lax.dot_general(
        ones,
        gate_rows[...],
        (((1,), (1,)), ((), ())),
        precision=lax.Precision.HIGHEST,
        preferred_element_type=jnp.float32,
    )
    first = total.astype(jnp.bfloat16).astype(jnp.float32)
    second = (total - first).astype(jnp.bfloat16).astype(jnp.float32)
    third = total - first - second
    addends = first + pltpu.roll(second, heads, 1) + pltpu.roll(third, 2 * heads, 1)
    ext_ref[bias_rows + 1 : bias_rows + 2, :] = addends[:1]
    for head in range(heads):
        ext_ref[bias_rows : bias_rows + 1, :] = delta_ref[head : head + 1, :]
        first_out[head, at + 2 * early :, :] = ext_ref[...].astype(jnp.bfloat16)
    body = slice(at + 2 * early, first_out.shape[1])
    copy = pltpu.make_async_copy(first_out.at[:, body], first_hbm.at[:, body], out_sems.at[0, bunches])
    copy.start()
    sent.append(copy)
    for copy in sent:
        copy.wait()


def assemble(in_ref, out_ref):
    part = out_ref.shape[1] // in_ref.shape[0]
    for source in range(in_ref.shape[0]):
        rows = slice(source * part, (source + 1) * part)
        out_ref[0, rows, :] = in_ref[source, :part, :]
        out_ref[1, rows, :] = in_ref[source, part : 2 * part, :]


def attend(begin, count, q_at, ext_at, qblocks, width, tile, final, own_ref, mate_ref, q_ref, ext_ref, *refs):
    if final:
        before_ref, out_ref, mark, minus, qx, dx, scores, high, total, acc, stage, sems = refs
        early_copy = pltpu.make_async_copy(before_ref, out_ref.at[:, :begin, :], sems.at[0])
        early_copy.start()
    else:
        out_ref, gate_ref, mark, minus, qx, dx, scores, high, total, acc = refs
    sources = q_ref.shape[0]
    units = qx.shape[1] // LANES - 1
    sides = (own_ref, mate_ref)
    steps_side = own_ref.shape[1] // width
    rows_unit = mark.shape[0]
    scale = 1.0 / math.sqrt(LANES)
    exponent = scale * math.log2(math.e)
    chunks = units // 2
    bias_rows = chunks * qblocks

    lane = lax.broadcasted_iota(jnp.int32, (BLK, LANES), 1)

    def note(block, carry):
        at = pl.ds(pl.multiple_of(block * BLK, BLK), BLK)
        mark[at, :] = jnp.where(lane == block, 1.0, 0.0).astype(jnp.bfloat16)
        return carry

    lax.fori_loop(0, LANES, note, 0, unroll=8)
    wide_lane = lax.broadcasted_iota(jnp.int32, (LANES, LANES), 1)
    for block in range(width // LANES):
        minus[block * LANES : (block + 1) * LANES, :] = jnp.where(wide_lane == 0, -1.0, 0.0).astype(jnp.bfloat16)


    def take(source, gate_sum):
        base = pl.multiple_of(source * count, BLK)
        mine = pl.ds(base, count)
        qx[mine, :LANES] = q_ref[source, q_at : q_at + count, :]
        dx[mine, :LANES] = q_ref[source, q_at + count : q_at + 2 * count, :]
        extra = ext_ref[source, ext_at:, :].astype(jnp.float32)
        code = extra[:bias_rows]
        second = jnp.where(code > 1.5, 1.0, 0.0)
        first = code - 2.0 * second
        for side, hit in enumerate((first, second)):
            bias = jnp.where(hit > 0.5, 0.0, FAR)
            for chunk in range(chunks):
                lanes = (1 + side * chunks + chunk) * LANES
                for block in range(count // BLK):
                    at = chunk * qblocks + begin // BLK + block
                    row = jnp.broadcast_to(bias[at : at + 1], (BLK, LANES)).astype(jnp.bfloat16)
                    qx[pl.ds(base + block * BLK, BLK), lanes : lanes + LANES] = row
        wide = jnp.broadcast_to(extra[bias_rows : bias_rows + 1], (LANES, LANES)).T
        wide = jnp.where(wide_lane == 0, wide, 0.0).astype(jnp.bfloat16)
        dx[mine, LANES:] = wide[begin : begin + count]
        return gate_sum + extra[bias_rows + 1 : bias_rows + 2]

    gate_sum = lax.fori_loop(0, sources, take, jnp.zeros((1, LANES), jnp.float32))
    if not final:
        gate_ref[...] = jnp.broadcast_to(gate_sum, gate_ref.shape)

    def one_tile(index, carry):
        here = pl.ds(pl.multiple_of(index * tile, tile), tile)
        high[...] = jnp.full_like(high, -3e38)
        for side, ref in enumerate(sides):
            for unit in range(units // 2):

                def score(at, carry, side=side, ref=ref, unit=unit):
                    rows = pl.ds(pl.multiple_of(unit * rows_unit + at * width, width), width)
                    marks = pl.ds(pl.multiple_of(at * width, width), width)
                    lanes = (1 + side * (units // 2) + unit) * LANES
                    left = jnp.concatenate([qx[here, :LANES], qx[here, lanes : lanes + LANES]], axis=1)
                    right = jnp.concatenate([ref[0, rows, :], mark[marks, :]], axis=1)
                    got = lax.dot_general(
                        left, right, (((1,), (1,)), ((), ())), preferred_element_type=jnp.float32
                    )
                    scores[side * steps_side + unit * (rows_unit // width) + at] = got
                    best = high[...]
                    for column in range(width // LANES):
                        best = jnp.maximum(best, got[:, column * LANES : (column + 1) * LANES])
                    high[...] = best
                    return carry

                lax.fori_loop(0, rows_unit // width, score, 0)
        high[...] = jnp.broadcast_to(jnp.max(high[...], 1, keepdims=True) * exponent, high.shape)
        total[...] = jnp.zeros_like(total)
        acc[...] = jnp.zeros_like(acc)
        for side, ref in enumerate(sides):

            def back(at, carry, side=side, ref=ref):
                rows = pl.ds(pl.multiple_of(at * width, width), width)
                prod = lax.dot_general(
                    dx[here, :],
                    jnp.concatenate([ref[1, rows, :], minus[...]], axis=1),
                    (((1,), (1,)), ((), ())),
                    preferred_element_type=jnp.float32,
                )
                got = scores[side * steps_side + at]
                level = high[...]
                added = total[...]
                pieces = []
                for column in range(width // LANES):
                    cols = slice(column * LANES, (column + 1) * LANES)
                    expo = jnp.exp2(got[:, cols] * exponent - level)
                    added = added + expo
                    pieces.append((expo * prod[:, cols]).astype(jnp.bfloat16))
                total[...] = added
                acc[...] += jnp.dot(
                    jnp.concatenate(pieces, axis=1), ref[0, rows, :], preferred_element_type=jnp.float32
                )
                return carry

            lax.fori_loop(0, steps_side, back, 0)
        weight = scale / jnp.sum(total[...], 1, keepdims=True)
        qx[here, :LANES] = (acc[...] * weight).astype(jnp.bfloat16)
        return carry

    lax.fori_loop(0, qx.shape[0] // tile, one_tile, 0)

    def give(source, carry):
        at = pl.ds(pl.multiple_of(source * count, BLK), count)
        (stage if final else out_ref)[source] = qx[at, :LANES]
        return carry

    lax.fori_loop(0, sources, give, 0)
    if final:
        late_copy = pltpu.make_async_copy(stage, out_ref.at[:, begin:, :], sems.at[1])
        late_copy.start()
        early_copy.wait()
        late_copy.wait()


def unpack(in_ref, out_ref):
    for head in range(in_ref.shape[0]):
        out_ref[:, head * LANES : (head + 1) * LANES] = in_ref[head]


def local(queries, d_out, o_mem, local_out, mem_keys, mem_values, gate_logit, block_ids):
    shards = lax.axis_size("mem")
    groups = lax.axis_size("grp")
    tokens = queries.shape[1]
    width = queries.shape[2]
    heads = gate_logit.shape[0]
    rows_dev = mem_keys.shape[0]
    qblocks = tokens // BLK
    members = heads
    chunks = shards // heads
    assert width == heads * LANES and shards % heads == 0 and groups % 2 == 0
    assert rows_dev == 16 * BLK and heads * 8 == LANES and tokens == LANES
    half_shard = rows_dev // 2
    units = 2 * chunks
    early = 5 * tokens // 8
    late = tokens - early
    extra = -(-(chunks * qblocks + 2) // 16) * 16
    ext_at = 2 * half_shard + 2 * early
    vmem = pl.BlockSpec(memory_space=pltpu.VMEM)
    smem = pl.BlockSpec(memory_space=pltpu.SMEM)
    hbm = pl.BlockSpec(memory_space=pltpu.HBM)
    bf16 = jnp.bfloat16
    small = pltpu.CompilerParams(vmem_limit_bytes=24 << 20)

    core_groups = [
        [(mo * heads + 2 * chip + core) * groups + 2 * go + gp for chip in range(heads // 2) for gp in range(2)]
        for mo in range(chunks)
        for go in range(groups // 2)
        for core in range(2)
    ]
    exchange = functools.partial(
        lax.all_to_all, axis_name=AXES, split_axis=0, concat_axis=0, tiled=True, axis_index_groups=core_groups
    )

    first_shape = (members, ext_at + extra, LANES)
    second_shape = (members, 2 * late, LANES)
    first_out, second_out = pl.pallas_call(
        functools.partial(pack, heads, chunks, early),
        out_shape=(pltpu.HBM(first_shape, bf16), pltpu.HBM(second_shape, bf16)),
        in_specs=[hbm] * 6 + [smem, vmem],
        out_specs=(hbm, hbm),
        scratch_shapes=[pltpu.VMEM((half_shard, width), bf16)] * 2
        + [pltpu.VMEM((tokens, width), bf16)] * 4
        + [
            pltpu.VMEM((extra, LANES), jnp.float32),
            pltpu.VMEM((heads, LANES), jnp.float32),
            pltpu.VMEM((LANES, LANES), jnp.float32),
            pltpu.VMEM(first_shape, bf16),
            pltpu.VMEM(second_shape, bf16),
            pltpu.SemaphoreType.DMA((4, 6)),
            pltpu.SemaphoreType.DMA((2, 5)),
        ],
        compiler_params=pltpu.CompilerParams(vmem_limit_bytes=56 << 20),
        name="pack",
    )(mem_keys, mem_values, queries[0], d_out[0], o_mem[0], local_out[0], gate_logit, block_ids[0])
    first_in = exchange(first_out)
    second_in = exchange(second_out)
    own = pl.pallas_call(
        assemble,
        out_shape=jax.ShapeDtypeStruct((2, members * half_shard, LANES), bf16),
        in_specs=[vmem],
        out_specs=vmem,
        compiler_params=small,
        name="assemble",
    )(first_in)
    if chunks > 1:
        same = [[mo * heads + mi for mo in range(chunks)] for mi in range(heads)]
        own = lax.all_gather(own, "mem", axis_index_groups=same, axis=1, tiled=True)
    mate = lax.ppermute(own, "mem", [(i, i ^ 1) for i in range(shards)])

    rows_all = 2 * own.shape[1]
    step_width = 512

    def attend_some(begin, count, q_at, final, out_shape, out_specs, *args):
        tile = members * count if chunks == 1 else 256
        return pl.pallas_call(
            functools.partial(attend, begin, count, q_at, ext_at, qblocks, step_width, tile, final),
            out_shape=out_shape,
            in_specs=[vmem] * len(args),
            out_specs=out_specs,
            scratch_shapes=[
                pltpu.VMEM((LANES * BLK, LANES), bf16),
                pltpu.VMEM((step_width, LANES), bf16),
                pltpu.VMEM((members * count, (1 + units) * LANES), bf16),
                pltpu.VMEM((members * count, 2 * LANES), bf16),
                pltpu.VMEM((rows_all // step_width, tile, step_width), jnp.float32),
                pltpu.VMEM((tile, LANES), jnp.float32),
                pltpu.VMEM((tile, LANES), jnp.float32),
                pltpu.VMEM((tile, LANES), jnp.float32),
            ]
            + [pltpu.VMEM((members, count, LANES), bf16), pltpu.SemaphoreType.DMA((2,))] * final,
            compiler_params=pltpu.CompilerParams(vmem_limit_bytes=(40 if chunks == 1 else 44) << 20),
            cost_estimate=pl.CostEstimate(
                flops=2 * members * count * rows_all * LANES * 5,
                bytes_accessed=4 * rows_all * LANES,
                transcendentals=members * count * rows_all,
            ),
            name="attend",
        )(*args)

    part, gate_sum = attend_some(
        0,
        early,
        2 * half_shard,
        False,
        [jax.ShapeDtypeStruct((members, early, LANES), bf16), jax.ShapeDtypeStruct((8, LANES), jnp.float32)],
        [vmem, vmem],
        own,
        mate,
        first_in,
        first_in,
    )
    gate_mate = lax.ppermute(gate_sum, "mem", [(i, i ^ 1) for i in range(shards)])
    grad = attend_some(
        early,
        late,
        0,
        True,
        pltpu.HBM((members, tokens, LANES), bf16),
        hbm,
        own,
        mate,
        second_in,
        first_in,
        part,
    )
    home = exchange(grad)
    d_query = pl.pallas_call(
        unpack,
        out_shape=jax.ShapeDtypeStruct((tokens, width), bf16),
        in_specs=[vmem],
        out_specs=vmem,
        compiler_params=small,
        name="unpack",
    )(home)
    addends = (gate_sum + gate_mate)[0, : 3 * heads]
    gate_total = addends[:heads] + addends[heads : 2 * heads] + addends[2 * heads :]
    if chunks > 1 or groups > 2:
        gate_total = lax.psum(gate_total, AXES) / (2 * members)
    sig = jax.nn.sigmoid(gate_logit)
    d_gate = sig * (1.0 - sig) * gate_total / (shards * groups * tokens * LANES) ** 0.5
    return (d_query[None], d_gate)


def solution(mesh):
    placed = (
        P("grp", "mem", None),
        P("grp", "mem", None),
        P("grp", "mem", None),
        P("grp", "mem", None),
        P("mem", None),
        P("mem", None),
        P(),
        P("grp", "mem", None),
    )
    return jax.shard_map(
        local, mesh=mesh, in_specs=placed, out_specs=(P("grp", "mem", None), P()), check_vma=False
    )
```

```python
import functools
import math

import jax
import jax.numpy as jnp
from jax import lax
from jax.experimental import pallas as pl
from jax.experimental.pallas import tpu as pltpu
from jax.sharding import PartitionSpec as P

BLK = 16
LANES = 128
AXES = ("mem", "grp")
FAR = -1e30


def pack(
    heads,
    chunks,
    early,
    k_hbm,
    v_hbm,
    q_hbm,
    dout_hbm,
    omem_hbm,
    local_hbm,
    gate_ref,
    ids_ref,
    first_hbm,
    second_hbm,
    k_ref,
    v_ref,
    q_ref,
    dout_ref,
    omem_ref,
    local_ref,
    ext_ref,
    delta_ref,
    gate_rows,
    first_out,
    second_out,
    sems,
    out_sems,
):
    tokens = q_ref.shape[0]
    half_shard = k_ref.shape[0]
    qblocks, names = ids_ref.shape
    core = lax.axis_index("mem") % 2
    parity = lax.axis_index("grp") % 2
    mine = pl.ds(pl.multiple_of(parity * half_shard, half_shard), half_shard)
    bunches = sems.shape[0]
    bunch = heads // bunches
    copies = []
    for index in range(bunches):
        cols = slice(index * bunch * LANES, (index + 1) * bunch * LANES)
        copies.append([])
        for at, (source, target) in enumerate(
            (
                (dout_hbm.at[:, cols], dout_ref),
                (omem_hbm.at[:, cols], omem_ref),
                (local_hbm.at[:, cols], local_ref),
                (q_hbm.at[:, cols], q_ref),
                (k_hbm.at[mine, cols], k_ref),
                (v_hbm.at[mine, cols], v_ref),
            )
        ):
            copy = pltpu.make_async_copy(source, target.at[:, cols], sems.at[index, at])
            copy.start()
            copies[index].append(copy)

    lane = lax.broadcasted_iota(jnp.int32, (1, LANES), 1)
    ids = ids_ref[...]
    bias_rows = chunks * qblocks
    ext_ref[...] = jnp.zeros_like(ext_ref)
    for chunk in range(chunks):
        hits = []
        for side in range(2):
            shard = chunk * heads + 2 * (lane // 16) + (core + side) % 2
            wanted = jnp.broadcast_to(16 * shard + lane % 16, (qblocks, LANES))
            hit = jnp.zeros((qblocks, LANES), jnp.float32)
            for name in range(names):
                hit = jnp.where(ids[:, name : name + 1] == wanted, 1.0, hit)
            hits.append(hit)
        ext_ref[chunk * qblocks : (chunk + 1) * qblocks, :] = hits[0] + 2.0 * hits[1]

    ones = jnp.ones((8, LANES), jnp.float32)
    wide_ones = jnp.ones((16, 2 * LANES), jnp.bfloat16)
    gate_rows[...] = jnp.zeros_like(gate_rows)
    at = 2 * half_shard
    late = tokens - early
    sent = []
    for head in range(heads):
        if head % bunch == 0:
            for copy in copies[head // bunch]:
                copy.wait()
        cols = slice(head * LANES, (head + 1) * LANES)
        sig = jax.nn.sigmoid(jnp.full((8, LANES), gate_ref[head], jnp.float32))[:1]
        d_out = dout_ref[:, cols].astype(jnp.float32)
        o_mem = omem_ref[:, cols].astype(jnp.float32)
        d_mem = (d_out * sig).astype(jnp.bfloat16)
        differ = o_mem - local_ref[:, cols].astype(jnp.float32)
        gate_rows[head : head + 1, :] = jnp.sum(d_out * differ, 0, keepdims=True)
        product = d_mem.astype(jnp.float32) * o_mem
        upper = product.astype(jnp.bfloat16)
        lower = (product - upper.astype(jnp.float32)).astype(jnp.bfloat16)
        row = lax.dot_general(
            wide_ones,
            jnp.concatenate([upper, lower], axis=1),
            (((1,), (1,)), ((), ())),
            preferred_element_type=jnp.float32,
        )
        delta_ref[head : head + 1, :] = row[:1]
        first_out[head, :half_shard, :] = k_ref[:, cols]
        first_out[head, half_shard:at, :] = v_ref[:, cols]
        first_out[head, at : at + early, :] = q_ref[:early, cols]
        first_out[head, at + early : at + 2 * early, :] = d_mem[:early]
        second_out[head, :late, :] = q_ref[early:, cols]
        second_out[head, late:, :] = d_mem[early:]
        if head % bunch == bunch - 1:
            some = slice(head + 1 - bunch, head + 1)
            body = slice(0, at + 2 * early)
            for index, (source, target) in enumerate(
                ((first_out.at[some, body], first_hbm.at[some, body]), (second_out.at[some], second_hbm.at[some]))
            ):
                copy = pltpu.make_async_copy(source, target, out_sems.at[index, head // bunch])
                copy.start()
                sent.append(copy)
    total = lax.dot_general(
        ones,
        gate_rows[...],
        (((1,), (1,)), ((), ())),
        precision=lax.Precision.HIGHEST,
        preferred_element_type=jnp.float32,
    )
    first = total.astype(jnp.bfloat16).astype(jnp.float32)
    second = (total - first).astype(jnp.bfloat16).astype(jnp.float32)
    third = total - first - second
    addends = first + pltpu.roll(second, heads, 1) + pltpu.roll(third, 2 * heads, 1)
    ext_ref[bias_rows + 1 : bias_rows + 2, :] = addends[:1]
    for head in range(heads):
        ext_ref[bias_rows : bias_rows + 1, :] = delta_ref[head : head + 1, :]
        first_out[head, at + 2 * early :, :] = ext_ref[...].astype(jnp.bfloat16)
    body = slice(at + 2 * early, first_out.shape[1])
    copy = pltpu.make_async_copy(first_out.at[:, body], first_hbm.at[:, body], out_sems.at[0, bunches])
    copy.start()
    sent.append(copy)
    for copy in sent:
        copy.wait()


def assemble(in_ref, out_ref):
    part = out_ref.shape[1] // in_ref.shape[0]
    for source in range(in_ref.shape[0]):
        rows = slice(source * part, (source + 1) * part)
        out_ref[0, rows, :] = in_ref[source, :part, :]
        out_ref[1, rows, :] = in_ref[source, part : 2 * part, :]


def attend(begin, count, q_at, ext_at, qblocks, width, tile, final, own_ref, mate_ref, q_ref, ext_ref, *refs):
    if final:
        before_ref, out_ref, mark, minus, qx, dx, scores, high, total, acc, stage, sems = refs
        early_copy = pltpu.make_async_copy(before_ref, out_ref.at[:, :begin, :], sems.at[0])
        early_copy.start()
    else:
        out_ref, gate_ref, mark, minus, qx, dx, scores, high, total, acc = refs
    sources = q_ref.shape[0]
    units = qx.shape[1] // LANES - 1
    sides = (own_ref, mate_ref)
    steps_side = own_ref.shape[1] // width
    rows_unit = mark.shape[0]
    scale = 1.0 / math.sqrt(LANES)
    exponent = scale * math.log2(math.e)
    chunks = units // 2
    bias_rows = chunks * qblocks

    lane = lax.broadcasted_iota(jnp.int32, (BLK, LANES), 1)
    for block in range(LANES):
        mark[block * BLK : (block + 1) * BLK, :] = jnp.where(lane == block, 1.0, 0.0).astype(jnp.bfloat16)
    wide_lane = lax.broadcasted_iota(jnp.int32, (LANES, LANES), 1)
    for block in range(width // LANES):
        minus[block * LANES : (block + 1) * LANES, :] = jnp.where(wide_lane == 0, -1.0, 0.0).astype(jnp.bfloat16)

    gate_sum = jnp.zeros((1, LANES), jnp.float32)
    for source in range(sources):
        base = source * count
        qx[base : base + count, :LANES] = q_ref[source, q_at : q_at + count, :]
        dx[base : base + count, :LANES] = q_ref[source, q_at + count : q_at + 2 * count, :]
        extra = ext_ref[source, ext_at:, :].astype(jnp.float32)
        code = extra[:bias_rows]
        second = jnp.where(code > 1.5, 1.0, 0.0)
        first = code - 2.0 * second
        for side, hit in enumerate((first, second)):
            bias = jnp.where(hit > 0.5, 0.0, FAR)
            for chunk in range(chunks):
                lanes = (1 + side * chunks + chunk) * LANES
                for block in range(count // BLK):
                    at = chunk * qblocks + begin // BLK + block
                    row = jnp.broadcast_to(bias[at : at + 1], (BLK, LANES)).astype(jnp.bfloat16)
                    qx[base + block * BLK : base + (block + 1) * BLK, lanes : lanes + LANES] = row
        if not final:
            gate_sum = gate_sum + extra[bias_rows + 1 : bias_rows + 2]
        wide = jnp.broadcast_to(extra[bias_rows : bias_rows + 1], (LANES, LANES)).T
        wide = jnp.where(wide_lane == 0, wide, 0.0).astype(jnp.bfloat16)
        dx[base : base + count, LANES:] = wide[begin : begin + count]
    if not final:
        gate_ref[...] = jnp.broadcast_to(gate_sum, gate_ref.shape)

    def one_tile(index, carry):
        here = pl.ds(pl.multiple_of(index * tile, tile), tile)
        high[...] = jnp.full_like(high, -3e38)
        for side, ref in enumerate(sides):
            for unit in range(units // 2):

                def score(at, carry, side=side, ref=ref, unit=unit):
                    rows = pl.ds(pl.multiple_of(unit * rows_unit + at * width, width), width)
                    marks = pl.ds(pl.multiple_of(at * width, width), width)
                    lanes = (1 + side * (units // 2) + unit) * LANES
                    left = jnp.concatenate([qx[here, :LANES], qx[here, lanes : lanes + LANES]], axis=1)
                    right = jnp.concatenate([ref[0, rows, :], mark[marks, :]], axis=1)
                    got = lax.dot_general(
                        left, right, (((1,), (1,)), ((), ())), preferred_element_type=jnp.float32
                    )
                    scores[side * steps_side + unit * (rows_unit // width) + at] = got
                    best = high[...]
                    for column in range(width // LANES):
                        best = jnp.maximum(best, got[:, column * LANES : (column + 1) * LANES])
                    high[...] = best
                    return carry

                lax.fori_loop(0, rows_unit // width, score, 0, unroll=2 if final else 1)
        high[...] = jnp.broadcast_to(jnp.max(high[...], 1, keepdims=True) * exponent, high.shape)
        total[...] = jnp.zeros_like(total)
        acc[...] = jnp.zeros_like(acc)
        for side, ref in enumerate(sides):

            def back(at, carry, side=side, ref=ref):
                rows = pl.ds(pl.multiple_of(at * width, width), width)
                prod = lax.dot_general(
                    dx[here, :],
                    jnp.concatenate([ref[1, rows, :], minus[...]], axis=1),
                    (((1,), (1,)), ((), ())),
                    preferred_element_type=jnp.float32,
                )
                got = scores[side * steps_side + at]
                level = high[...]
                added = total[...]
                pieces = []
                for column in range(width // LANES):
                    cols = slice(column * LANES, (column + 1) * LANES)
                    expo = jnp.exp2(got[:, cols] * exponent - level)
                    added = added + expo
                    pieces.append((expo * prod[:, cols]).astype(jnp.bfloat16))
                total[...] = added
                acc[...] += jnp.dot(
                    jnp.concatenate(pieces, axis=1), ref[0, rows, :], preferred_element_type=jnp.float32
                )
                return carry

            lax.fori_loop(0, steps_side, back, 0, unroll=2 if final else 1)
        weight = scale / jnp.sum(total[...], 1, keepdims=True)
        qx[here, :LANES] = (acc[...] * weight).astype(jnp.bfloat16)
        return carry

    lax.fori_loop(0, qx.shape[0] // tile, one_tile, 0)
    for source in range(sources):
        (stage if final else out_ref)[source] = qx[source * count : (source + 1) * count, :LANES]
    if final:
        late_copy = pltpu.make_async_copy(stage, out_ref.at[:, begin:, :], sems.at[1])
        late_copy.start()
        early_copy.wait()
        late_copy.wait()


def unpack(in_ref, out_ref):
    for head in range(in_ref.shape[0]):
        out_ref[:, head * LANES : (head + 1) * LANES] = in_ref[head]


def local(queries, d_out, o_mem, local_out, mem_keys, mem_values, gate_logit, block_ids):
    shards = lax.axis_size("mem")
    groups = lax.axis_size("grp")
    tokens = queries.shape[1]
    width = queries.shape[2]
    heads = gate_logit.shape[0]
    rows_dev = mem_keys.shape[0]
    qblocks = tokens // BLK
    members = heads
    chunks = shards // heads
    assert width == heads * LANES and shards % heads == 0 and groups % 2 == 0
    assert rows_dev == 16 * BLK and heads * 8 == LANES and tokens == LANES
    half_shard = rows_dev // 2
    units = 2 * chunks
    early = tokens // 2
    late = tokens - early
    extra = -(-(chunks * qblocks + 2) // 16) * 16
    ext_at = 2 * half_shard + 2 * early
    vmem = pl.BlockSpec(memory_space=pltpu.VMEM)
    smem = pl.BlockSpec(memory_space=pltpu.SMEM)
    hbm = pl.BlockSpec(memory_space=pltpu.HBM)
    bf16 = jnp.bfloat16
    small = pltpu.CompilerParams(vmem_limit_bytes=24 << 20)

    core_groups = [
        [(mo * heads + 2 * chip + core) * groups + 2 * go + gp for chip in range(heads // 2) for gp in range(2)]
        for mo in range(chunks)
        for go in range(groups // 2)
        for core in range(2)
    ]
    exchange = functools.partial(
        lax.all_to_all, axis_name=AXES, split_axis=0, concat_axis=0, tiled=True, axis_index_groups=core_groups
    )

    first_shape = (members, ext_at + extra, LANES)
    second_shape = (members, 2 * late, LANES)
    first_out, second_out = pl.pallas_call(
        functools.partial(pack, heads, chunks, early),
        out_shape=(pltpu.HBM(first_shape, bf16), pltpu.HBM(second_shape, bf16)),
        in_specs=[hbm] * 6 + [smem, vmem],
        out_specs=(hbm, hbm),
        scratch_shapes=[pltpu.VMEM((half_shard, width), bf16)] * 2
        + [pltpu.VMEM((tokens, width), bf16)] * 4
        + [
            pltpu.VMEM((extra, LANES), jnp.float32),
            pltpu.VMEM((heads, LANES), jnp.float32),
            pltpu.VMEM((LANES, LANES), jnp.float32),
            pltpu.VMEM(first_shape, bf16),
            pltpu.VMEM(second_shape, bf16),
            pltpu.SemaphoreType.DMA((2, 6)),
            pltpu.SemaphoreType.DMA((2, 3)),
        ],
        compiler_params=pltpu.CompilerParams(vmem_limit_bytes=56 << 20),
        name="pack",
    )(mem_keys, mem_values, queries[0], d_out[0], o_mem[0], local_out[0], gate_logit, block_ids[0])
    first_in = exchange(first_out)
    second_in = exchange(second_out)
    own = pl.pallas_call(
        assemble,
        out_shape=jax.ShapeDtypeStruct((2, members * half_shard, LANES), bf16),
        in_specs=[vmem],
        out_specs=vmem,
        compiler_params=small,
        name="assemble",
    )(first_in)
    if chunks > 1:
        same = [[mo * heads + mi for mo in range(chunks)] for mi in range(heads)]
        own = lax.all_gather(own, "mem", axis_index_groups=same, axis=1, tiled=True)
    mate = lax.ppermute(own, "mem", [(i, i ^ 1) for i in range(shards)])

    rows_all = 2 * own.shape[1]
    step_width = 512

    def attend_some(begin, count, q_at, final, out_shape, out_specs, *args):
        tile = members * count if chunks == 1 else 256
        return pl.pallas_call(
            functools.partial(attend, begin, count, q_at, ext_at, qblocks, step_width, tile, final),
            out_shape=out_shape,
            in_specs=[vmem] * len(args),
            out_specs=out_specs,
            scratch_shapes=[
                pltpu.VMEM((LANES * BLK, LANES), bf16),
                pltpu.VMEM((step_width, LANES), bf16),
                pltpu.VMEM((members * count, (1 + units) * LANES), bf16),
                pltpu.VMEM((members * count, 2 * LANES), bf16),
                pltpu.VMEM((rows_all // step_width, tile, step_width), jnp.float32),
                pltpu.VMEM((tile, LANES), jnp.float32),
                pltpu.VMEM((tile, LANES), jnp.float32),
                pltpu.VMEM((tile, LANES), jnp.float32),
            ]
            + [pltpu.VMEM((members, count, LANES), bf16), pltpu.SemaphoreType.DMA((2,))] * final,
            compiler_params=pltpu.CompilerParams(vmem_limit_bytes=(40 if chunks == 1 else 44) << 20),
            cost_estimate=pl.CostEstimate(
                flops=2 * members * count * rows_all * LANES * 5,
                bytes_accessed=4 * rows_all * LANES,
                transcendentals=members * count * rows_all,
            ),
            name="attend",
        )(*args)

    part, gate_sum = attend_some(
        0,
        early,
        2 * half_shard,
        False,
        [jax.ShapeDtypeStruct((members, early, LANES), bf16), jax.ShapeDtypeStruct((8, LANES), jnp.float32)],
        [vmem, vmem],
        own,
        mate,
        first_in,
        first_in,
    )
    gate_mate = lax.ppermute(gate_sum, "mem", [(i, i ^ 1) for i in range(shards)])
    grad = attend_some(
        early,
        late,
        0,
        True,
        pltpu.HBM((members, tokens, LANES), bf16),
        hbm,
        own,
        mate,
        second_in,
        first_in,
        part,
    )
    home = exchange(grad)
    d_query = pl.pallas_call(
        unpack,
        out_shape=jax.ShapeDtypeStruct((tokens, width), bf16),
        in_specs=[vmem],
        out_specs=vmem,
        compiler_params=small,
        name="unpack",
    )(home)
    addends = (gate_sum + gate_mate)[0, : 3 * heads]
    gate_total = addends[:heads] + addends[heads : 2 * heads] + addends[2 * heads :]
    if chunks > 1 or groups > 2:
        gate_total = lax.psum(gate_total, AXES) / (2 * members)
    sig = jax.nn.sigmoid(gate_logit)
    d_gate = sig * (1.0 - sig) * gate_total / (shards * groups * tokens * LANES) ** 0.5
    return (d_query[None], d_gate)


def solution(mesh):
    placed = (
        P("grp", "mem", None),
        P("grp", "mem", None),
        P("grp", "mem", None),
        P("grp", "mem", None),
        P("mem", None),
        P("mem", None),
        P(),
        P("grp", "mem", None),
    )
    return jax.shard_map(
        local, mesh=mesh, in_specs=placed, out_specs=(P("grp", "mem", None), P()), check_vma=False
    )
```

```python
import functools
import math

import jax
import jax.numpy as jnp
from jax import lax
from jax.experimental import pallas as pl
from jax.experimental.pallas import tpu as pltpu
from jax.sharding import PartitionSpec as P

BLK = 16
LANES = 128
AXES = ("mem", "grp")
FAR = -1e30


def pack(
    heads,
    chunks,
    early,
    k_hbm,
    v_hbm,
    q_hbm,
    dout_hbm,
    omem_hbm,
    local_hbm,
    gate_ref,
    ids_ref,
    first_hbm,
    second_hbm,
    k_ref,
    v_ref,
    q_ref,
    dout_ref,
    omem_ref,
    local_ref,
    ext_ref,
    delta_ref,
    gate_rows,
    first_out,
    second_out,
    sems,
    out_sems,
):
    tokens = q_ref.shape[0]
    half_shard = k_ref.shape[0]
    qblocks, names = ids_ref.shape
    core = lax.axis_index("mem") % 2
    parity = lax.axis_index("grp") % 2
    mine = pl.ds(pl.multiple_of(parity * half_shard, half_shard), half_shard)
    bunches = sems.shape[0]
    bunch = heads // bunches
    copies = []
    for index in range(bunches):
        cols = slice(index * bunch * LANES, (index + 1) * bunch * LANES)
        copies.append([])
        for at, (source, target) in enumerate(
            (
                (dout_hbm.at[:, cols], dout_ref),
                (omem_hbm.at[:, cols], omem_ref),
                (local_hbm.at[:, cols], local_ref),
                (q_hbm.at[:, cols], q_ref),
                (k_hbm.at[mine, cols], k_ref),
                (v_hbm.at[mine, cols], v_ref),
            )
        ):
            copy = pltpu.make_async_copy(source, target.at[:, cols], sems.at[index, at])
            copy.start()
            copies[index].append(copy)

    lane = lax.broadcasted_iota(jnp.int32, (1, LANES), 1)
    ids = ids_ref[...]
    bias_rows = chunks * qblocks
    ext_ref[...] = jnp.zeros_like(ext_ref)
    for chunk in range(chunks):
        hits = []
        for side in range(2):
            shard = chunk * heads + 2 * (lane // 16) + (core + side) % 2
            wanted = jnp.broadcast_to(16 * shard + lane % 16, (qblocks, LANES))
            hit = jnp.zeros((qblocks, LANES), jnp.float32)
            for name in range(names):
                hit = jnp.where(ids[:, name : name + 1] == wanted, 1.0, hit)
            hits.append(hit)
        ext_ref[chunk * qblocks : (chunk + 1) * qblocks, :] = hits[0] + 2.0 * hits[1]

    ones = jnp.ones((8, LANES), jnp.float32)
    wide_ones = jnp.ones((16, 2 * LANES), jnp.bfloat16)
    gate_rows[...] = jnp.zeros_like(gate_rows)
    at = 2 * half_shard
    late = tokens - early
    sent = []
    for head in range(heads):
        if head % bunch == 0:
            for copy in copies[head // bunch]:
                copy.wait()
        cols = slice(head * LANES, (head + 1) * LANES)
        sig = jax.nn.sigmoid(jnp.full((8, LANES), gate_ref[head], jnp.float32))[:1]
        d_out = dout_ref[:, cols].astype(jnp.float32)
        o_mem = omem_ref[:, cols].astype(jnp.float32)
        d_mem = (d_out * sig).astype(jnp.bfloat16)
        differ = o_mem - local_ref[:, cols].astype(jnp.float32)
        gate_rows[head : head + 1, :] = jnp.sum(d_out * differ, 0, keepdims=True)
        product = d_mem.astype(jnp.float32) * o_mem
        upper = product.astype(jnp.bfloat16)
        lower = (product - upper.astype(jnp.float32)).astype(jnp.bfloat16)
        row = lax.dot_general(
            wide_ones,
            jnp.concatenate([upper, lower], axis=1),
            (((1,), (1,)), ((), ())),
            preferred_element_type=jnp.float32,
        )
        delta_ref[head : head + 1, :] = row[:1]
        first_out[head, :half_shard, :] = k_ref[:, cols]
        first_out[head, half_shard:at, :] = v_ref[:, cols]
        first_out[head, at : at + early, :] = q_ref[:early, cols]
        first_out[head, at + early : at + 2 * early, :] = d_mem[:early]
        second_out[head, :late, :] = q_ref[early:, cols]
        second_out[head, late:, :] = d_mem[early:]
        if head % bunch == bunch - 1:
            some = slice(head + 1 - bunch, head + 1)
            body = slice(0, at + 2 * early)
            for index, (source, target) in enumerate(
                ((first_out.at[some, body], first_hbm.at[some, body]), (second_out.at[some], second_hbm.at[some]))
            ):
                copy = pltpu.make_async_copy(source, target, out_sems.at[index, head // bunch])
                copy.start()
                sent.append(copy)
    total = lax.dot_general(
        ones,
        gate_rows[...],
        (((1,), (1,)), ((), ())),
        precision=lax.Precision.HIGHEST,
        preferred_element_type=jnp.float32,
    )
    first = total.astype(jnp.bfloat16).astype(jnp.float32)
    second = (total - first).astype(jnp.bfloat16).astype(jnp.float32)
    third = total - first - second
    addends = first + pltpu.roll(second, heads, 1) + pltpu.roll(third, 2 * heads, 1)
    ext_ref[bias_rows + 1 : bias_rows + 2, :] = addends[:1]
    for head in range(heads):
        ext_ref[bias_rows : bias_rows + 1, :] = delta_ref[head : head + 1, :]
        first_out[head, at + 2 * early :, :] = ext_ref[...].astype(jnp.bfloat16)
    body = slice(at + 2 * early, first_out.shape[1])
    copy = pltpu.make_async_copy(first_out.at[:, body], first_hbm.at[:, body], out_sems.at[0, bunches])
    copy.start()
    sent.append(copy)
    for copy in sent:
        copy.wait()


def assemble(in_ref, out_ref):
    part = out_ref.shape[1] // in_ref.shape[0]
    for source in range(in_ref.shape[0]):
        rows = slice(source * part, (source + 1) * part)
        out_ref[0, rows, :] = in_ref[source, :part, :]
        out_ref[1, rows, :] = in_ref[source, part : 2 * part, :]


def attend(begin, count, q_at, ext_at, qblocks, width, tile, final, own_ref, mate_ref, q_ref, ext_ref, *refs):
    if final:
        before_ref, out_ref, mark, minus, qx, dx, scores, high, total, acc, stage, sems = refs
        early_copy = pltpu.make_async_copy(before_ref, out_ref.at[:, :begin, :], sems.at[0])
        early_copy.start()
    else:
        out_ref, gate_ref, mark, minus, qx, dx, scores, high, total, acc, delta = refs
    sources = q_ref.shape[0]
    units = qx.shape[1] // LANES - 1
    sides = (own_ref, mate_ref)
    steps_side = own_ref.shape[1] // width
    rows_unit = mark.shape[0]
    scale = 1.0 / math.sqrt(LANES)
    exponent = scale * math.log2(math.e)
    chunks = units // 2
    bias_rows = chunks * qblocks

    lane = lax.broadcasted_iota(jnp.int32, (BLK, LANES), 1)
    for block in range(LANES):
        mark[block * BLK : (block + 1) * BLK, :] = jnp.where(lane == block, 1.0, 0.0).astype(jnp.bfloat16)
    wide_lane = lax.broadcasted_iota(jnp.int32, (LANES, LANES), 1)
    for block in range(width // LANES):
        minus[block * LANES : (block + 1) * LANES, :] = jnp.where(wide_lane == 0, -1.0, 0.0).astype(jnp.bfloat16)

    gate_sum = jnp.zeros((1, LANES), jnp.float32)
    for source in range(sources):
        base = source * count
        qx[base : base + count, :LANES] = q_ref[source, q_at : q_at + count, :]
        dx[base : base + count, :LANES] = q_ref[source, q_at + count : q_at + 2 * count, :]
        extra = ext_ref[source, ext_at:, :].astype(jnp.float32)
        code = extra[:bias_rows]
        second = jnp.where(code > 1.5, 1.0, 0.0)
        first = code - 2.0 * second
        for side, hit in enumerate((first, second)):
            bias = jnp.where(hit > 0.5, 0.0, FAR)
            for chunk in range(chunks):
                lanes = (1 + side * chunks + chunk) * LANES
                for block in range(count // BLK):
                    at = chunk * qblocks + begin // BLK + block
                    row = jnp.broadcast_to(bias[at : at + 1], (BLK, LANES)).astype(jnp.bfloat16)
                    qx[base + block * BLK : base + (block + 1) * BLK, lanes : lanes + LANES] = row
        if not final:
            gate_sum = gate_sum + extra[bias_rows + 1 : bias_rows + 2]
        wide = jnp.broadcast_to(extra[bias_rows : bias_rows + 1], (LANES, LANES)).T
        if final:
            wide = jnp.where(wide_lane == 0, wide, 0.0).astype(jnp.bfloat16)
            dx[base : base + count, LANES:] = wide[begin : begin + count]
        else:
            delta[base : base + count, :] = wide[begin : begin + count]
    if not final:
        gate_ref[...] = jnp.broadcast_to(gate_sum, gate_ref.shape)

    def one_tile(index, carry):
        here = pl.ds(pl.multiple_of(index * tile, tile), tile)
        high[...] = jnp.full_like(high, -3e38)
        for side, ref in enumerate(sides):
            for unit in range(units // 2):

                def score(at, carry, side=side, ref=ref, unit=unit):
                    rows = pl.ds(pl.multiple_of(unit * rows_unit + at * width, width), width)
                    marks = pl.ds(pl.multiple_of(at * width, width), width)
                    lanes = (1 + side * (units // 2) + unit) * LANES
                    left = jnp.concatenate([qx[here, :LANES], qx[here, lanes : lanes + LANES]], axis=1)
                    right = jnp.concatenate([ref[0, rows, :], mark[marks, :]], axis=1)
                    got = lax.dot_general(
                        left, right, (((1,), (1,)), ((), ())), preferred_element_type=jnp.float32
                    )
                    scores[side * steps_side + unit * (rows_unit // width) + at] = got
                    best = high[...]
                    for column in range(width // LANES):
                        best = jnp.maximum(best, got[:, column * LANES : (column + 1) * LANES])
                    high[...] = best
                    return carry

                lax.fori_loop(0, rows_unit // width, score, 0, unroll=4 if final else 2)
        high[...] = jnp.broadcast_to(jnp.max(high[...], 1, keepdims=True) * exponent, high.shape)
        total[...] = jnp.zeros_like(total)
        acc[...] = jnp.zeros_like(acc)
        for side, ref in enumerate(sides):

            def back(at, carry, side=side, ref=ref):
                rows = pl.ds(pl.multiple_of(at * width, width), width)
                if final:
                    left, right = dx[here, :], jnp.concatenate([ref[1, rows, :], minus[...]], axis=1)
                else:
                    left, right = dx[here, :LANES], ref[1, rows, :]
                prod = lax.dot_general(
                    left, right, (((1,), (1,)), ((), ())), preferred_element_type=jnp.float32
                )
                if not final:
                    less = delta[here, :]
                got = scores[side * steps_side + at]
                level = high[...]
                added = total[...]
                pieces = []
                for column in range(width // LANES):
                    cols = slice(column * LANES, (column + 1) * LANES)
                    expo = jnp.exp2(got[:, cols] * exponent - level)
                    added = added + expo
                    moved = prod[:, cols] if final else prod[:, cols] - less
                    pieces.append((expo * moved).astype(jnp.bfloat16))
                total[...] = added
                acc[...] += jnp.dot(
                    jnp.concatenate(pieces, axis=1), ref[0, rows, :], preferred_element_type=jnp.float32
                )
                return carry

            lax.fori_loop(0, steps_side, back, 0, unroll=2)
        weight = scale / jnp.sum(total[...], 1, keepdims=True)
        qx[here, :LANES] = (acc[...] * weight).astype(jnp.bfloat16)
        return carry

    lax.fori_loop(0, qx.shape[0] // tile, one_tile, 0)
    for source in range(sources):
        (stage if final else out_ref)[source] = qx[source * count : (source + 1) * count, :LANES]
    if final:
        late_copy = pltpu.make_async_copy(stage, out_ref.at[:, begin:, :], sems.at[1])
        late_copy.start()
        early_copy.wait()
        late_copy.wait()


def unpack(in_ref, out_ref):
    for head in range(in_ref.shape[0]):
        out_ref[:, head * LANES : (head + 1) * LANES] = in_ref[head]


def local(queries, d_out, o_mem, local_out, mem_keys, mem_values, gate_logit, block_ids):
    shards = lax.axis_size("mem")
    groups = lax.axis_size("grp")
    tokens = queries.shape[1]
    width = queries.shape[2]
    heads = gate_logit.shape[0]
    rows_dev = mem_keys.shape[0]
    qblocks = tokens // BLK
    members = heads
    chunks = shards // heads
    assert width == heads * LANES and shards % heads == 0 and groups % 2 == 0
    assert rows_dev == 16 * BLK and heads * 8 == LANES and tokens == LANES
    half_shard = rows_dev // 2
    units = 2 * chunks
    early = tokens // 2
    late = tokens - early
    extra = -(-(chunks * qblocks + 2) // 16) * 16
    ext_at = 2 * half_shard + 2 * early
    vmem = pl.BlockSpec(memory_space=pltpu.VMEM)
    smem = pl.BlockSpec(memory_space=pltpu.SMEM)
    hbm = pl.BlockSpec(memory_space=pltpu.HBM)
    bf16 = jnp.bfloat16
    small = pltpu.CompilerParams(vmem_limit_bytes=24 << 20)

    core_groups = [
        [(mo * heads + 2 * chip + core) * groups + 2 * go + gp for chip in range(heads // 2) for gp in range(2)]
        for mo in range(chunks)
        for go in range(groups // 2)
        for core in range(2)
    ]
    exchange = functools.partial(
        lax.all_to_all, axis_name=AXES, split_axis=0, concat_axis=0, tiled=True, axis_index_groups=core_groups
    )

    first_shape = (members, ext_at + extra, LANES)
    second_shape = (members, 2 * late, LANES)
    first_out, second_out = pl.pallas_call(
        functools.partial(pack, heads, chunks, early),
        out_shape=(pltpu.HBM(first_shape, bf16), pltpu.HBM(second_shape, bf16)),
        in_specs=[hbm] * 6 + [smem, vmem],
        out_specs=(hbm, hbm),
        scratch_shapes=[pltpu.VMEM((half_shard, width), bf16)] * 2
        + [pltpu.VMEM((tokens, width), bf16)] * 4
        + [
            pltpu.VMEM((extra, LANES), jnp.float32),
            pltpu.VMEM((heads, LANES), jnp.float32),
            pltpu.VMEM((LANES, LANES), jnp.float32),
            pltpu.VMEM(first_shape, bf16),
            pltpu.VMEM(second_shape, bf16),
            pltpu.SemaphoreType.DMA((2, 6)),
            pltpu.SemaphoreType.DMA((2, 3)),
        ],
        compiler_params=pltpu.CompilerParams(vmem_limit_bytes=56 << 20),
        name="pack",
    )(mem_keys, mem_values, queries[0], d_out[0], o_mem[0], local_out[0], gate_logit, block_ids[0])
    first_in = exchange(first_out)
    second_in = exchange(second_out)
    own = pl.pallas_call(
        assemble,
        out_shape=jax.ShapeDtypeStruct((2, members * half_shard, LANES), bf16),
        in_specs=[vmem],
        out_specs=vmem,
        compiler_params=small,
        name="assemble",
    )(first_in)
    if chunks > 1:
        same = [[mo * heads + mi for mo in range(chunks)] for mi in range(heads)]
        own = lax.all_gather(own, "mem", axis_index_groups=same, axis=1, tiled=True)
    mate = lax.ppermute(own, "mem", [(i, i ^ 1) for i in range(shards)])

    rows_all = 2 * own.shape[1]
    step_width = 512

    def attend_some(begin, count, q_at, final, out_shape, out_specs, *args):
        tile = members * count if chunks == 1 else 256
        return pl.pallas_call(
            functools.partial(attend, begin, count, q_at, ext_at, qblocks, step_width, tile, final),
            out_shape=out_shape,
            in_specs=[vmem] * len(args),
            out_specs=out_specs,
            scratch_shapes=[
                pltpu.VMEM((LANES * BLK, LANES), bf16),
                pltpu.VMEM((step_width, LANES), bf16),
                pltpu.VMEM((members * count, (1 + units) * LANES), bf16),
                pltpu.VMEM((members * count, 2 * LANES), bf16),
                pltpu.VMEM((rows_all // step_width, tile, step_width), jnp.float32),
                pltpu.VMEM((tile, LANES), jnp.float32),
                pltpu.VMEM((tile, LANES), jnp.float32),
                pltpu.VMEM((tile, LANES), jnp.float32),
            ]
            + [pltpu.VMEM((members, count, LANES), bf16), pltpu.SemaphoreType.DMA((2,))] * final
            + [pltpu.VMEM((members * count, LANES), jnp.float32)] * (not final),
            compiler_params=pltpu.CompilerParams(vmem_limit_bytes=(40 if chunks == 1 else 44) << 20),
            cost_estimate=pl.CostEstimate(
                flops=2 * members * count * rows_all * LANES * 5,
                bytes_accessed=4 * rows_all * LANES,
                transcendentals=members * count * rows_all,
            ),
            name="attend",
        )(*args)

    part, gate_sum = attend_some(
        0,
        early,
        2 * half_shard,
        False,
        [jax.ShapeDtypeStruct((members, early, LANES), bf16), jax.ShapeDtypeStruct((8, LANES), jnp.float32)],
        [vmem, vmem],
        own,
        mate,
        first_in,
        first_in,
    )
    gate_mate = lax.ppermute(gate_sum, "mem", [(i, i ^ 1) for i in range(shards)])
    grad = attend_some(
        early,
        late,
        0,
        True,
        pltpu.HBM((members, tokens, LANES), bf16),
        hbm,
        own,
        mate,
        second_in,
        first_in,
        part,
    )
    home = exchange(grad)
    d_query = pl.pallas_call(
        unpack,
        out_shape=jax.ShapeDtypeStruct((tokens, width), bf16),
        in_specs=[vmem],
        out_specs=vmem,
        compiler_params=small,
        name="unpack",
    )(home)
    addends = (gate_sum + gate_mate)[0, : 3 * heads]
    gate_total = addends[:heads] + addends[heads : 2 * heads] + addends[2 * heads :]
    if chunks > 1 or groups > 2:
        gate_total = lax.psum(gate_total, AXES) / (2 * members)
    sig = jax.nn.sigmoid(gate_logit)
    d_gate = sig * (1.0 - sig) * gate_total / (shards * groups * tokens * LANES) ** 0.5
    return (d_query[None], d_gate)


def solution(mesh):
    placed = (
        P("grp", "mem", None),
        P("grp", "mem", None),
        P("grp", "mem", None),
        P("grp", "mem", None),
        P("mem", None),
        P("mem", None),
        P(),
        P("grp", "mem", None),
    )
    return jax.shard_map(
        local, mesh=mesh, in_specs=placed, out_specs=(P("grp", "mem", None), P()), check_vma=False
    )
```

```python
import functools
import math

import jax
import jax.numpy as jnp
from jax import lax
from jax.experimental import pallas as pl
from jax.experimental.pallas import tpu as pltpu
from jax.sharding import PartitionSpec as P

BLK = 16
LANES = 128
AXES = ("mem", "grp")
FAR = -1e30


def pack(
    heads,
    chunks,
    early,
    k_hbm,
    v_hbm,
    q_hbm,
    dout_hbm,
    omem_hbm,
    local_hbm,
    gate_ref,
    ids_ref,
    first_hbm,
    second_hbm,
    k_ref,
    v_ref,
    q_ref,
    dout_ref,
    omem_ref,
    local_ref,
    ext_ref,
    delta_ref,
    gate_rows,
    first_out,
    second_out,
    sems,
    out_sems,
):
    tokens = q_ref.shape[0]
    half_shard = k_ref.shape[0]
    qblocks, names = ids_ref.shape
    core = lax.axis_index("mem") % 2
    parity = lax.axis_index("grp") % 2
    mine = pl.ds(pl.multiple_of(parity * half_shard, half_shard), half_shard)
    bunches = sems.shape[0]
    bunch = heads // bunches
    copies = []
    for index in range(bunches):
        cols = slice(index * bunch * LANES, (index + 1) * bunch * LANES)
        copies.append([])
        for at, (source, target) in enumerate(
            (
                (dout_hbm.at[:, cols], dout_ref),
                (omem_hbm.at[:, cols], omem_ref),
                (local_hbm.at[:, cols], local_ref),
                (q_hbm.at[:, cols], q_ref),
                (k_hbm.at[mine, cols], k_ref),
                (v_hbm.at[mine, cols], v_ref),
            )
        ):
            copy = pltpu.make_async_copy(source, target.at[:, cols], sems.at[index, at])
            copy.start()
            copies[index].append(copy)

    lane = lax.broadcasted_iota(jnp.int32, (1, LANES), 1)
    ids = ids_ref[...]
    per = qblocks // 2
    bias_rows = chunks * per
    ext_ref[...] = jnp.zeros_like(ext_ref)
    for chunk in range(chunks):
        hits = []
        for side in range(2):
            shard = chunk * heads + 2 * (lane // 16) + (core + side) % 2
            wanted = jnp.broadcast_to(16 * shard + lane % 16, (qblocks, LANES))
            hit = jnp.zeros((qblocks, LANES), jnp.float32)
            for name in range(names):
                hit = jnp.where(ids[:, name : name + 1] == wanted, 1.0, hit)
            hits.append(hit)
        code = hits[0] + 2.0 * hits[1]
        ext_ref[chunk * per : (chunk + 1) * per, :] = code[:per] + 4.0 * code[per:]

    ones = jnp.ones((8, LANES), jnp.float32)
    wide_ones = jnp.ones((16, 2 * LANES), jnp.bfloat16)
    gate_rows[...] = jnp.zeros_like(gate_rows)
    at = 2 * half_shard
    late = tokens - early
    sent = []
    for head in range(heads):
        if head % bunch == 0:
            for copy in copies[head // bunch]:
                copy.wait()
        cols = slice(head * LANES, (head + 1) * LANES)
        sig = jax.nn.sigmoid(jnp.full((8, LANES), gate_ref[head], jnp.float32))[:1]
        d_out = dout_ref[:, cols].astype(jnp.float32)
        o_mem = omem_ref[:, cols].astype(jnp.float32)
        d_mem = (d_out * sig).astype(jnp.bfloat16)
        differ = o_mem - local_ref[:, cols].astype(jnp.float32)
        gate_rows[head : head + 1, :] = jnp.sum(d_out * differ, 0, keepdims=True)
        product = d_mem.astype(jnp.float32) * o_mem
        upper = product.astype(jnp.bfloat16)
        lower = (product - upper.astype(jnp.float32)).astype(jnp.bfloat16)
        row = lax.dot_general(
            wide_ones,
            jnp.concatenate([upper, lower], axis=1),
            (((1,), (1,)), ((), ())),
            preferred_element_type=jnp.float32,
        )
        delta_ref[head : head + 1, :] = row[:1]
        first_out[head, :half_shard, :] = k_ref[:, cols]
        first_out[head, half_shard:at, :] = v_ref[:, cols]
        first_out[head, at : at + early, :] = q_ref[:early, cols]
        first_out[head, at + early : at + 2 * early, :] = d_mem[:early]
        second_out[head, :late, :] = q_ref[early:, cols]
        second_out[head, late:, :] = d_mem[early:]
        if head % bunch == bunch - 1:
            some = slice(head + 1 - bunch, head + 1)
            copy = pltpu.make_async_copy(second_out.at[some], second_hbm.at[some], out_sems.at[1, head // bunch])
            copy.start()
            sent.append(copy)
    total = lax.dot_general(
        ones,
        gate_rows[...],
        (((1,), (1,)), ((), ())),
        precision=lax.Precision.HIGHEST,
        preferred_element_type=jnp.float32,
    )
    first = total.astype(jnp.bfloat16).astype(jnp.float32)
    second = (total - first).astype(jnp.bfloat16).astype(jnp.float32)
    third = total - first - second
    addends = first + pltpu.roll(second, heads, 1) + pltpu.roll(third, 2 * heads, 1)
    ext_ref[bias_rows + 1 : bias_rows + 2, :] = addends[:1]
    for head in range(heads):
        ext_ref[bias_rows : bias_rows + 1, :] = delta_ref[head : head + 1, :]
        first_out[head, at + 2 * early :, :] = ext_ref[...].astype(jnp.bfloat16)
        if head % 4 == 3:
            some = slice(head - 3, head + 1)
            copy = pltpu.make_async_copy(first_out.at[some], first_hbm.at[some], out_sems.at[0, head // 4])
            copy.start()
            sent.append(copy)
    for copy in sent:
        copy.wait()


def assemble(in_ref, out_ref):
    part = out_ref.shape[1] // in_ref.shape[0]
    for source in range(in_ref.shape[0]):
        rows = slice(source * part, (source + 1) * part)
        out_ref[0, rows, :] = in_ref[source, :part, :]
        out_ref[1, rows, :] = in_ref[source, part : 2 * part, :]


def attend(begin, count, q_at, ext_at, qblocks, width, tile, final, own_ref, mate_ref, q_ref, ext_ref, *refs):
    if final:
        before_ref, out_ref, mark, minus, qx, dx, scores, high, total, acc, stage, sems = refs
        early_copy = pltpu.make_async_copy(before_ref, out_ref.at[:, :begin, :], sems.at[0])
        early_copy.start()
    else:
        out_ref, gate_ref, mark, minus, qx, dx, scores, high, total, acc = refs
    sources = q_ref.shape[0]
    units = qx.shape[1] // LANES - 1
    sides = (own_ref, mate_ref)
    steps_side = own_ref.shape[1] // width
    rows_unit = mark.shape[0]
    scale = 1.0 / math.sqrt(LANES)
    exponent = scale * math.log2(math.e)
    chunks = units // 2
    per = qblocks // 2
    bias_rows = chunks * per

    lane = lax.broadcasted_iota(jnp.int32, (BLK, LANES), 1)
    for block in range(LANES):
        mark[block * BLK : (block + 1) * BLK, :] = jnp.where(lane == block, 1.0, 0.0).astype(jnp.bfloat16)
    wide_lane = lax.broadcasted_iota(jnp.int32, (LANES, LANES), 1)
    for block in range(width // LANES):
        minus[block * LANES : (block + 1) * LANES, :] = jnp.where(wide_lane == 0, -1.0, 0.0).astype(jnp.bfloat16)

    gate_sum = jnp.zeros((1, LANES), jnp.float32)
    for source in range(sources):
        base = source * count
        qx[base : base + count, :LANES] = q_ref[source, q_at : q_at + count, :]
        dx[base : base + count, :LANES] = q_ref[source, q_at + count : q_at + 2 * count, :]
        extra = ext_ref[source, ext_at:, :].astype(jnp.float32)
        code = extra[:bias_rows]
        upper = jnp.floor(code * 0.25)
        code = upper if final else code - 4.0 * upper
        second = jnp.where(code > 1.5, 1.0, 0.0)
        first = code - 2.0 * second
        for side, hit in enumerate((first, second)):
            bias = jnp.where(hit > 0.5, 0.0, FAR)
            for chunk in range(chunks):
                lanes = (1 + side * chunks + chunk) * LANES
                for block in range(count // BLK):
                    at = chunk * per + block
                    row = jnp.broadcast_to(bias[at : at + 1], (BLK, LANES)).astype(jnp.bfloat16)
                    qx[base + block * BLK : base + (block + 1) * BLK, lanes : lanes + LANES] = row
        if not final:
            gate_sum = gate_sum + extra[bias_rows + 1 : bias_rows + 2]
        wide = jnp.broadcast_to(extra[bias_rows : bias_rows + 1], (LANES, LANES)).T
        wide = jnp.where(wide_lane == 0, wide, 0.0).astype(jnp.bfloat16)
        dx[base : base + count, LANES:] = wide[begin : begin + count]
    if not final:
        gate_ref[...] = jnp.broadcast_to(gate_sum, gate_ref.shape)

    def one_tile(index, carry):
        here = pl.ds(pl.multiple_of(index * tile, tile), tile)
        high[...] = jnp.full_like(high, -3e38)
        for side, ref in enumerate(sides):
            for unit in range(units // 2):

                def score(at, carry, side=side, ref=ref, unit=unit):
                    rows = pl.ds(pl.multiple_of(unit * rows_unit + at * width, width), width)
                    marks = pl.ds(pl.multiple_of(at * width, width), width)
                    lanes = (1 + side * (units // 2) + unit) * LANES
                    left = jnp.concatenate([qx[here, :LANES], qx[here, lanes : lanes + LANES]], axis=1)
                    right = jnp.concatenate([ref[0, rows, :], mark[marks, :]], axis=1)
                    got = lax.dot_general(
                        left, right, (((1,), (1,)), ((), ())), preferred_element_type=jnp.float32
                    )
                    scores[side * steps_side + unit * (rows_unit // width) + at] = got
                    best = high[...]
                    for column in range(width // LANES):
                        best = jnp.maximum(best, got[:, column * LANES : (column + 1) * LANES])
                    high[...] = best
                    return carry

                lax.fori_loop(0, rows_unit // width, score, 0, unroll=True)
        high[...] = jnp.broadcast_to(jnp.max(high[...], 1, keepdims=True) * exponent, high.shape)
        total[...] = jnp.zeros_like(total)
        acc[...] = jnp.zeros_like(acc)
        for side, ref in enumerate(sides):

            def back(at, carry, side=side, ref=ref):
                rows = pl.ds(pl.multiple_of(at * width, width), width)
                prod = lax.dot_general(
                    dx[here, :],
                    jnp.concatenate([ref[1, rows, :], minus[...]], axis=1),
                    (((1,), (1,)), ((), ())),
                    preferred_element_type=jnp.float32,
                )
                got = scores[side * steps_side + at]
                level = high[...]
                added = total[...]
                pieces = []
                for column in range(width // LANES):
                    cols = slice(column * LANES, (column + 1) * LANES)
                    expo = jnp.exp2(got[:, cols] * exponent - level)
                    added = added + expo
                    pieces.append((expo * prod[:, cols]).astype(jnp.bfloat16))
                total[...] = added
                acc[...] += jnp.dot(
                    jnp.concatenate(pieces, axis=1), ref[0, rows, :], preferred_element_type=jnp.float32
                )
                return carry

            lax.fori_loop(0, steps_side, back, 0, unroll=2 if final else 1)
        weight = scale / jnp.sum(total[...], 1, keepdims=True)
        qx[here, :LANES] = (acc[...] * weight).astype(jnp.bfloat16)
        return carry

    lax.fori_loop(0, qx.shape[0] // tile, one_tile, 0)
    for source in range(sources):
        (stage if final else out_ref)[source] = qx[source * count : (source + 1) * count, :LANES]
    if final:
        copies = [early_copy]
        for part in range(4):
            some = slice(part * sources // 4, (part + 1) * sources // 4)
            copy = pltpu.make_async_copy(stage.at[some], out_ref.at[some, begin:, :], sems.at[1 + part])
            copy.start()
            copies.append(copy)
        for copy in copies:
            copy.wait()


def unpack(in_ref, out_ref):
    for head in range(in_ref.shape[0]):
        out_ref[:, head * LANES : (head + 1) * LANES] = in_ref[head]


def local(queries, d_out, o_mem, local_out, mem_keys, mem_values, gate_logit, block_ids):
    shards = lax.axis_size("mem")
    groups = lax.axis_size("grp")
    tokens = queries.shape[1]
    width = queries.shape[2]
    heads = gate_logit.shape[0]
    rows_dev = mem_keys.shape[0]
    qblocks = tokens // BLK
    members = heads
    chunks = shards // heads
    assert width == heads * LANES and shards % heads == 0 and groups % 2 == 0
    assert rows_dev == 16 * BLK and heads * 8 == LANES and tokens == LANES
    half_shard = rows_dev // 2
    units = 2 * chunks
    early = tokens // 2
    late = tokens - early
    extra = -(-(chunks * (qblocks // 2) + 2) // 8) * 8
    ext_at = 2 * half_shard + 2 * early
    vmem = pl.BlockSpec(memory_space=pltpu.VMEM)
    smem = pl.BlockSpec(memory_space=pltpu.SMEM)
    hbm = pl.BlockSpec(memory_space=pltpu.HBM)
    bf16 = jnp.bfloat16
    small = pltpu.CompilerParams(vmem_limit_bytes=24 << 20)

    core_groups = [
        [(mo * heads + 2 * chip + core) * groups + 2 * go + gp for chip in range(heads // 2) for gp in range(2)]
        for mo in range(chunks)
        for go in range(groups // 2)
        for core in range(2)
    ]
    exchange = functools.partial(
        lax.all_to_all, axis_name=AXES, split_axis=0, concat_axis=0, tiled=True, axis_index_groups=core_groups
    )

    first_shape = (members, ext_at + extra, LANES)
    second_shape = (members, 2 * late, LANES)
    first_out, second_out = pl.pallas_call(
        functools.partial(pack, heads, chunks, early),
        out_shape=(pltpu.HBM(first_shape, bf16), pltpu.HBM(second_shape, bf16)),
        in_specs=[hbm] * 6 + [smem, vmem],
        out_specs=(hbm, hbm),
        scratch_shapes=[pltpu.VMEM((half_shard, width), bf16)] * 2
        + [pltpu.VMEM((tokens, width), bf16)] * 4
        + [
            pltpu.VMEM((extra, LANES), jnp.float32),
            pltpu.VMEM((heads, LANES), jnp.float32),
            pltpu.VMEM((LANES, LANES), jnp.float32),
            pltpu.VMEM(first_shape, bf16),
            pltpu.VMEM(second_shape, bf16),
            pltpu.SemaphoreType.DMA((2, 6)),
            pltpu.SemaphoreType.DMA((2, heads // 4)),
        ],
        compiler_params=pltpu.CompilerParams(vmem_limit_bytes=56 << 20),
        name="pack",
    )(mem_keys, mem_values, queries[0], d_out[0], o_mem[0], local_out[0], gate_logit, block_ids[0])
    first_in = exchange(first_out)
    second_in = exchange(second_out)
    own = pl.pallas_call(
        assemble,
        out_shape=jax.ShapeDtypeStruct((2, members * half_shard, LANES), bf16),
        in_specs=[vmem],
        out_specs=vmem,
        compiler_params=small,
        name="assemble",
    )(first_in)
    if chunks > 1:
        same = [[mo * heads + mi for mo in range(chunks)] for mi in range(heads)]
        own = lax.all_gather(own, "mem", axis_index_groups=same, axis=1, tiled=True)
    mate = lax.ppermute(own, "mem", [(i, i ^ 1) for i in range(shards)])

    rows_all = 2 * own.shape[1]
    step_width = 512

    def attend_some(begin, count, q_at, final, out_shape, out_specs, *args):
        tile = members * count if chunks == 1 else 256
        return pl.pallas_call(
            functools.partial(attend, begin, count, q_at, ext_at, qblocks, step_width, tile, final),
            out_shape=out_shape,
            in_specs=[vmem] * len(args),
            out_specs=out_specs,
            scratch_shapes=[
                pltpu.VMEM((LANES * BLK, LANES), bf16),
                pltpu.VMEM((step_width, LANES), bf16),
                pltpu.VMEM((members * count, (1 + units) * LANES), bf16),
                pltpu.VMEM((members * count, 2 * LANES), bf16),
                pltpu.VMEM((rows_all // step_width, tile, step_width), jnp.float32),
                pltpu.VMEM((tile, LANES), jnp.float32),
                pltpu.VMEM((tile, LANES), jnp.float32),
                pltpu.VMEM((tile, LANES), jnp.float32),
            ]
            + [pltpu.VMEM((members, count, LANES), bf16), pltpu.SemaphoreType.DMA((5,))] * final,
            compiler_params=pltpu.CompilerParams(vmem_limit_bytes=(40 if chunks == 1 else 44) << 20),
            cost_estimate=pl.CostEstimate(
                flops=2 * members * count * rows_all * LANES * 5,
                bytes_accessed=4 * rows_all * LANES,
                transcendentals=members * count * rows_all,
            ),
            name="attend",
        )(*args)

    part, gate_sum = attend_some(
        0,
        early,
        2 * half_shard,
        False,
        [jax.ShapeDtypeStruct((members, early, LANES), bf16), jax.ShapeDtypeStruct((8, LANES), jnp.float32)],
        [vmem, vmem],
        own,
        mate,
        first_in,
        first_in,
    )
    gate_mate = lax.ppermute(gate_sum, "mem", [(i, i ^ 1) for i in range(shards)])
    grad = attend_some(
        early,
        late,
        0,
        True,
        pltpu.HBM((members, tokens, LANES), bf16),
        hbm,
        own,
        mate,
        second_in,
        first_in,
        part,
    )
    home = exchange(grad)
    d_query = pl.pallas_call(
        unpack,
        out_shape=jax.ShapeDtypeStruct((tokens, width), bf16),
        in_specs=[vmem],
        out_specs=vmem,
        compiler_params=small,
        name="unpack",
    )(home)
    addends = (gate_sum + gate_mate)[0, : 3 * heads]
    gate_total = addends[:heads] + addends[heads : 2 * heads] + addends[2 * heads :]
    if chunks > 1 or groups > 2:
        gate_total = lax.psum(gate_total, AXES) / (2 * members)
    sig = jax.nn.sigmoid(gate_logit)
    d_gate = sig * (1.0 - sig) * gate_total / (shards * groups * tokens * LANES) ** 0.5
    return (d_query[None], d_gate)


def solution(mesh):
    placed = (
        P("grp", "mem", None),
        P("grp", "mem", None),
        P("grp", "mem", None),
        P("grp", "mem", None),
        P("mem", None),
        P("mem", None),
        P(),
        P("grp", "mem", None),
    )
    return jax.shard_map(
        local, mesh=mesh, in_specs=placed, out_specs=(P("grp", "mem", None), P()), check_vma=False
    )
```

```python
import functools
import math

import jax
import jax.numpy as jnp
from jax import lax
from jax.experimental import pallas as pl
from jax.experimental.pallas import tpu as pltpu
from jax.sharding import PartitionSpec as P

BLK = 16
LANES = 128
AXES = ("mem", "grp")
FAR = -1e30


def pack(
    heads,
    chunks,
    early,
    k_hbm,
    v_hbm,
    q_hbm,
    dout_hbm,
    omem_hbm,
    local_hbm,
    gate_ref,
    ids_ref,
    first_out,
    second_hbm,
    k_ref,
    v_ref,
    q_ref,
    dout_ref,
    omem_ref,
    local_ref,
    ext_ref,
    delta_ref,
    gate_rows,
    second_out,
    sems,
    out_sems,
):
    tokens = q_ref.shape[0]
    half_shard = k_ref.shape[0]
    qblocks, names = ids_ref.shape
    core = lax.axis_index("mem") % 2
    parity = lax.axis_index("grp") % 2
    mine = pl.ds(pl.multiple_of(parity * half_shard, half_shard), half_shard)
    bunches = sems.shape[0]
    bunch = heads // bunches
    copies = []
    for index in range(bunches):
        cols = slice(index * bunch * LANES, (index + 1) * bunch * LANES)
        copies.append([])
        for at, (source, target) in enumerate(
            (
                (dout_hbm.at[:, cols], dout_ref),
                (omem_hbm.at[:, cols], omem_ref),
                (local_hbm.at[:, cols], local_ref),
                (q_hbm.at[:, cols], q_ref),
                (k_hbm.at[mine, cols], k_ref),
                (v_hbm.at[mine, cols], v_ref),
            )
        ):
            copy = pltpu.make_async_copy(source, target.at[:, cols], sems.at[index, at])
            copy.start()
            copies[index].append(copy)

    lane = lax.broadcasted_iota(jnp.int32, (1, LANES), 1)
    ids = ids_ref[...]
    per = qblocks // 2
    bias_rows = chunks * per
    ext_ref[...] = jnp.zeros_like(ext_ref)
    for chunk in range(chunks):
        hits = []
        for side in range(2):
            shard = chunk * heads + 2 * (lane // 16) + (core + side) % 2
            wanted = jnp.broadcast_to(16 * shard + lane % 16, (qblocks, LANES))
            hit = jnp.zeros((qblocks, LANES), jnp.float32)
            for name in range(names):
                hit = jnp.where(ids[:, name : name + 1] == wanted, 1.0, hit)
            hits.append(hit)
        code = hits[0] + 2.0 * hits[1]
        ext_ref[chunk * per : (chunk + 1) * per, :] = code[:per] + 4.0 * code[per:]

    ones = jnp.ones((8, LANES), jnp.float32)
    wide_ones = jnp.ones((16, 2 * LANES), jnp.bfloat16)
    gate_rows[...] = jnp.zeros_like(gate_rows)
    at = 2 * half_shard
    late = tokens - early
    sent = []
    for head in range(heads):
        if head % bunch == 0:
            for copy in copies[head // bunch]:
                copy.wait()
        cols = slice(head * LANES, (head + 1) * LANES)
        sig = jax.nn.sigmoid(jnp.full((8, LANES), gate_ref[head], jnp.float32))[:1]
        d_out = dout_ref[:, cols].astype(jnp.float32)
        o_mem = omem_ref[:, cols].astype(jnp.float32)
        d_mem = (d_out * sig).astype(jnp.bfloat16)
        differ = o_mem - local_ref[:, cols].astype(jnp.float32)
        gate_rows[head : head + 1, :] = jnp.sum(d_out * differ, 0, keepdims=True)
        product = d_mem.astype(jnp.float32) * o_mem
        upper = product.astype(jnp.bfloat16)
        lower = (product - upper.astype(jnp.float32)).astype(jnp.bfloat16)
        row = lax.dot_general(
            wide_ones,
            jnp.concatenate([upper, lower], axis=1),
            (((1,), (1,)), ((), ())),
            preferred_element_type=jnp.float32,
        )
        delta_ref[head : head + 1, :] = row[:1]
        first_out[head, :half_shard, :] = k_ref[:, cols]
        first_out[head, half_shard:at, :] = v_ref[:, cols]
        first_out[head, at : at + early, :] = q_ref[:early, cols]
        first_out[head, at + early : at + 2 * early, :] = d_mem[:early]
        second_out[head, :late, :] = q_ref[early:, cols]
        second_out[head, late:, :] = d_mem[early:]
        if head % bunch == bunch - 1:
            some = slice(head + 1 - bunch, head + 1)
            copy = pltpu.make_async_copy(second_out.at[some], second_hbm.at[some], out_sems.at[1, head // bunch])
            copy.start()
            sent.append(copy)
    total = lax.dot_general(
        ones,
        gate_rows[...],
        (((1,), (1,)), ((), ())),
        precision=lax.Precision.HIGHEST,
        preferred_element_type=jnp.float32,
    )
    first = total.astype(jnp.bfloat16).astype(jnp.float32)
    second = (total - first).astype(jnp.bfloat16).astype(jnp.float32)
    third = total - first - second
    addends = first + pltpu.roll(second, heads, 1) + pltpu.roll(third, 2 * heads, 1)
    ext_ref[bias_rows + 1 : bias_rows + 2, :] = addends[:1]
    for head in range(heads):
        ext_ref[bias_rows : bias_rows + 1, :] = delta_ref[head : head + 1, :]
        first_out[head, at + 2 * early :, :] = ext_ref[...].astype(jnp.bfloat16)
    for copy in sent:
        copy.wait()


def assemble(in_ref, out_ref):
    part = out_ref.shape[1] // in_ref.shape[0]
    for source in range(in_ref.shape[0]):
        rows = slice(source * part, (source + 1) * part)
        out_ref[0, rows, :] = in_ref[source, :part, :]
        out_ref[1, rows, :] = in_ref[source, part : 2 * part, :]


def attend(begin, count, q_at, ext_at, qblocks, width, tile, final, own_ref, mate_ref, q_ref, ext_ref, *refs):
    if final:
        before_ref, bias_ref, delta_ref, out_ref, mark, minus, qx, dx, scores, high, total, acc, stage, sems = refs
        early_copy = pltpu.make_async_copy(before_ref, out_ref.at[:, :begin, :], sems.at[0])
        early_copy.start()
    else:
        out_ref, gate_ref, bias_next, delta_next, mark, minus, qx, dx, scores, high, total, acc = refs
        bias_ref, delta_ref = qx.at[:, LANES:], dx.at[:, LANES:]
    sources = q_ref.shape[0]
    units = bias_ref.shape[1] // LANES
    sides = (own_ref, mate_ref)
    steps_side = own_ref.shape[1] // width
    rows_unit = mark.shape[0]
    scale = 1.0 / math.sqrt(LANES)
    exponent = scale * math.log2(math.e)
    chunks = units // 2
    per = qblocks // 2
    bias_rows = chunks * per

    lane = lax.broadcasted_iota(jnp.int32, (BLK, LANES), 1)
    for block in range(LANES):
        mark[block * BLK : (block + 1) * BLK, :] = jnp.where(lane == block, 1.0, 0.0).astype(jnp.bfloat16)
    wide_lane = lax.broadcasted_iota(jnp.int32, (LANES, LANES), 1)
    for block in range(width // LANES):
        minus[block * LANES : (block + 1) * LANES, :] = jnp.where(wide_lane == 0, -1.0, 0.0).astype(jnp.bfloat16)

    gate_sum = jnp.zeros((1, LANES), jnp.float32)
    for source in range(sources):
        base = source * count
        qx[base : base + count, :LANES] = q_ref[source, q_at : q_at + count, :]
        dx[base : base + count, :LANES] = q_ref[source, q_at + count : q_at + 2 * count, :]
        if final:
            continue
        extra = ext_ref[source, ext_at:, :].astype(jnp.float32)
        gate_sum = gate_sum + extra[bias_rows + 1 : bias_rows + 2]
        wide = jnp.broadcast_to(extra[bias_rows : bias_rows + 1], (LANES, LANES)).T
        wide = jnp.where(wide_lane == 0, wide, 0.0).astype(jnp.bfloat16)
        dx[base : base + count, LANES:] = wide[:count]
        delta_next[base : base + count, :] = wide[count:]
        upper = jnp.floor(extra[:bias_rows] * 0.25)
        for late, code in enumerate((extra[:bias_rows] - 4.0 * upper, upper)):
            second = jnp.where(code > 1.5, 1.0, 0.0)
            first = code - 2.0 * second
            for side, hit in enumerate((first, second)):
                bias = jnp.where(hit > 0.5, 0.0, FAR)
                for chunk in range(chunks):
                    at_lane = (side * chunks + chunk) * LANES
                    for block in range(per):
                        at = chunk * per + block
                        row = jnp.broadcast_to(bias[at : at + 1], (BLK, LANES)).astype(jnp.bfloat16)
                        rows = slice(base + block * BLK, base + (block + 1) * BLK)
                        if late:
                            bias_next[rows, at_lane : at_lane + LANES] = row
                        else:
                            qx[rows, LANES + at_lane : 2 * LANES + at_lane] = row
    if not final:
        gate_ref[...] = jnp.broadcast_to(gate_sum, gate_ref.shape)

    def one_tile(index, carry):
        here = pl.ds(pl.multiple_of(index * tile, tile), tile)
        high[...] = jnp.full_like(high, -3e38)
        for side, ref in enumerate(sides):
            for unit in range(units // 2):

                def score(at, carry, side=side, ref=ref, unit=unit):
                    rows = pl.ds(pl.multiple_of(unit * rows_unit + at * width, width), width)
                    marks = pl.ds(pl.multiple_of(at * width, width), width)
                    lanes = (side * (units // 2) + unit) * LANES
                    left = jnp.concatenate([qx[here, :LANES], bias_ref[here, lanes : lanes + LANES]], axis=1)
                    right = jnp.concatenate([ref[0, rows, :], mark[marks, :]], axis=1)
                    got = lax.dot_general(
                        left, right, (((1,), (1,)), ((), ())), preferred_element_type=jnp.float32
                    )
                    scores[side * steps_side + unit * (rows_unit // width) + at] = got
                    best = high[...]
                    for column in range(width // LANES):
                        best = jnp.maximum(best, got[:, column * LANES : (column + 1) * LANES])
                    high[...] = best
                    return carry

                lax.fori_loop(0, rows_unit // width, score, 0, unroll=True)
        high[...] = jnp.broadcast_to(jnp.max(high[...], 1, keepdims=True) * exponent, high.shape)
        total[...] = jnp.zeros_like(total)
        acc[...] = jnp.zeros_like(acc)
        for side, ref in enumerate(sides):

            def back(at, carry, side=side, ref=ref):
                rows = pl.ds(pl.multiple_of(at * width, width), width)
                prod = lax.dot_general(
                    jnp.concatenate([dx[here, :LANES], delta_ref[here, :]], axis=1),
                    jnp.concatenate([ref[1, rows, :], minus[...]], axis=1),
                    (((1,), (1,)), ((), ())),
                    preferred_element_type=jnp.float32,
                )
                got = scores[side * steps_side + at]
                level = high[...]
                added = total[...]
                pieces = []
                for column in range(width // LANES):
                    cols = slice(column * LANES, (column + 1) * LANES)
                    expo = jnp.exp2(got[:, cols] * exponent - level)
                    added = added + expo
                    pieces.append((expo * prod[:, cols]).astype(jnp.bfloat16))
                total[...] = added
                acc[...] += jnp.dot(
                    jnp.concatenate(pieces, axis=1), ref[0, rows, :], preferred_element_type=jnp.float32
                )
                return carry

            lax.fori_loop(0, steps_side, back, 0, unroll=2 if final else 2)
        weight = scale / jnp.sum(total[...], 1, keepdims=True)
        qx[here, :LANES] = (acc[...] * weight).astype(jnp.bfloat16)
        return carry

    lax.fori_loop(0, qx.shape[0] // tile, one_tile, 0)
    for source in range(sources):
        (stage if final else out_ref)[source] = qx[source * count : (source + 1) * count, :LANES]
    if final:
        copies = [early_copy]
        for part in range(4):
            some = slice(part * sources // 4, (part + 1) * sources // 4)
            copy = pltpu.make_async_copy(stage.at[some], out_ref.at[some, begin:, :], sems.at[1 + part])
            copy.start()
            copies.append(copy)
        for copy in copies:
            copy.wait()


def unpack(in_ref, out_ref):
    for head in range(in_ref.shape[0]):
        out_ref[:, head * LANES : (head + 1) * LANES] = in_ref[head]


def local(queries, d_out, o_mem, local_out, mem_keys, mem_values, gate_logit, block_ids):
    shards = lax.axis_size("mem")
    groups = lax.axis_size("grp")
    tokens = queries.shape[1]
    width = queries.shape[2]
    heads = gate_logit.shape[0]
    rows_dev = mem_keys.shape[0]
    qblocks = tokens // BLK
    members = heads
    chunks = shards // heads
    assert width == heads * LANES and shards % heads == 0 and groups % 2 == 0
    assert qblocks == 8 and rows_dev == 16 * BLK and heads * 8 == LANES and tokens == LANES
    half_shard = rows_dev // 2
    units = 2 * chunks
    early = tokens // 2
    late = tokens - early
    extra = -(-(chunks * (qblocks // 2) + 2) // 8) * 8
    ext_at = 2 * half_shard + 2 * early
    vmem = pl.BlockSpec(memory_space=pltpu.VMEM)
    smem = pl.BlockSpec(memory_space=pltpu.SMEM)
    hbm = pl.BlockSpec(memory_space=pltpu.HBM)
    bf16 = jnp.bfloat16
    small = pltpu.CompilerParams(vmem_limit_bytes=24 << 20)

    core_groups = [
        [(mo * heads + 2 * chip + core) * groups + 2 * go + gp for chip in range(heads // 2) for gp in range(2)]
        for mo in range(chunks)
        for go in range(groups // 2)
        for core in range(2)
    ]
    exchange = functools.partial(
        lax.all_to_all, axis_name=AXES, split_axis=0, concat_axis=0, tiled=True, axis_index_groups=core_groups
    )

    first_shape = (members, ext_at + extra, LANES)
    second_shape = (members, 2 * late, LANES)
    first_out, second_out = pl.pallas_call(
        functools.partial(pack, heads, chunks, early),
        out_shape=(pltpu.VMEM(first_shape, bf16), pltpu.HBM(second_shape, bf16)),
        in_specs=[hbm] * 6 + [smem, vmem],
        out_specs=(vmem, hbm),
        scratch_shapes=[pltpu.VMEM((half_shard, width), bf16)] * 2
        + [pltpu.VMEM((tokens, width), bf16)] * 4
        + [
            pltpu.VMEM((extra, LANES), jnp.float32),
            pltpu.VMEM((heads, LANES), jnp.float32),
            pltpu.VMEM((LANES, LANES), jnp.float32),
            pltpu.VMEM(second_shape, bf16),
            pltpu.SemaphoreType.DMA((2, 6)),
            pltpu.SemaphoreType.DMA((2, 2)),
        ],
        compiler_params=pltpu.CompilerParams(vmem_limit_bytes=56 << 20),
        name="pack",
    )(mem_keys, mem_values, queries[0], d_out[0], o_mem[0], local_out[0], gate_logit, block_ids[0])
    first_in = exchange(first_out)
    second_in = exchange(second_out)
    own = pl.pallas_call(
        assemble,
        out_shape=jax.ShapeDtypeStruct((2, members * half_shard, LANES), bf16),
        in_specs=[vmem],
        out_specs=vmem,
        compiler_params=small,
        name="assemble",
    )(first_in)
    if chunks > 1:
        same = [[mo * heads + mi for mo in range(chunks)] for mi in range(heads)]
        own = lax.all_gather(own, "mem", axis_index_groups=same, axis=1, tiled=True)
    mate = lax.ppermute(own, "mem", [(i, i ^ 1) for i in range(shards)])

    rows_all = 2 * own.shape[1]
    step_width = 512

    def attend_some(begin, count, q_at, final, out_shape, out_specs, *args):
        tile = members * count if chunks == 1 else 256
        return pl.pallas_call(
            functools.partial(attend, begin, count, q_at, ext_at, qblocks, step_width, tile, final),
            out_shape=out_shape,
            in_specs=[vmem] * len(args),
            out_specs=out_specs,
            scratch_shapes=[
                pltpu.VMEM((LANES * BLK, LANES), bf16),
                pltpu.VMEM((step_width, LANES), bf16),
                pltpu.VMEM((members * count, (1 if final else 1 + units) * LANES), bf16),
                pltpu.VMEM((members * count, (1 if final else 2) * LANES), bf16),
                pltpu.VMEM((rows_all // step_width, tile, step_width), jnp.float32),
                pltpu.VMEM((tile, LANES), jnp.float32),
                pltpu.VMEM((tile, LANES), jnp.float32),
                pltpu.VMEM((tile, LANES), jnp.float32),
            ]
            + [pltpu.VMEM((members, count, LANES), bf16), pltpu.SemaphoreType.DMA((5,))] * final,
            compiler_params=pltpu.CompilerParams(vmem_limit_bytes=(40 if chunks == 1 else 44) << 20),
            cost_estimate=pl.CostEstimate(
                flops=2 * members * count * rows_all * LANES * 5,
                bytes_accessed=4 * rows_all * LANES,
                transcendentals=members * count * rows_all,
            ),
            name="attend",
        )(*args)

    part, gate_sum, bias_late, delta_late = attend_some(
        0,
        early,
        2 * half_shard,
        False,
        [
            jax.ShapeDtypeStruct((members, early, LANES), bf16),
            jax.ShapeDtypeStruct((8, LANES), jnp.float32),
            jax.ShapeDtypeStruct((members * late, units * LANES), bf16),
            jax.ShapeDtypeStruct((members * late, LANES), bf16),
        ],
        [vmem] * 4,
        own,
        mate,
        first_in,
        first_in,
    )
    gate_mate = lax.ppermute(gate_sum, "mem", [(i, i ^ 1) for i in range(shards)])
    grad = attend_some(
        early,
        late,
        0,
        True,
        pltpu.HBM((members, tokens, LANES), bf16),
        hbm,
        own,
        mate,
        second_in,
        first_in,
        part,
        bias_late,
        delta_late,
    )
    home = exchange(grad)
    d_query = pl.pallas_call(
        unpack,
        out_shape=jax.ShapeDtypeStruct((tokens, width), bf16),
        in_specs=[vmem],
        out_specs=vmem,
        compiler_params=small,
        name="unpack",
    )(home)
    addends = (gate_sum + gate_mate)[0, : 3 * heads]
    gate_total = addends[:heads] + addends[heads : 2 * heads] + addends[2 * heads :]
    if chunks > 1 or groups > 2:
        gate_total = lax.psum(gate_total, AXES) / (2 * members)
    sig = jax.nn.sigmoid(gate_logit)
    d_gate = sig * (1.0 - sig) * gate_total / (shards * groups * tokens * LANES) ** 0.5
    return (d_query[None], d_gate)


def solution(mesh):
    placed = (
        P("grp", "mem", None),
        P("grp", "mem", None),
        P("grp", "mem", None),
        P("grp", "mem", None),
        P("mem", None),
        P("mem", None),
        P(),
        P("grp", "mem", None),
    )
    return jax.shard_map(
        local, mesh=mesh, in_specs=placed, out_specs=(P("grp", "mem", None), P()), check_vma=False
    )
```

```python
import functools
import math

import jax
import jax.numpy as jnp
from jax import lax
from jax.experimental import pallas as pl
from jax.experimental.pallas import tpu as pltpu
from jax.sharding import PartitionSpec as P

BLK = 16
LANES = 128
AXES = ("mem", "grp")
FAR = -1e30


def pack(
    heads,
    chunks,
    early,
    k_hbm,
    v_hbm,
    q_hbm,
    dout_hbm,
    omem_hbm,
    local_hbm,
    gate_ref,
    ids_ref,
    first_out,
    second_hbm,
    k_ref,
    v_ref,
    q_ref,
    dout_ref,
    omem_ref,
    local_ref,
    ext_ref,
    delta_ref,
    gate_rows,
    second_out,
    sems,
    out_sems,
):
    tokens = q_ref.shape[0]
    half_shard = k_ref.shape[0]
    qblocks, names = ids_ref.shape
    core = lax.axis_index("mem") % 2
    parity = lax.axis_index("grp") % 2
    mine = pl.ds(pl.multiple_of(parity * half_shard, half_shard), half_shard)
    bunches = sems.shape[0]
    bunch = heads // bunches
    copies = []
    for index in range(bunches):
        cols = slice(index * bunch * LANES, (index + 1) * bunch * LANES)
        copies.append([])
        for at, (source, target) in enumerate(
            (
                (dout_hbm.at[:, cols], dout_ref),
                (omem_hbm.at[:, cols], omem_ref),
                (local_hbm.at[:, cols], local_ref),
                (q_hbm.at[:, cols], q_ref),
                (k_hbm.at[mine, cols], k_ref),
                (v_hbm.at[mine, cols], v_ref),
            )
        ):
            copy = pltpu.make_async_copy(source, target.at[:, cols], sems.at[index, at])
            copy.start()
            copies[index].append(copy)

    lane = lax.broadcasted_iota(jnp.int32, (1, LANES), 1)
    ids = ids_ref[...]
    per = qblocks // 2
    bias_rows = chunks * per
    ext_ref[...] = jnp.zeros_like(ext_ref)
    for chunk in range(chunks):
        hits = []
        for side in range(2):
            shard = chunk * heads + 2 * (lane // 16) + (core + side) % 2
            wanted = jnp.broadcast_to(16 * shard + lane % 16, (qblocks, LANES))
            hit = jnp.zeros((qblocks, LANES), jnp.float32)
            for name in range(names):
                hit = jnp.where(ids[:, name : name + 1] == wanted, 1.0, hit)
            hits.append(hit)
        code = hits[0] + 2.0 * hits[1]
        ext_ref[chunk * per : (chunk + 1) * per, :] = code[:per] + 4.0 * code[per:]

    ones = jnp.ones((8, LANES), jnp.float32)
    wide_ones = jnp.ones((16, 2 * LANES), jnp.bfloat16)
    gate_rows[...] = jnp.zeros_like(gate_rows)
    at = 2 * half_shard
    late = tokens - early
    sent = []
    for head in range(heads):
        if head % bunch == 0:
            for copy in copies[head // bunch]:
                copy.wait()
        cols = slice(head * LANES, (head + 1) * LANES)
        sig = jax.nn.sigmoid(jnp.full((8, LANES), gate_ref[head], jnp.float32))[:1]
        d_out = dout_ref[:, cols].astype(jnp.float32)
        o_mem = omem_ref[:, cols].astype(jnp.float32)
        d_mem = (d_out * sig).astype(jnp.bfloat16)
        differ = o_mem - local_ref[:, cols].astype(jnp.float32)
        gate_rows[head : head + 1, :] = jnp.sum(d_out * differ, 0, keepdims=True)
        product = d_mem.astype(jnp.float32) * o_mem
        upper = product.astype(jnp.bfloat16)
        lower = (product - upper.astype(jnp.float32)).astype(jnp.bfloat16)
        row = lax.dot_general(
            wide_ones,
            jnp.concatenate([upper, lower], axis=1),
            (((1,), (1,)), ((), ())),
            preferred_element_type=jnp.float32,
        )
        delta_ref[head : head + 1, :] = row[:1]
        first_out[head, :half_shard, :] = k_ref[:, cols]
        first_out[head, half_shard:at, :] = v_ref[:, cols]
        first_out[head, at : at + early, :] = q_ref[:early, cols]
        first_out[head, at + early : at + 2 * early, :] = d_mem[:early]
        second_out[head, :late, :] = q_ref[early:, cols]
        second_out[head, late:, :] = d_mem[early:]
        if head % bunch == bunch - 1:
            some = slice(head + 1 - bunch, head + 1)
            copy = pltpu.make_async_copy(second_out.at[some], second_hbm.at[some], out_sems.at[1, head // bunch])
            copy.start()
            sent.append(copy)
    total = lax.dot_general(
        ones,
        gate_rows[...],
        (((1,), (1,)), ((), ())),
        precision=lax.Precision.HIGHEST,
        preferred_element_type=jnp.float32,
    )
    first = total.astype(jnp.bfloat16).astype(jnp.float32)
    second = (total - first).astype(jnp.bfloat16).astype(jnp.float32)
    third = total - first - second
    addends = first + pltpu.roll(second, heads, 1) + pltpu.roll(third, 2 * heads, 1)
    ext_ref[bias_rows + 1 : bias_rows + 2, :] = addends[:1]
    for head in range(heads):
        ext_ref[bias_rows : bias_rows + 1, :] = delta_ref[head : head + 1, :]
        first_out[head, at + 2 * early :, :] = ext_ref[...].astype(jnp.bfloat16)
    for copy in sent:
        copy.wait()


def assemble(in_ref, out_ref):
    part = out_ref.shape[1] // in_ref.shape[0]
    for source in range(in_ref.shape[0]):
        rows = slice(source * part, (source + 1) * part)
        out_ref[0, rows, :] = in_ref[source, :part, :]
        out_ref[1, rows, :] = in_ref[source, part : 2 * part, :]


def attend(begin, count, q_at, ext_at, qblocks, width, tile, final, own_ref, mate_ref, q_ref, ext_ref, *refs):
    if final:
        before_ref, out_ref, mark, minus, qx, dx, scores, high, total, acc, stage, sems = refs
        early_copy = pltpu.make_async_copy(before_ref, out_ref.at[:, :begin, :], sems.at[0])
        early_copy.start()
    else:
        out_ref, gate_ref, mark, minus, qx, dx, scores, high, total, acc = refs
    sources = q_ref.shape[0]
    units = qx.shape[1] // LANES - 1
    sides = (own_ref, mate_ref)
    steps_side = own_ref.shape[1] // width
    rows_unit = mark.shape[0]
    scale = 1.0 / math.sqrt(LANES)
    exponent = scale * math.log2(math.e)
    chunks = units // 2
    per = qblocks // 2
    bias_rows = chunks * per

    lane = lax.broadcasted_iota(jnp.int32, (BLK, LANES), 1)
    for block in range(LANES):
        mark[block * BLK : (block + 1) * BLK, :] = jnp.where(lane == block, 1.0, 0.0).astype(jnp.bfloat16)
    wide_lane = lax.broadcasted_iota(jnp.int32, (LANES, LANES), 1)
    for block in range(width // LANES):
        minus[block * LANES : (block + 1) * LANES, :] = jnp.where(wide_lane == 0, -1.0, 0.0).astype(jnp.bfloat16)

    gate_sum = jnp.zeros((1, LANES), jnp.float32)
    for source in range(sources):
        base = source * count
        qx[base : base + count, :LANES] = q_ref[source, q_at : q_at + count, :]
        dx[base : base + count, :LANES] = q_ref[source, q_at + count : q_at + 2 * count, :]
        extra = ext_ref[source, ext_at:, :].astype(jnp.float32)
        code = extra[:bias_rows]
        upper = jnp.floor(code * 0.25)
        code = upper if final else code - 4.0 * upper
        second = jnp.where(code > 1.5, 1.0, 0.0)
        first = code - 2.0 * second
        for side, hit in enumerate((first, second)):
            bias = jnp.where(hit > 0.5, 0.0, FAR)
            for chunk in range(chunks):
                lanes = (1 + side * chunks + chunk) * LANES
                for block in range(count // BLK):
                    at = chunk * per + block
                    row = jnp.broadcast_to(bias[at : at + 1], (BLK, LANES)).astype(jnp.bfloat16)
                    qx[base + block * BLK : base + (block + 1) * BLK, lanes : lanes + LANES] = row
        if not final:
            gate_sum = gate_sum + extra[bias_rows + 1 : bias_rows + 2]
        wide = jnp.broadcast_to(extra[bias_rows : bias_rows + 1], (LANES, LANES)).T
        wide = jnp.where(wide_lane == 0, wide, 0.0).astype(jnp.bfloat16)
        dx[base : base + count, LANES:] = wide[begin : begin + count]
    if not final:
        gate_ref[...] = jnp.broadcast_to(gate_sum, gate_ref.shape)

    def one_tile(index, carry):
        here = pl.ds(pl.multiple_of(index * tile, tile), tile)
        high[...] = jnp.full_like(high, -3e38)
        for side, ref in enumerate(sides):
            for unit in range(units // 2):

                def score(at, carry, side=side, ref=ref, unit=unit):
                    rows = pl.ds(pl.multiple_of(unit * rows_unit + at * width, width), width)
                    marks = pl.ds(pl.multiple_of(at * width, width), width)
                    lanes = (1 + side * (units // 2) + unit) * LANES
                    left = jnp.concatenate([qx[here, :LANES], qx[here, lanes : lanes + LANES]], axis=1)
                    right = jnp.concatenate([ref[0, rows, :], mark[marks, :]], axis=1)
                    got = lax.dot_general(
                        left, right, (((1,), (1,)), ((), ())), preferred_element_type=jnp.float32
                    )
                    scores[side * steps_side + unit * (rows_unit // width) + at] = got
                    best = high[...]
                    for column in range(width // LANES):
                        best = jnp.maximum(best, got[:, column * LANES : (column + 1) * LANES])
                    high[...] = best
                    return carry

                lax.fori_loop(0, rows_unit // width, score, 0, unroll=True)
        high[...] = jnp.broadcast_to(jnp.max(high[...], 1, keepdims=True) * exponent, high.shape)
        total[...] = jnp.zeros_like(total)
        acc[...] = jnp.zeros_like(acc)
        def back(at, carry):
            for side, ref in enumerate(sides):
                rows = pl.ds(pl.multiple_of(at * width, width), width)
                prod = lax.dot_general(
                    dx[here, :],
                    jnp.concatenate([ref[1, rows, :], minus[...]], axis=1),
                    (((1,), (1,)), ((), ())),
                    preferred_element_type=jnp.float32,
                )
                got = scores[side * steps_side + at]
                level = high[...]
                added = total[...]
                pieces = []
                for column in range(width // LANES):
                    cols = slice(column * LANES, (column + 1) * LANES)
                    expo = jnp.exp2(got[:, cols] * exponent - level)
                    added = added + expo
                    pieces.append((expo * prod[:, cols]).astype(jnp.bfloat16))
                total[...] = added
                acc[...] += jnp.dot(
                    jnp.concatenate(pieces, axis=1), ref[0, rows, :], preferred_element_type=jnp.float32
                )
            return carry

        lax.fori_loop(0, steps_side, back, 0, unroll=1 if final else 2)
        weight = scale / jnp.sum(total[...], 1, keepdims=True)
        qx[here, :LANES] = (acc[...] * weight).astype(jnp.bfloat16)
        return carry

    lax.fori_loop(0, qx.shape[0] // tile, one_tile, 0)
    for source in range(sources):
        (stage if final else out_ref)[source] = qx[source * count : (source + 1) * count, :LANES]
    if final:
        copies = [early_copy]
        for part in range(4):
            some = slice(part * sources // 4, (part + 1) * sources // 4)
            copy = pltpu.make_async_copy(stage.at[some], out_ref.at[some, begin:, :], sems.at[1 + part])
            copy.start()
            copies.append(copy)
        for copy in copies:
            copy.wait()


def unpack(in_ref, out_ref):
    for head in range(in_ref.shape[0]):
        out_ref[:, head * LANES : (head + 1) * LANES] = in_ref[head]


def local(queries, d_out, o_mem, local_out, mem_keys, mem_values, gate_logit, block_ids):
    shards = lax.axis_size("mem")
    groups = lax.axis_size("grp")
    tokens = queries.shape[1]
    width = queries.shape[2]
    heads = gate_logit.shape[0]
    rows_dev = mem_keys.shape[0]
    qblocks = tokens // BLK
    members = heads
    chunks = shards // heads
    assert width == heads * LANES and shards % heads == 0 and groups % 2 == 0
    assert rows_dev == 16 * BLK and heads * 8 == LANES and tokens == LANES
    half_shard = rows_dev // 2
    units = 2 * chunks
    early = tokens // 2
    late = tokens - early
    extra = -(-(chunks * (qblocks // 2) + 2) // 8) * 8
    ext_at = 2 * half_shard + 2 * early
    vmem = pl.BlockSpec(memory_space=pltpu.VMEM)
    smem = pl.BlockSpec(memory_space=pltpu.SMEM)
    hbm = pl.BlockSpec(memory_space=pltpu.HBM)
    bf16 = jnp.bfloat16
    small = pltpu.CompilerParams(vmem_limit_bytes=24 << 20)

    core_groups = [
        [(mo * heads + 2 * chip + core) * groups + 2 * go + gp for chip in range(heads // 2) for gp in range(2)]
        for mo in range(chunks)
        for go in range(groups // 2)
        for core in range(2)
    ]
    exchange = functools.partial(
        lax.all_to_all, axis_name=AXES, split_axis=0, concat_axis=0, tiled=True, axis_index_groups=core_groups
    )

    first_shape = (members, ext_at + extra, LANES)
    second_shape = (members, 2 * late, LANES)
    first_out, second_out = pl.pallas_call(
        functools.partial(pack, heads, chunks, early),
        out_shape=(pltpu.VMEM(first_shape, bf16), pltpu.HBM(second_shape, bf16)),
        in_specs=[hbm] * 6 + [smem, vmem],
        out_specs=(vmem, hbm),
        scratch_shapes=[pltpu.VMEM((half_shard, width), bf16)] * 2
        + [pltpu.VMEM((tokens, width), bf16)] * 4
        + [
            pltpu.VMEM((extra, LANES), jnp.float32),
            pltpu.VMEM((heads, LANES), jnp.float32),
            pltpu.VMEM((LANES, LANES), jnp.float32),
            pltpu.VMEM(second_shape, bf16),
            pltpu.SemaphoreType.DMA((2, 6)),
            pltpu.SemaphoreType.DMA((2, 2)),
        ],
        compiler_params=pltpu.CompilerParams(vmem_limit_bytes=56 << 20),
        name="pack",
    )(mem_keys, mem_values, queries[0], d_out[0], o_mem[0], local_out[0], gate_logit, block_ids[0])
    first_in = exchange(first_out)
    second_in = exchange(second_out)
    own = pl.pallas_call(
        assemble,
        out_shape=jax.ShapeDtypeStruct((2, members * half_shard, LANES), bf16),
        in_specs=[vmem],
        out_specs=vmem,
        compiler_params=small,
        name="assemble",
    )(first_in)
    if chunks > 1:
        same = [[mo * heads + mi for mo in range(chunks)] for mi in range(heads)]
        own = lax.all_gather(own, "mem", axis_index_groups=same, axis=1, tiled=True)
    mate = lax.ppermute(own, "mem", [(i, i ^ 1) for i in range(shards)])

    rows_all = 2 * own.shape[1]
    step_width = 512

    def attend_some(begin, count, q_at, final, out_shape, out_specs, *args):
        tile = members * count if chunks == 1 else 256
        return pl.pallas_call(
            functools.partial(attend, begin, count, q_at, ext_at, qblocks, step_width, tile, final),
            out_shape=out_shape,
            in_specs=[vmem] * len(args),
            out_specs=out_specs,
            scratch_shapes=[
                pltpu.VMEM((LANES * BLK, LANES), bf16),
                pltpu.VMEM((step_width, LANES), bf16),
                pltpu.VMEM((members * count, (1 + units) * LANES), bf16),
                pltpu.VMEM((members * count, 2 * LANES), bf16),
                pltpu.VMEM((rows_all // step_width, tile, step_width), jnp.float32),
                pltpu.VMEM((tile, LANES), jnp.float32),
                pltpu.VMEM((tile, LANES), jnp.float32),
                pltpu.VMEM((tile, LANES), jnp.float32),
            ]
            + [pltpu.VMEM((members, count, LANES), bf16), pltpu.SemaphoreType.DMA((5,))] * final,
            compiler_params=pltpu.CompilerParams(vmem_limit_bytes=(40 if chunks == 1 else 44) << 20),
            cost_estimate=pl.CostEstimate(
                flops=2 * members * count * rows_all * LANES * 5,
                bytes_accessed=4 * rows_all * LANES,
                transcendentals=members * count * rows_all,
            ),
            name="attend",
        )(*args)

    part, gate_sum = attend_some(
        0,
        early,
        2 * half_shard,
        False,
        [jax.ShapeDtypeStruct((members, early, LANES), bf16), jax.ShapeDtypeStruct((8, LANES), jnp.float32)],
        [vmem, vmem],
        own,
        mate,
        first_in,
        first_in,
    )
    gate_mate = lax.ppermute(gate_sum, "mem", [(i, i ^ 1) for i in range(shards)])
    grad = attend_some(
        early,
        late,
        0,
        True,
        pltpu.HBM((members, tokens, LANES), bf16),
        hbm,
        own,
        mate,
        second_in,
        first_in,
        part,
    )
    home = exchange(grad)
    d_query = pl.pallas_call(
        unpack,
        out_shape=jax.ShapeDtypeStruct((tokens, width), bf16),
        in_specs=[vmem],
        out_specs=vmem,
        compiler_params=small,
        name="unpack",
    )(home)
    addends = (gate_sum + gate_mate)[0, : 3 * heads]
    gate_total = addends[:heads] + addends[heads : 2 * heads] + addends[2 * heads :]
    if chunks > 1 or groups > 2:
        gate_total = lax.psum(gate_total, AXES) / (2 * members)
    sig = jax.nn.sigmoid(gate_logit)
    d_gate = sig * (1.0 - sig) * gate_total / (shards * groups * tokens * LANES) ** 0.5
    return (d_query[None], d_gate)


def solution(mesh):
    placed = (
        P("grp", "mem", None),
        P("grp", "mem", None),
        P("grp", "mem", None),
        P("grp", "mem", None),
        P("mem", None),
        P("mem", None),
        P(),
        P("grp", "mem", None),
    )
    return jax.shard_map(
        local, mesh=mesh, in_specs=placed, out_specs=(P("grp", "mem", None), P()), check_vma=False
    )
```

```python
import functools
import math

import jax
import jax.numpy as jnp
from jax import lax
from jax.experimental import pallas as pl
from jax.experimental.pallas import tpu as pltpu
from jax.sharding import PartitionSpec as P

BLK = 16
LANES = 128
AXES = ("mem", "grp")
FAR = -1e30


def pack(
    heads,
    chunks,
    early,
    k_hbm,
    v_hbm,
    q_hbm,
    dout_hbm,
    omem_hbm,
    local_hbm,
    gate_ref,
    ids_ref,
    first_out,
    second_hbm,
    k_ref,
    v_ref,
    q_ref,
    dout_ref,
    omem_ref,
    local_ref,
    ext_ref,
    delta_ref,
    gate_rows,
    second_out,
    sems,
    out_sems,
):
    tokens = q_ref.shape[0]
    half_shard = k_ref.shape[0]
    qblocks, names = ids_ref.shape
    core = lax.axis_index("mem") % 2
    parity = lax.axis_index("grp") % 2
    mine = pl.ds(pl.multiple_of(parity * half_shard, half_shard), half_shard)
    bunches = sems.shape[0]
    bunch = heads // bunches
    copies = []
    for index in range(bunches):
        cols = slice(index * bunch * LANES, (index + 1) * bunch * LANES)
        copies.append([])
        for at, (source, target) in enumerate(
            (
                (dout_hbm.at[:, cols], dout_ref),
                (omem_hbm.at[:, cols], omem_ref),
                (local_hbm.at[:, cols], local_ref),
                (q_hbm.at[:, cols], q_ref),
                (k_hbm.at[mine, cols], k_ref),
                (v_hbm.at[mine, cols], v_ref),
            )
        ):
            copy = pltpu.make_async_copy(source, target.at[:, cols], sems.at[index, at])
            copy.start()
            copies[index].append(copy)

    lane = lax.broadcasted_iota(jnp.int32, (1, LANES), 1)
    ids = ids_ref[...]
    per = qblocks // 2
    bias_rows = chunks * per
    ext_ref[...] = jnp.zeros_like(ext_ref)
    for chunk in range(chunks):
        hits = []
        for side in range(2):
            shard = chunk * heads + 2 * (lane // 16) + (core + side) % 2
            wanted = jnp.broadcast_to(16 * shard + lane % 16, (qblocks, LANES))
            hit = jnp.zeros((qblocks, LANES), jnp.float32)
            for name in range(names):
                hit = jnp.where(ids[:, name : name + 1] == wanted, 1.0, hit)
            hits.append(hit)
        code = hits[0] + 2.0 * hits[1]
        ext_ref[chunk * per : (chunk + 1) * per, :] = code[:per] + 4.0 * code[per:]

    ones = jnp.ones((8, LANES), jnp.float32)
    wide_ones = jnp.ones((16, 2 * LANES), jnp.bfloat16)
    gate_rows[...] = jnp.zeros_like(gate_rows)
    at = 2 * half_shard
    late = tokens - early
    sent = []
    for head in range(heads):
        if head % bunch == 0:
            for copy in copies[head // bunch]:
                copy.wait()
        cols = slice(head * LANES, (head + 1) * LANES)
        sig = jax.nn.sigmoid(jnp.full((8, LANES), gate_ref[head], jnp.float32))[:1]
        d_out = dout_ref[:, cols].astype(jnp.float32)
        o_mem = omem_ref[:, cols].astype(jnp.float32)
        d_mem = (d_out * sig).astype(jnp.bfloat16)
        differ = o_mem - local_ref[:, cols].astype(jnp.float32)
        gate_rows[head : head + 1, :] = jnp.sum(d_out * differ, 0, keepdims=True)
        product = d_mem.astype(jnp.float32) * o_mem
        upper = product.astype(jnp.bfloat16)
        lower = (product - upper.astype(jnp.float32)).astype(jnp.bfloat16)
        row = lax.dot_general(
            wide_ones,
            jnp.concatenate([upper, lower], axis=1),
            (((1,), (1,)), ((), ())),
            preferred_element_type=jnp.float32,
        )
        delta_ref[head : head + 1, :] = row[:1]
        first_out[head, :half_shard, :] = k_ref[:, cols]
        first_out[head, half_shard:at, :] = v_ref[:, cols]
        first_out[head, at : at + early, :] = q_ref[:early, cols]
        first_out[head, at + early : at + 2 * early, :] = d_mem[:early]
        second_out[head, :late, :] = q_ref[early:, cols]
        second_out[head, late:, :] = d_mem[early:]
        if head % bunch == bunch - 1:
            some = slice(head + 1 - bunch, head + 1)
            copy = pltpu.make_async_copy(second_out.at[some], second_hbm.at[some], out_sems.at[1, head // bunch])
            copy.start()
            sent.append(copy)
    total = lax.dot_general(
        ones,
        gate_rows[...],
        (((1,), (1,)), ((), ())),
        precision=lax.Precision.HIGHEST,
        preferred_element_type=jnp.float32,
    )
    first = total.astype(jnp.bfloat16).astype(jnp.float32)
    second = (total - first).astype(jnp.bfloat16).astype(jnp.float32)
    third = total - first - second
    addends = first + pltpu.roll(second, heads, 1) + pltpu.roll(third, 2 * heads, 1)
    ext_ref[bias_rows + 1 : bias_rows + 2, :] = addends[:1]
    for head in range(heads):
        ext_ref[bias_rows : bias_rows + 1, :] = delta_ref[head : head + 1, :]
        first_out[head, at + 2 * early :, :] = ext_ref[...].astype(jnp.bfloat16)
    for copy in sent:
        copy.wait()


def assemble(in_ref, out_ref):
    part = out_ref.shape[1] // in_ref.shape[0]
    for source in range(in_ref.shape[0]):
        rows = slice(source * part, (source + 1) * part)
        out_ref[0, rows, :] = in_ref[source, :part, :]
        out_ref[1, rows, :] = in_ref[source, part : 2 * part, :]


def attend(begin, count, q_at, ext_at, qblocks, width, tile, final, own_ref, mate_ref, q_ref, ext_ref, *refs):
    if final:
        before_ref, out_ref, mark, minus, qx, dx, scores, high, total, acc, stage, sems = refs
        early_copy = pltpu.make_async_copy(before_ref, out_ref.at[:, :begin, :], sems.at[0])
        early_copy.start()
    else:
        out_ref, gate_ref, mark, minus, qx, dx, scores, high, total, acc = refs
    sources = q_ref.shape[0]
    units = qx.shape[1] // LANES - 1
    sides = (own_ref, mate_ref)
    steps_side = own_ref.shape[1] // width
    rows_unit = mark.shape[0]
    scale = 1.0 / math.sqrt(LANES)
    exponent = scale * math.log2(math.e)
    chunks = units // 2
    per = qblocks // 2
    bias_rows = chunks * per

    lane = lax.broadcasted_iota(jnp.int32, (BLK, LANES), 1)
    for block in range(LANES):
        mark[block * BLK : (block + 1) * BLK, :] = jnp.where(lane == block, 1.0, 0.0).astype(jnp.bfloat16)
    wide_lane = lax.broadcasted_iota(jnp.int32, (LANES, LANES), 1)
    for block in range(width // LANES):
        minus[block * LANES : (block + 1) * LANES, :] = jnp.where(wide_lane == 0, -1.0, 0.0).astype(jnp.bfloat16)

    gate_sum = jnp.zeros((1, LANES), jnp.float32)
    for source in range(sources):
        base = source * count
        qx[base : base + count, :LANES] = q_ref[source, q_at : q_at + count, :]
        dx[base : base + count, :LANES] = q_ref[source, q_at + count : q_at + 2 * count, :]
        extra = ext_ref[source, ext_at:, :].astype(jnp.float32)
        code = extra[:bias_rows]
        upper = jnp.floor(code * 0.25)
        code = upper if final else code - 4.0 * upper
        second = jnp.where(code > 1.5, 1.0, 0.0)
        first = code - 2.0 * second
        for side, hit in enumerate((first, second)):
            bias = jnp.where(hit > 0.5, 0.0, FAR)
            for chunk in range(chunks):
                lanes = (1 + side * chunks + chunk) * LANES
                for block in range(count // BLK):
                    at = chunk * per + block
                    row = jnp.broadcast_to(bias[at : at + 1], (BLK, LANES)).astype(jnp.bfloat16)
                    qx[base + block * BLK : base + (block + 1) * BLK, lanes : lanes + LANES] = row
        if not final:
            gate_sum = gate_sum + extra[bias_rows + 1 : bias_rows + 2]
        wide = jnp.broadcast_to(extra[bias_rows : bias_rows + 1], (LANES, LANES)).T
        wide = jnp.where(wide_lane == 0, wide, 0.0).astype(jnp.bfloat16)
        dx[base : base + count, LANES:] = wide[begin : begin + count]
    if not final:
        gate_ref[...] = jnp.broadcast_to(gate_sum, gate_ref.shape)

    def one_tile(index, carry):
        here = pl.ds(pl.multiple_of(index * tile, tile), tile)
        high[...] = jnp.full_like(high, -3e38)
        for side, ref in enumerate(sides):
            for unit in range(units // 2):

                def score(at, carry, side=side, ref=ref, unit=unit):
                    rows = pl.ds(pl.multiple_of(unit * rows_unit + at * width, width), width)
                    marks = pl.ds(pl.multiple_of(at * width, width), width)
                    lanes = (1 + side * (units // 2) + unit) * LANES
                    left = jnp.concatenate([qx[here, :LANES], qx[here, lanes : lanes + LANES]], axis=1)
                    right = jnp.concatenate([ref[0, rows, :], mark[marks, :]], axis=1)
                    got = lax.dot_general(
                        left, right, (((1,), (1,)), ((), ())), preferred_element_type=jnp.float32
                    )
                    scores[side * steps_side + unit * (rows_unit // width) + at] = got
                    best = high[...]
                    for column in range(width // LANES):
                        best = jnp.maximum(best, got[:, column * LANES : (column + 1) * LANES])
                    high[...] = best
                    return carry

                lax.fori_loop(0, rows_unit // width, score, 0, unroll=True)
        high[...] = jnp.broadcast_to(jnp.max(high[...], 1, keepdims=True) * exponent, high.shape)
        total[...] = jnp.zeros_like(total)
        acc[...] = jnp.zeros_like(acc)
        def back(at, carry):
            for side, ref in enumerate(sides):
                rows = pl.ds(pl.multiple_of(at * width, width), width)
                prod = lax.dot_general(
                    dx[here, :],
                    jnp.concatenate([ref[1, rows, :], minus[...]], axis=1),
                    (((1,), (1,)), ((), ())),
                    preferred_element_type=jnp.float32,
                )
                got = scores[side * steps_side + at]
                level = high[...]
                added = total[...]
                pieces = []
                for column in range(width // LANES):
                    cols = slice(column * LANES, (column + 1) * LANES)
                    expo = jnp.exp2(got[:, cols] * exponent - level)
                    added = added + expo
                    pieces.append((expo * prod[:, cols]).astype(jnp.bfloat16))
                total[...] = added
                acc[...] += jnp.dot(
                    jnp.concatenate(pieces, axis=1), ref[0, rows, :], preferred_element_type=jnp.float32
                )
            return carry

        lax.fori_loop(0, steps_side, back, 0, unroll=2 if final else 2)
        weight = scale / jnp.sum(total[...], 1, keepdims=True)
        qx[here, :LANES] = (acc[...] * weight).astype(jnp.bfloat16)
        return carry

    lax.fori_loop(0, qx.shape[0] // tile, one_tile, 0)
    for source in range(sources):
        (stage if final else out_ref)[source] = qx[source * count : (source + 1) * count, :LANES]
    if final:
        copies = [early_copy]
        for part in range(4):
            some = slice(part * sources // 4, (part + 1) * sources // 4)
            copy = pltpu.make_async_copy(stage.at[some], out_ref.at[some, begin:, :], sems.at[1 + part])
            copy.start()
            copies.append(copy)
        for copy in copies:
            copy.wait()


def unpack(in_ref, out_ref):
    for head in range(in_ref.shape[0]):
        out_ref[:, head * LANES : (head + 1) * LANES] = in_ref[head]


def local(queries, d_out, o_mem, local_out, mem_keys, mem_values, gate_logit, block_ids):
    shards = lax.axis_size("mem")
    groups = lax.axis_size("grp")
    tokens = queries.shape[1]
    width = queries.shape[2]
    heads = gate_logit.shape[0]
    rows_dev = mem_keys.shape[0]
    qblocks = tokens // BLK
    members = heads
    chunks = shards // heads
    assert width == heads * LANES and shards % heads == 0 and groups % 2 == 0
    assert rows_dev == 16 * BLK and heads * 8 == LANES and tokens == LANES
    half_shard = rows_dev // 2
    units = 2 * chunks
    early = tokens // 2
    late = tokens - early
    extra = -(-(chunks * (qblocks // 2) + 2) // 8) * 8
    ext_at = 2 * half_shard + 2 * early
    vmem = pl.BlockSpec(memory_space=pltpu.VMEM)
    smem = pl.BlockSpec(memory_space=pltpu.SMEM)
    hbm = pl.BlockSpec(memory_space=pltpu.HBM)
    bf16 = jnp.bfloat16
    small = pltpu.CompilerParams(vmem_limit_bytes=24 << 20)

    core_groups = [
        [(mo * heads + 2 * chip + core) * groups + 2 * go + gp for chip in range(heads // 2) for gp in range(2)]
        for mo in range(chunks)
        for go in range(groups // 2)
        for core in range(2)
    ]
    exchange = functools.partial(
        lax.all_to_all, axis_name=AXES, split_axis=0, concat_axis=0, tiled=True, axis_index_groups=core_groups
    )

    first_shape = (members, ext_at + extra, LANES)
    second_shape = (members, 2 * late, LANES)
    first_out, second_out = pl.pallas_call(
        functools.partial(pack, heads, chunks, early),
        out_shape=(pltpu.VMEM(first_shape, bf16), pltpu.HBM(second_shape, bf16)),
        in_specs=[hbm] * 6 + [smem, vmem],
        out_specs=(vmem, hbm),
        scratch_shapes=[pltpu.VMEM((half_shard, width), bf16)] * 2
        + [pltpu.VMEM((tokens, width), bf16)] * 4
        + [
            pltpu.VMEM((extra, LANES), jnp.float32),
            pltpu.VMEM((heads, LANES), jnp.float32),
            pltpu.VMEM((LANES, LANES), jnp.float32),
            pltpu.VMEM(second_shape, bf16),
            pltpu.SemaphoreType.DMA((2, 6)),
            pltpu.SemaphoreType.DMA((2, 2)),
        ],
        compiler_params=pltpu.CompilerParams(vmem_limit_bytes=56 << 20),
        name="pack",
    )(mem_keys, mem_values, queries[0], d_out[0], o_mem[0], local_out[0], gate_logit, block_ids[0])
    first_in = exchange(first_out)
    second_in = exchange(second_out)
    own = pl.pallas_call(
        assemble,
        out_shape=jax.ShapeDtypeStruct((2, members * half_shard, LANES), bf16),
        in_specs=[vmem],
        out_specs=vmem,
        compiler_params=small,
        name="assemble",
    )(first_in)
    if chunks > 1:
        same = [[mo * heads + mi for mo in range(chunks)] for mi in range(heads)]
        own = lax.all_gather(own, "mem", axis_index_groups=same, axis=1, tiled=True)
    mate = lax.ppermute(own, "mem", [(i, i ^ 1) for i in range(shards)])

    rows_all = 2 * own.shape[1]
    step_width = 512

    def attend_some(begin, count, q_at, final, out_shape, out_specs, *args):
        tile = members * count if chunks == 1 else 256
        return pl.pallas_call(
            functools.partial(attend, begin, count, q_at, ext_at, qblocks, step_width, tile, final),
            out_shape=out_shape,
            in_specs=[vmem] * len(args),
            out_specs=out_specs,
            scratch_shapes=[
                pltpu.VMEM((LANES * BLK, LANES), bf16),
                pltpu.VMEM((step_width, LANES), bf16),
                pltpu.VMEM((members * count, (1 + units) * LANES), bf16),
                pltpu.VMEM((members * count, 2 * LANES), bf16),
                pltpu.VMEM((rows_all // step_width, tile, step_width), jnp.float32),
                pltpu.VMEM((tile, LANES), jnp.float32),
                pltpu.VMEM((tile, LANES), jnp.float32),
                pltpu.VMEM((tile, LANES), jnp.float32),
            ]
            + [pltpu.VMEM((members, count, LANES), bf16), pltpu.SemaphoreType.DMA((5,))] * final,
            compiler_params=pltpu.CompilerParams(vmem_limit_bytes=(40 if chunks == 1 else 44) << 20),
            cost_estimate=pl.CostEstimate(
                flops=2 * members * count * rows_all * LANES * 5,
                bytes_accessed=4 * rows_all * LANES,
                transcendentals=members * count * rows_all,
            ),
            name="attend",
        )(*args)

    part, gate_sum = attend_some(
        0,
        early,
        2 * half_shard,
        False,
        [jax.ShapeDtypeStruct((members, early, LANES), bf16), jax.ShapeDtypeStruct((8, LANES), jnp.float32)],
        [vmem, vmem],
        own,
        mate,
        first_in,
        first_in,
    )
    gate_mate = lax.ppermute(gate_sum, "mem", [(i, i ^ 1) for i in range(shards)])
    grad = attend_some(
        early,
        late,
        0,
        True,
        pltpu.HBM((members, tokens, LANES), bf16),
        hbm,
        own,
        mate,
        second_in,
        first_in,
        part,
    )
    home = exchange(grad)
    d_query = pl.pallas_call(
        unpack,
        out_shape=jax.ShapeDtypeStruct((tokens, width), bf16),
        in_specs=[vmem],
        out_specs=vmem,
        compiler_params=small,
        name="unpack",
    )(home)
    addends = (gate_sum + gate_mate)[0, : 3 * heads]
    gate_total = addends[:heads] + addends[heads : 2 * heads] + addends[2 * heads :]
    if chunks > 1 or groups > 2:
        gate_total = lax.psum(gate_total, AXES) / (2 * members)
    sig = jax.nn.sigmoid(gate_logit)
    d_gate = sig * (1.0 - sig) * gate_total / (shards * groups * tokens * LANES) ** 0.5
    return (d_query[None], d_gate)


def solution(mesh):
    placed = (
        P("grp", "mem", None),
        P("grp", "mem", None),
        P("grp", "mem", None),
        P("grp", "mem", None),
        P("mem", None),
        P("mem", None),
        P(),
        P("grp", "mem", None),
    )
    return jax.shard_map(
        local, mesh=mesh, in_specs=placed, out_specs=(P("grp", "mem", None), P()), check_vma=False
    )
```
